32 devices in a mesh: dp: 32 (over z, y, x, core).
Axes of the slice: x: 2, y: 2, z: 4, core: 2. Of those that a mesh axis runs over, the one named last changes fastest.
Arguments:
- tokens: bfloat16 [65536, 512], P('dp'), may hold values from -11 to 11
- cotangent: bfloat16 [65536, 512], P('dp'), may hold values from -6 to 6
- segment_ids: int32 [65536], P('dp'), may hold values from 0 to 1023, never falling along the last dimension, each value on 1 to 128 neighbouring positions
- row_lengths: int32 [64], P('dp'), may hold values from 0 to 2048, as said below
- row_widths: int32 [32], P('dp'), may hold values from 0 to 1, as said below
- params: float32 [3151872], P('dp'), may hold values from -3 to 3, as said below
- momenta: float32 [3151872], P('dp'), may hold values from -0.0034179688 to 0.0034179688
- averages: float32 [3151872], P('dp'), may hold values from -3 to 3
Outputs:
- layer_output: bfloat16 [65536, 512], P('dp')
- input_grad: float32 [65536, 512], P('dp')
- grad_norm: float32 [], replicated
- vector_grads: float32 [512, 12], replicated
- new_params: float32 [3151872], P('dp')
- new_momenta: float32 [3151872], P('dp')
- new_averages: float32 [3151872], P('dp')
The draws below stay inside these ranges and needn't reach their ends.
Inputs may be any that keep to these rules, and one draw needn't show every extreme that they name: `segment_ids`: never falling along the slots; each sentence covers 1 to 128 consecutive slots, some exactly 128. `row_lengths`: entries 2g and 2g + 1 belong to group g. In a group of two rows they are the live slots of each row, 512 to 1024; in a group of one row the first is its live slots, 1024 to 2048, and the second is 0. In every draw some group is one row with all 2048 slots live. `row_widths`: in every draw some groups are one row and some are two. `params`: gains are positive.
All inputs are finite; a program needn't handle non-finite values.
Results may differ from the reference program's by a relative error of at most 0.012.
Values may be sent and summed in bfloat16 or wider, within the bound.
No kernel may reach another device: no remote copies, remote signals or barrier semaphores. Data moves between devices by JAX's collectives and lax.ppermute only.
A program may use at most 192 MiB of HBM per device.

```python
import math
import jax
import jax.numpy as jnp
import numpy as np
from jax import lax

D = 512
H = 8
HD = 64
FF = 2048
ROW = 1024
SENT = 64
SLOTS = 2048
TOKENS = 65536
PARAMS = 3151872
N_DP = 32


def rising(count, bottom, ratio):
    return bottom * ratio ** (jnp.arange(count, dtype=jnp.float32) / (count - 1))


def parameter_table(noise_table, bottom, ratio):
    column_scale = jnp.concatenate([jnp.full((3 * D,), D ** (-0.5), jnp.float32), jnp.full((D,), (SENT / (4.0 * D)) ** 0.5, jnp.float32), jnp.full((FF,), D ** (-0.5), jnp.float32), jnp.full((FF,), FF ** (-0.5), jnp.float32), jnp.full((12,), 0.3, jnp.float32)])
    values = noise_table * column_scale
    gain_first = rising(D, bottom, ratio) * (1.0 + 0.1 * noise_table[:, 12 * D + 4])
    gain_second = rising(D, bottom, ratio) * (1.0 + 0.1 * noise_table[:, 12 * D + 6])
    values = values.at[:, 12 * D + 4].set(gain_first).at[:, 12 * D + 6].set(gain_second)
    return values.reshape(-1)


def row_plan(key):
    width_key, length_key, pick_key = jax.random.split(key, 3)
    devices = jnp.arange(N_DP, dtype=jnp.int32)
    wide_rows = (jax.random.randint(width_key, (N_DP,), 0, 4) == 0).astype(jnp.int32)
    chosen = jax.random.randint(pick_key, (), 0, N_DP)
    wide_rows = jnp.where(devices == chosen, 1, jnp.where(devices == (chosen + 1) % N_DP, 0, wide_rows)).astype(jnp.int32)
    narrow_lengths = jax.random.randint(length_key, (N_DP, 2), ROW // 2, ROW + 1)
    wide_lengths = jax.random.randint(jax.random.fold_in(length_key, 1), (N_DP,), ROW, 2 * ROW + 1)
    wide_lengths = jnp.where(devices == chosen, 2 * ROW, wide_lengths)
    first_length = jnp.where(wide_rows == 1, wide_lengths, narrow_lengths[:, 0])
    second_length = jnp.where(wide_rows == 1, 0, narrow_lengths[:, 1])
    return (wide_rows, jnp.stack([first_length, second_length], axis=1).reshape(-1).astype(jnp.int32))


def draw_row_widths(key, part):
    wide_rows, _ = row_plan(key)
    return wide_rows


def draw_row_lengths(key, part):
    _, lengths_all = row_plan(key)
    return lengths_all


def draw_tokens(key, part):
    key = jax.random.fold_in(key, 11)
    noise_table = jnp.clip(jax.random.normal(key, (TOKENS, D), jnp.float32), -6.0, 6.0)
    return (noise_table * rising(D, 0.6, 3.0)).astype(jnp.bfloat16)


def draw_params(key, part):
    key = jax.random.fold_in(key, 21)
    table_shape = (D, 12 * (D + 1))
    noise_table = jnp.clip(jax.random.normal(key, table_shape, jnp.float32), -6.0, 6.0)
    return parameter_table(noise_table, 0.6, 3.0)


def draw_averages(key, part):
    key = jax.random.fold_in(key, 31)
    table_shape = (D, 12 * (D + 1))
    noise_table = jnp.clip(jax.random.normal(key, table_shape, jnp.float32), -6.0, 6.0)
    return parameter_table(noise_table, 0.6, 3.0)


def block_scale(stream_key, extent, cuts, low, high):
    level = 1.0
    for axis_at, parts in cuts:
        heights = jax.random.uniform(jax.random.fold_in(jax.random.fold_in(stream_key, 6), axis_at), (parts,), jnp.float32, low / len(cuts), high / len(cuts))
        level = level * jnp.repeat(jnp.exp(heights), extent[axis_at] // parts).reshape((-1,) + (1,) * (len(extent) - 1 - axis_at))
    return level


def split_up(amount, total, reach, lean):
    weights = [(1 << 20) // math.isqrt(standing ** lean) + 1 for standing in range(2, amount + 1)]
    surplus, given = total - reach - (amount - 1), [1] * (amount - 1)
    while surplus > 0:
        candidates = [i for i in range(amount - 1) if given[i] < reach]
        mass, budget = sum([weights[i] for i in candidates]), surplus
        for i in candidates:
            more = min(reach - given[i], max(1, budget * weights[i] // mass), surplus)
            given[i] = given[i] + more
            surplus = surplus - more
    return np.array([reach] + given)


def uneven(key, number_of, total, bound, slope):
    if number_of == 2:
        one = jax.random.randint(key, (), max(1, total - bound), min(bound, total - 1) + 1)
        return jnp.stack([one, total - one])
    tallies = jnp.asarray(split_up(number_of, total, bound, slope), jnp.int32)
    pairs = (number_of - 1) // 2
    giver, taker = tallies[1:1 + 2 * pairs:2], tallies[2:2 + 2 * pairs:2]
    slack = jnp.minimum(giver - 1, bound - taker)
    passed = jax.random.randint(jax.random.fold_in(key, 1), (pairs,), 0, 1 << 20) % (slack + 1)
    tallies = tallies.at[1:1 + 2 * pairs:2].set(giver - passed).at[2:2 + 2 * pairs:2].set(taker + passed)
    return tallies[jax.random.permutation(jax.random.fold_in(key, 2), number_of)]


def gaussian(key, dims, scale, bound, cuts=(), held_as=jnp.bfloat16):
    loudness = block_scale(key, dims, cuts, -0.22, 0.18) if cuts else 1.0
    drawn = jax.random.normal(key, dims, jnp.float32) * scale * loudness
    return jnp.minimum(jnp.maximum(drawn, -bound), bound).astype(held_as)


def setup_inputs(seed: int = 0) -> dict:
    key_list = jax.random.split(jax.random.key(seed), 9)
    tokens = draw_tokens(jax.random.fold_in(key_list[8], 71), 0)
    cotangent = gaussian(key_list[1], (TOKENS, D), 1.0, 6.0, ((0, 32),))
    segment_ids = jnp.searchsorted(jnp.cumsum(uneven(key_list[2], TOKENS // SENT, TOKENS, 2 * SENT, 1)), jnp.arange(TOKENS), side="right").astype(jnp.int32)
    row_lengths = draw_row_lengths(jax.random.fold_in(key_list[8], 71), 0)
    row_widths = draw_row_widths(jax.random.fold_in(key_list[8], 71), 0)
    params = draw_params(jax.random.fold_in(key_list[8], 71), 0)
    momenta = gaussian(key_list[6], (PARAMS,), ((12 * D * (D + 1)) ** -0.5), 0.0034179688, ((0, 32),), jnp.float32)
    averages = draw_averages(jax.random.fold_in(key_list[8], 71), 0)
    return {"tokens": tokens, "cotangent": cotangent, "segment_ids": segment_ids, "row_lengths": row_lengths, "row_widths": row_widths, "params": params, "momenta": momenta, "averages": averages}


@jax.custom_vjp
def low(v):
    return lax.optimization_barrier(v.astype(jnp.bfloat16)).astype(jnp.float32)

@jax.custom_vjp
def low_back(v):
    return v

def low_keep(v):
    return (low(v), None)

def low_pass(kept, grad):
    return (grad,)

def back_keep(v):
    return (v, None)

def back_low(kept, grad):
    return (low(grad),)
low.defvjp(low_keep, low_pass)
low_back.defvjp(back_keep, back_low)
EPSILON = 1e-05
CLIP_NORM = 1.0
LEARN_RATE = 20.0
MOMENTUM = 0.5
AVERAGE_DECAY = 0.5
MASKED = -1e+30

def exact_dot(left_side, right_side):
    return jnp.dot(left_side, right_side, precision=lax.Precision.HIGHEST, preferred_element_type=jnp.float32)

def round_both(values):
    return low(low_back(values))

def norm_rows(values, gain_vec, shift_vec):
    centre = lax.optimization_barrier(jnp.mean(values, axis=-1, keepdims=True))
    centred = values - centre
    spread = lax.optimization_barrier(jnp.mean(centred * centred, axis=-1, keepdims=True))
    return centred * lax.rsqrt(spread + EPSILON) * gain_vec + shift_vec

def device_layer(weights, block_x, groups, limits, row_width):
    table = weights.reshape(D, 12 * (D + 1))
    w_query = table[:, :D]
    w_key = table[:, D:2 * D]
    w_value = table[:, 2 * D:3 * D]
    w_out = table[:, 3 * D:4 * D]
    w_up = table[:, 4 * D:4 * D + FF]
    w_down = table[:, 4 * D + FF:12 * D]
    extra = table[:, 12 * D:]
    positions = jnp.arange(SLOTS, dtype=jnp.int32)
    row_number = jnp.where(row_width == 1, 0, positions // ROW).astype(jnp.int32)
    row_limit = jnp.where(row_number == 0, limits[0], limits[1])
    live_slot = positions - row_number * ROW < row_limit
    allowed = (row_number[:, None] == row_number[None, :]) & (groups[:, None] == groups[None, :]) & live_slot[None, :] | (positions[:, None] == positions[None, :])
    query_low = round_both(exact_dot(block_x, w_query) + extra[:, 0]).reshape(SLOTS, H, HD)
    key_low = round_both(exact_dot(block_x, w_key)).reshape(SLOTS, H, HD)
    value_low = round_both(exact_dot(block_x, w_value) + extra[:, 1]).reshape(SLOTS, H, HD)
    scores = low_back(jnp.einsum('qhd,khd->hqk', query_low, key_low, precision=lax.Precision.HIGHEST) * HD ** (-0.5))
    scores = jnp.where(allowed[None], scores, MASKED)
    chances = low(jax.nn.softmax(scores, axis=-1))
    attended = jnp.einsum('hqk,khd->qhd', chances, value_low, precision=lax.Precision.HIGHEST)
    attended = round_both(attended.reshape(SLOTS, D))
    branch_one = low_back(exact_dot(attended, w_out.T) + extra[:, 2])
    first_norm = norm_rows(block_x + branch_one, extra[:, 4], extra[:, 5])
    hidden_pre = low_back(exact_dot(low(first_norm), w_up) + extra[:, 8:].reshape(FF))
    hidden_low = low(jax.nn.gelu(hidden_pre))
    branch_two = low_back(exact_dot(hidden_low, w_down.T) + extra[:, 3])
    second_norm = norm_rows(first_norm + branch_two + block_x, extra[:, 6], extra[:, 7])
    return jnp.where(live_slot[:, None], second_norm, 0.0)

def reference(tokens, cotangent, segment_ids, row_lengths, row_widths, params, momenta, averages):
    inputs = tokens.astype(jnp.float32).reshape(N_DP, SLOTS, D)
    returned = cotangent.astype(jnp.float32).reshape(N_DP, SLOTS, D)
    groups = segment_ids.reshape(N_DP, SLOTS)
    limits = row_lengths.reshape(N_DP, 2)
    layer_step = jax.checkpoint(device_layer)

    def whole_layer(buffer, activations):
        weights = low(buffer)

        def device_step(loop_state, pieces):
            block_x, block_groups, block_limits, block_width = pieces
            return (loop_state, layer_step(weights, block_x, block_groups, block_limits, block_width))
        _, results = lax.scan(device_step, jnp.zeros((), jnp.float32), (activations, groups, limits, row_widths))
        return results
    results, pullback = jax.vjp(whole_layer, params, inputs)
    param_grads, input_grad = pullback(returned)
    vector_grads = param_grads.reshape(D, 12 * (D + 1))[:, 12 * D:]
    squares = jnp.sum(param_grads * param_grads)
    grad_norm = jnp.sqrt(squares)
    factor = jnp.minimum(1.0, CLIP_NORM / (grad_norm + 1e-06))
    clipped = param_grads * factor
    new_momenta = MOMENTUM * momenta + clipped
    new_params = params - LEARN_RATE * (clipped + MOMENTUM * new_momenta)
    new_averages = AVERAGE_DECAY * averages + (1.0 - AVERAGE_DECAY) * new_params
    layer_output = results.reshape(TOKENS, D).astype(jnp.bfloat16)
    return (layer_output, input_grad.reshape(TOKENS, D), grad_norm, vector_grads, new_params, new_momenta, new_averages)
```

```python
import jax
import jax.numpy as jnp
from jax import lax
from jax.sharding import PartitionSpec as P

HD = 64
ROW = 1024
SENT = 64


EPSILON = 1e-05
CLIP_NORM = 1.0
LEARN_RATE = 20.0
MOMENTUM = 0.5
AVERAGE_DECAY = 0.5
MASKED = -1e30


def mixed_dot(left_side, right_side):
    return jnp.dot(left_side, right_side, preferred_element_type=jnp.float32)


def cross_rows(left_side, right_side):
    return jnp.einsum("ta,tb->ab", left_side, right_side, preferred_element_type=jnp.float32)


def column_sum(values):
    return jnp.sum(values.astype(jnp.float32), axis=0)


def unpack(buffer, model_width):
    table = buffer.reshape(model_width, 12 * (model_width + 1))
    hidden_width = 4 * model_width
    matrices = (
        table[:, :model_width],
        table[:, model_width : 2 * model_width],
        table[:, 2 * model_width : 3 * model_width],
        table[:, 3 * model_width : 4 * model_width],
        table[:, 4 * model_width : 4 * model_width + hidden_width],
        table[:, 4 * model_width + hidden_width : 12 * model_width],
    )
    vectors = table[:, 12 * model_width :].astype(jnp.float32)
    return (matrices, vectors)


def exchange(values, bit, count):
    return lax.ppermute(values, "dp", [(at, at ^ bit) for at in range(count)])


def gather_blocks(block, count):
    bit = count // 2
    while bit:
        block = jnp.concatenate([block, exchange(block, bit, count)], axis=0)
        bit //= 2
    return block


def scatter_blocks(blocks, count):
    bit = 1
    while bit < count:
        half = blocks.shape[0] // 2
        arrived = exchange(blocks[half:], bit, count)
        total = blocks[:half].astype(jnp.float32) + arrived.astype(jnp.float32)
        blocks = total.astype(blocks.dtype) if bit * 2 < count else total
        bit *= 2
    return blocks


def sum_everywhere(values, count):
    bit = 1
    while bit < count:
        values = values + exchange(values, bit, count)
        bit *= 2
    return values


def reversed_bits(count):
    width = count.bit_length() - 1
    return [sum(((at >> k) & 1) << (width - 1 - k) for k in range(width)) for at in range(count)]


def to_natural(blocks, count, mine):
    rows = blocks.shape[0] // count
    places = jnp.array(reversed_bits(count), jnp.int32)[jnp.arange(count) ^ mine]
    return jnp.take(blocks.reshape(count, rows, -1), places, axis=0).reshape(blocks.shape)


def from_natural(table, count, mine):
    rows = table.shape[0] // count
    owners = jnp.array(reversed_bits(count), jnp.int32) ^ mine
    return jnp.take(table.reshape(count, rows, -1), owners, axis=0).reshape(table.shape)


def norm_forward(values, gain_vec, shift_vec):
    centre = jnp.mean(values, axis=-1, keepdims=True)
    centred = values - centre
    inverse = lax.rsqrt(jnp.mean(centred * centred, axis=-1, keepdims=True) + EPSILON)
    normed = centred * inverse
    return (normed * gain_vec + shift_vec, normed, inverse)


def norm_backward(grad_out, normed, inverse, gain_vec):
    scaled = grad_out * gain_vec
    grad_in = inverse * (
        scaled
        - jnp.mean(scaled, axis=-1, keepdims=True)
        - normed * jnp.mean(scaled * normed, axis=-1, keepdims=True)
    )
    return (grad_in, jnp.sum(grad_out * normed, axis=0), jnp.sum(grad_out, axis=0))


def block_allowed(layout, begin_at, block_rows, window):
    row_number, segments, positions, key_rows, key_groups, key_live, key_places = layout
    query_row = lax.dynamic_slice_in_dim(row_number, begin_at, block_rows)
    query_group = lax.dynamic_slice_in_dim(segments, begin_at, block_rows)
    query_place = lax.dynamic_slice_in_dim(positions, begin_at, block_rows)
    key_row = lax.dynamic_slice_in_dim(key_rows, begin_at, window)
    key_group = lax.dynamic_slice_in_dim(key_groups, begin_at, window)
    key_alive = lax.dynamic_slice_in_dim(key_live, begin_at, window)
    key_place = lax.dynamic_slice_in_dim(key_places, begin_at, window)
    joined = (
        (query_row[:, None] == key_row[None, :])
        & (query_group[:, None] == key_group[None, :])
        & key_alive[None, :]
    )
    return joined | (query_place[:, None] == key_place[None, :])


def pad_keys(values, margin):
    return jnp.pad(values, ((margin, margin), (0, 0), (0, 0)))


def attend_forward(query_low, key_low, value_low, layout, block_rows, margin):
    slot_count, head_count, head_dim = query_low.shape
    window = block_rows + 2 * margin
    score_scale = head_dim ** (-0.5)
    key_wide = pad_keys(key_low, margin)
    value_wide = pad_keys(value_low, margin)

    def forward_block(block_index):
        begin_at = block_index * block_rows
        query_block = lax.dynamic_slice_in_dim(query_low, begin_at, block_rows, 0)
        key_block = lax.dynamic_slice_in_dim(key_wide, begin_at, window, 0)
        value_block = lax.dynamic_slice_in_dim(value_wide, begin_at, window, 0)
        allowed = block_allowed(layout, begin_at, block_rows, window)
        scores = (
            jnp.einsum("qhd,khd->hqk", query_block, key_block, preferred_element_type=jnp.float32)
            * score_scale
        )
        scores = jnp.where(allowed[None], scores, MASKED)
        highest = jnp.max(scores, axis=-1, keepdims=True)
        exponent = jnp.exp(scores - highest)
        row_total = jnp.sum(exponent, axis=-1, keepdims=True)
        chances_low = (exponent / row_total).astype(jnp.bfloat16)
        outputs = jnp.einsum(
            "hqk,khd->qhd", chances_low, value_block, preferred_element_type=jnp.float32
        )
        return (outputs.astype(jnp.bfloat16), highest + jnp.log(row_total))

    outputs, logsum = lax.map(forward_block, jnp.arange(slot_count // block_rows))
    return (outputs.reshape(slot_count, head_count * head_dim), logsum)


def attend_backward(grad_out, query_low, key_low, value_low, logsum, layout, block_rows, margin):
    slot_count, head_count, head_dim = query_low.shape
    window = block_rows + 2 * margin
    score_scale = head_dim ** (-0.5)
    key_wide = pad_keys(key_low, margin)
    value_wide = pad_keys(value_low, margin)
    zeros_wide = jnp.zeros(key_wide.shape, jnp.float32)

    def backward_block(carried, block_index):
        key_grads, value_grads = carried
        begin_at = block_index * block_rows
        query_block = lax.dynamic_slice_in_dim(query_low, begin_at, block_rows, 0)
        key_block = lax.dynamic_slice_in_dim(key_wide, begin_at, window, 0)
        value_block = lax.dynamic_slice_in_dim(value_wide, begin_at, window, 0)
        grad_block = lax.dynamic_slice_in_dim(grad_out, begin_at, block_rows, 0)
        allowed = block_allowed(layout, begin_at, block_rows, window)
        scores = (
            jnp.einsum("qhd,khd->hqk", query_block, key_block, preferred_element_type=jnp.float32)
            * score_scale
        )
        scores = jnp.where(allowed[None], scores, MASKED)
        chances = jnp.exp(scores - logsum[block_index])
        chances_low = chances.astype(jnp.bfloat16)
        value_part = jnp.einsum(
            "hqk,qhd->khd", chances_low, grad_block, preferred_element_type=jnp.float32
        )
        grad_chance = jnp.einsum(
            "qhd,khd->hqk", grad_block, value_block, preferred_element_type=jnp.float32
        )
        centre = jnp.sum(chances * grad_chance, axis=-1, keepdims=True)
        grad_score = (chances * (grad_chance - centre)).astype(jnp.bfloat16)
        query_part = (
            jnp.einsum("hqk,khd->qhd", grad_score, key_block, preferred_element_type=jnp.float32)
            * score_scale
        )
        key_part = (
            jnp.einsum("hqk,qhd->khd", grad_score, query_block, preferred_element_type=jnp.float32)
            * score_scale
        )
        key_grads = lax.dynamic_update_slice_in_dim(
            key_grads,
            lax.dynamic_slice_in_dim(key_grads, begin_at, window, 0) + key_part,
            begin_at,
            0,
        )
        value_grads = lax.dynamic_update_slice_in_dim(
            value_grads,
            lax.dynamic_slice_in_dim(value_grads, begin_at, window, 0) + value_part,
            begin_at,
            0,
        )
        return ((key_grads, value_grads), query_part)

    (key_grads, value_grads), query_parts = lax.scan(
        backward_block, (zeros_wide, zeros_wide), jnp.arange(slot_count // block_rows)
    )
    flat_width = head_count * head_dim
    grad_query = query_parts.reshape(slot_count, flat_width)
    grad_key = key_grads[margin : margin + slot_count].reshape(slot_count, flat_width)
    grad_value = value_grads[margin : margin + slot_count].reshape(slot_count, flat_width)
    return (grad_query, grad_key, grad_value)


def body(tokens, cotangent, segment_ids, row_lengths, row_widths, params, momenta, averages):
    slot_count, model_width = tokens.shape
    head_dim = HD
    head_count = model_width // head_dim
    split_shape = (slot_count, head_count, head_dim)
    block_rows = min(512, slot_count)
    margin = 2 * SENT
    positions = jnp.arange(slot_count, dtype=jnp.int32)
    row_number = jnp.where(row_widths[0] == 1, 0, positions // ROW)
    row_limit = jnp.where(row_number == 0, row_lengths[0], row_lengths[1])
    live_slot = positions - row_number * ROW < row_limit
    layout = (
        row_number,
        segment_ids,
        positions,
        jnp.pad(row_number, margin, constant_values=-1),
        jnp.pad(segment_ids, margin, constant_values=-1),
        jnp.pad(live_slot, margin),
        jnp.arange(slot_count + 2 * margin, dtype=jnp.int32) - margin,
    )
    count = lax.axis_size("dp")
    mine = lax.axis_index("dp")
    table_width = 12 * (model_width + 1)
    own_weights = params.astype(jnp.bfloat16).reshape(-1, table_width)
    gathered = to_natural(gather_blocks(own_weights, count), count, mine)
    matrices, vectors = unpack(gathered, model_width)
    w_query, w_key, w_value, w_out, w_up, w_down = matrices
    bias_up = vectors[:, 8:].reshape(-1)
    inputs = tokens.astype(jnp.float32)
    query_low = (mixed_dot(tokens, w_query) + vectors[:, 0]).astype(jnp.bfloat16)
    key_low = mixed_dot(tokens, w_key).astype(jnp.bfloat16)
    value_low = (mixed_dot(tokens, w_value) + vectors[:, 1]).astype(jnp.bfloat16)
    attended, logsum = attend_forward(
        query_low.reshape(split_shape),
        key_low.reshape(split_shape),
        value_low.reshape(split_shape),
        layout,
        block_rows,
        margin,
    )
    branch_one = mixed_dot(attended, w_out.T) + vectors[:, 2]
    first_norm, normed_one, inverse_one = norm_forward(
        inputs + branch_one, vectors[:, 4], vectors[:, 5]
    )
    first_low = first_norm.astype(jnp.bfloat16)
    hidden_pre = mixed_dot(first_low, w_up) + bias_up
    hidden_low = jax.nn.gelu(hidden_pre).astype(jnp.bfloat16)
    branch_two = mixed_dot(hidden_low, w_down.T) + vectors[:, 3]
    second_norm, normed_two, inverse_two = norm_forward(
        first_norm + branch_two + inputs, vectors[:, 6], vectors[:, 7]
    )
    live_column = live_slot[:, None]
    layer_output = jnp.where(live_column, second_norm, 0.0).astype(jnp.bfloat16)
    grad_output = jnp.where(live_column, cotangent.astype(jnp.float32), 0.0)
    grad_two, grad_gain_two, grad_shift_two = norm_backward(
        grad_output, normed_two, inverse_two, vectors[:, 6]
    )
    grad_feed = grad_two.astype(jnp.bfloat16)
    grad_w_down = cross_rows(grad_feed, hidden_low)
    grad_hidden = mixed_dot(grad_feed, w_down)
    _, gelu_back = jax.vjp(jax.nn.gelu, hidden_pre)
    grad_up = gelu_back(grad_hidden)[0].astype(jnp.bfloat16)
    grad_w_up = cross_rows(first_low, grad_up)
    grad_first = grad_two + mixed_dot(grad_up, w_up.T)
    grad_one, grad_gain_one, grad_shift_one = norm_backward(
        grad_first, normed_one, inverse_one, vectors[:, 4]
    )
    grad_branch = grad_one.astype(jnp.bfloat16)
    grad_w_out = cross_rows(grad_branch, attended)
    grad_attended = mixed_dot(grad_branch, w_out).astype(jnp.bfloat16)
    grad_query, grad_key, grad_value = attend_backward(
        grad_attended.reshape(split_shape),
        query_low.reshape(split_shape),
        key_low.reshape(split_shape),
        value_low.reshape(split_shape),
        logsum,
        layout,
        block_rows,
        margin,
    )
    query_back = grad_query.astype(jnp.bfloat16)
    key_back = grad_key.astype(jnp.bfloat16)
    value_back = grad_value.astype(jnp.bfloat16)
    grad_w_query = cross_rows(tokens, query_back)
    grad_w_key = cross_rows(tokens, key_back)
    grad_w_value = cross_rows(tokens, value_back)
    input_grad = (
        grad_two
        + grad_one
        + mixed_dot(query_back, w_query.T)
        + mixed_dot(key_back, w_key.T)
        + mixed_dot(value_back, w_value.T)
    )
    vector_local = jnp.concatenate(
        [
            jnp.stack(
                [
                    column_sum(query_back),
                    column_sum(value_back),
                    column_sum(grad_branch),
                    column_sum(grad_feed),
                    grad_gain_one,
                    grad_shift_one,
                    grad_gain_two,
                    grad_shift_two,
                ],
                axis=1,
            ),
            column_sum(grad_up).reshape(model_width, 4),
        ],
        axis=1,
    )
    matrix_grads = jnp.concatenate(
        [grad_w_query, grad_w_key, grad_w_value, grad_w_out, grad_w_up, grad_w_down], axis=1
    ).astype(jnp.bfloat16)
    own_matrix = scatter_blocks(from_natural(matrix_grads, count, mine), count)
    vector_grads = sum_everywhere(vector_local.T, count).T
    squares = sum_everywhere(jnp.sum(own_matrix * own_matrix).reshape(1, 1), count)[0, 0]
    grad_norm = jnp.sqrt(squares + jnp.sum(vector_grads * vector_grads))
    own_count = own_matrix.shape[0]
    own_vector = lax.dynamic_slice_in_dim(vector_grads, mine * own_count, own_count)
    own_rows = jnp.concatenate([own_matrix, own_vector], axis=1).reshape(-1)
    factor = jnp.minimum(1.0, CLIP_NORM / (grad_norm + 1e-06))
    clipped = own_rows * factor
    new_momenta = MOMENTUM * momenta + clipped
    new_params = params - LEARN_RATE * (clipped + MOMENTUM * new_momenta)
    new_averages = AVERAGE_DECAY * averages + (1.0 - AVERAGE_DECAY) * new_params
    return (
        layer_output,
        input_grad,
        grad_norm,
        vector_grads,
        new_params,
        new_momenta,
        new_averages,
    )


def solution(mesh):
    placed = (P("dp", None), P("dp", None), P("dp"), P("dp"), P("dp"), P("dp"), P("dp"), P("dp"))
    return jax.shard_map(
        body,
        mesh=mesh,
        in_specs=placed,
        out_specs=(P("dp", None), P("dp", None), P(), P(), P("dp"), P("dp"), P("dp")),
        check_vma=False,
    )
```

```python
import functools

import jax
import jax.numpy as jnp
from jax import lax
from jax.experimental import pallas as pl
from jax.experimental.pallas import tpu as pltpu
from jax.sharding import PartitionSpec as P

HD = 64
ROW = 1024
EPSILON = 1e-05
CLIP_NORM = 1.0
LEARN_RATE = 20.0
MOMENTUM = 0.5
AVERAGE_DECAY = 0.5
MASKED = -1e30
GELU_IN = 0.7978845608028654
GELU_CUBE = 0.044715

D = 512
FF = 2048
PAIR = 2 * HD
PAIRS = D // PAIR
LANES = 128
WINDOW = 3 * LANES
BLOCK = 16
BLOCKS = D // BLOCK
VECTORS = 12
FIRST_WIDTH = 3 * D + LANES
REST_WIDTH = D + 2 * FF
VMEM_BYTES = 60 * 1024 * 1024

f32 = jnp.float32
bf16 = jnp.bfloat16


def nn(left, right):
    return lax.dot_general(left, right, (((1,), (0,)), ((), ())), preferred_element_type=f32)


def nt(left, right):
    return lax.dot_general(left, right, (((1,), (1,)), ((), ())), preferred_element_type=f32)


def identity(size):
    down = lax.broadcasted_iota(jnp.int32, (size, size), 0)
    across = lax.broadcasted_iota(jnp.int32, (size, size), 1)
    return jnp.where(down == across, 1.0, 0.0).astype(bf16)


def turned(values, unit):
    return nt(unit, values).astype(bf16)


def place_blocks(target, halves, codes, mine, width):
    for half_at, half in enumerate(halves):
        for block_at in range(BLOCKS // 2):
            natural = mine ^ codes[half_at * (BLOCKS // 2) + block_at]
            to_rows = pl.ds(pl.multiple_of(natural * BLOCK, BLOCK), BLOCK)
            target[to_rows, :width] = half[block_at * BLOCK : (block_at + 1) * BLOCK, :width]


def spread_blocks(halves, source, codes, mine, begin, width):
    for half_at, half in enumerate(halves):
        for block_at in range(BLOCKS // 2):
            natural = mine ^ codes[half_at * (BLOCKS // 2) + block_at]
            from_rows = pl.ds(pl.multiple_of(natural * BLOCK, BLOCK), BLOCK)
            half[block_at * BLOCK : (block_at + 1) * BLOCK, begin : begin + width] = source[
                from_rows, :
            ].astype(bf16)


def project_kernel(
    codes, mine_ref, x_ref, near_ref, far_ref,
    xt_ref, qt_ref, kt_ref, vt_ref, k_ref, v_ref, vec_ref, pairs_ref,
    table, turned_weights, columns, rows,
):
    @pl.when(pl.program_id(0) == 0)
    def _():
        place_blocks(table, (near_ref, far_ref), codes, mine_ref[0], FIRST_WIDTH)
        unit = identity(256)
        for kind in range(3):
            for half in range(2):
                turned_weights[kind * D + half * 256 : kind * D + half * 256 + 256, :] = turned(
                    table[:, kind * D + half * 256 : kind * D + half * 256 + 256], unit
                )
        for pair in range(PAIRS):
            for kind in range(3):
                at = pair * 3 * PAIR + kind * PAIR
                pairs_ref[:, at : at + PAIR] = table[
                    :, kind * D + pair * PAIR : kind * D + (pair + 1) * PAIR
                ]
        vectors = table[:, 3 * D :].astype(f32)
        vec_ref[...] = vectors
        columns[0] = jnp.broadcast_to(vectors[:, 0:1], (D, LANES))
        columns[1] = jnp.broadcast_to(vectors[:, 1:2], (D, LANES))
        rows[...] = vectors.T[:8, :]

    x = x_ref[...]
    width = x.shape[0]
    reps = width // LANES
    unit = identity(256)
    for half in range(2):
        xt_ref[half * 256 : half * 256 + 256, :] = turned(x[:, half * 256 : half * 256 + 256], unit)
    bias_q = jnp.concatenate([columns[0]] * reps, axis=1)
    bias_v = jnp.concatenate([columns[1]] * reps, axis=1)
    query = nt(turned_weights[:D, :], x) + bias_q
    qt_ref[...] = (query.astype(bf16).astype(f32) * HD ** (-0.5)).astype(bf16)
    kt_ref[...] = nt(turned_weights[D : 2 * D, :], x).astype(bf16)
    vt_ref[...] = (nt(turned_weights[2 * D :, :], x) + bias_v).astype(bf16)
    k_ref[...] = nn(x, table[:, D : 2 * D]).astype(bf16)
    v_ref[...] = (nn(x, table[:, 2 * D : 3 * D]) + rows[1:2, :]).astype(bf16)


def fill_bias(bias, seg_ref, limits_ref):
    blocks = bias.shape[0]
    lane = lax.broadcasted_iota(jnp.int32, (1, LANES), 1)
    across = lax.broadcasted_iota(jnp.int32, (LANES, LANES), 1)
    down = lax.broadcasted_iota(jnp.int32, (LANES, LANES), 0)

    def codes_of(block):
        row = jnp.where(limits_ref[2] == 1, 0, block // (ROW // LANES))
        limit = jnp.where(row == 0, limits_ref[0], limits_ref[1])
        code = seg_ref[pl.ds(block, 1), :] * 2 + row
        live = lane + block * LANES - row * ROW < limit
        return code.astype(f32), jnp.where(live, code, -1).astype(f32)

    def one_block(block, carry):
        query_code, _ = codes_of(block)
        first = jnp.clip(block - 1, 0, blocks - 3)
        for part in range(3):
            _, key_code = codes_of(first + part)
            key_column = jnp.broadcast_to(key_code, (LANES, LANES)).T
            same = (first + part - block) * LANES
            allowed = (key_column == query_code) | (down + same == across)
            bias[block, part * LANES : (part + 1) * LANES, :] = jnp.where(allowed, 0.0, MASKED)
        return carry

    lax.fori_loop(0, blocks, one_block, 0)


def two_heads(values):
    zeros = jnp.zeros((HD, values.shape[1]), values.dtype)
    left = jnp.concatenate([values[:HD], zeros], axis=0)
    right = jnp.concatenate([zeros, values[HD:]], axis=0)
    return jnp.concatenate([left, right], axis=1)


def own_heads(values):
    return jnp.concatenate([values[:HD, :LANES], values[HD:, LANES:]], axis=0)


def attend_kernel(limits_ref, seg_ref, qt_ref, k_ref, vt_ref, att_ref, logsum_ref, bias):
    @pl.when(pl.program_id(0) == 0)
    def _():
        fill_bias(bias, seg_ref, limits_ref)

    blocks = bias.shape[0]

    def one_block(block, carry):
        here = pl.ds(pl.multiple_of(block * LANES, LANES), LANES)
        begin = pl.multiple_of(jnp.clip(block - 1, 0, blocks - 3) * LANES, LANES)
        window = pl.ds(begin, WINDOW)
        mask = bias[block]
        scores = nn(k_ref[window, :], two_heads(qt_ref[:, here]))
        scores = scores + jnp.concatenate([mask, mask], axis=1)
        highest = jnp.max(scores, axis=0, keepdims=True)
        exponent = jnp.exp(scores - highest)
        total = jnp.sum(exponent, axis=0, keepdims=True)
        outputs = nn(vt_ref[:, window], exponent.astype(bf16)) * (1.0 / total)
        att_ref[:, here] = own_heads(outputs).astype(bf16)
        logsum_ref[0, pl.ds(block, 1), :] = highest + jnp.log(total)
        return carry

    lax.fori_loop(0, blocks, one_block, 0, unroll=2)


def mean_down(values):
    return jnp.sum(values, axis=0, keepdims=True) * (1.0 / D)


def lane_parts(values):
    total = values[:, :LANES]
    for at in range(LANES, values.shape[1], LANES):
        total = total + values[:, at : at + LANES]
    return total


def feed_kernel(
    codes, mine_ref, limits_ref, xt_ref, att_ref, cot_ref, vec_ref, up_bias_ref, near_ref, far_ref,
    layer_ref, ga_ref, both_ref, keep_ref, send_ref, sums_ref,
    table, out_turned, up_turned, down_turned, columns, slopes, hidden, grad_up,
    acc_down, acc_up, acc_out, acc_vec,
):
    step = pl.program_id(0)
    width = xt_ref.shape[1]
    reps = width // LANES
    unit = identity(256)
    chunk = 512

    @pl.when(step == 0)
    def _():
        place_blocks(table, (near_ref, far_ref), codes, mine_ref[0], REST_WIDTH)
        for at in range(0, D, 256):
            out_turned[at : at + 256, :] = turned(table[:, at : at + 256], unit)
        for at in range(0, FF, 256):
            up_turned[at : at + 256, :] = turned(table[:, D + at : D + at + 256], unit)
            down_turned[at : at + 256, :] = turned(table[:, D + FF + at : D + FF + at + 256], unit)
        for kind in range(6):
            columns[kind] = jnp.broadcast_to(vec_ref[:, kind + 2 : kind + 3], (D, LANES))
        acc_down[...] = jnp.zeros_like(acc_down)
        acc_up[...] = jnp.zeros_like(acc_up)
        acc_out[...] = jnp.zeros_like(acc_out)
        acc_vec[...] = jnp.zeros_like(acc_vec)

    def column(kind):
        return jnp.concatenate([columns[kind]] * reps, axis=1)

    place = lax.broadcasted_iota(jnp.int32, (1, width), 1) + step * width
    row = jnp.where(limits_ref[2] == 1, 0, place // ROW)
    limit = jnp.where(row == 0, limits_ref[0], limits_ref[1])
    live = place - row * ROW < limit

    x = xt_ref[...].astype(f32)
    att = att_ref[...]
    z_one = x + nn(table[:, :D], att) + column(0)
    centred = z_one - mean_down(z_one)
    inverse_one = lax.rsqrt(mean_down(centred * centred) + EPSILON)
    normed_one = centred * inverse_one
    first = normed_one * column(2) + column(3)
    first_low = first.astype(bf16)
    z_two = first + x + column(1)
    for at in range(0, FF, chunk):
        bias = jnp.concatenate([up_bias_ref[at : at + chunk, :]] * reps, axis=1)
        pre = nn(up_turned[at : at + chunk, :], first_low) + bias
        square = pre * pre
        tanh = jnp.tanh(pre * (GELU_IN + (GELU_IN * GELU_CUBE) * square))
        half = 0.5 + 0.5 * tanh
        value = pre * half
        slopes[at : at + chunk, :] = half + value * (1.0 - tanh) * (
            GELU_IN + (3.0 * GELU_IN * GELU_CUBE) * square
        )
        hidden[at : at + chunk, :] = value.astype(bf16)
    z_two = z_two + nn(table[:, D + FF :], hidden[...])
    centred = z_two - mean_down(z_two)
    inverse_two = lax.rsqrt(mean_down(centred * centred) + EPSILON)
    normed_two = centred * inverse_two
    gain_two = column(4)
    layer = jnp.where(live, normed_two * gain_two + column(5), 0.0).astype(bf16)
    for at in range(0, width, 256):
        layer_ref[at : at + 256, :] = nt(unit, layer[:, at : at + 256]).astype(bf16)
    cot = jnp.concatenate([nt(unit, cot_ref[:, at : at + 256]) for at in range(0, D, 256)], axis=0)
    cot = jnp.where(live, cot, 0.0)
    scaled = cot * gain_two
    grad_two = inverse_two * (scaled - mean_down(scaled) - normed_two * mean_down(scaled * normed_two))
    grad_feed = grad_two.astype(bf16)
    acc_vec[1] += lane_parts(grad_feed.astype(f32))
    acc_vec[4] += lane_parts(cot * normed_two)
    acc_vec[5] += lane_parts(cot)
    for at in range(0, FF, chunk):
        grad_hidden = nn(down_turned[at : at + chunk, :], grad_feed)
        grad_up[at : at + chunk, :] = (grad_hidden * slopes[at : at + chunk, :]).astype(bf16)
    grad_first = grad_two + nn(table[:, D : D + FF], grad_up[...])
    acc_vec[2] += lane_parts(grad_first * normed_one)
    acc_vec[3] += lane_parts(grad_first)
    scaled = grad_first * column(2)
    grad_one = inverse_one * (scaled - mean_down(scaled) - normed_one * mean_down(scaled * normed_one))
    both_ref[...] = grad_two + grad_one
    grad_branch = grad_one.astype(bf16)
    acc_vec[0] += lane_parts(grad_branch.astype(f32))
    ga_ref[...] = nn(out_turned[...], grad_branch).astype(bf16)
    acc_down[...] += nt(grad_feed, hidden[...])
    ones = jnp.ones((BLOCK, width), bf16)
    acc_up[...] += nt(jnp.concatenate([first_low, ones], axis=0), grad_up[...])
    acc_out[...] += nt(grad_branch, att)

    @pl.when(step == pl.num_programs(0) - 1)
    def _():
        halves = (keep_ref, send_ref)
        spread_blocks(halves, acc_out, codes, mine_ref[0], 0, D)
        spread_blocks(halves, acc_up, codes, mine_ref[0], D, FF)
        spread_blocks(halves, acc_down, codes, mine_ref[0], D + FF, FF)
        for kind in range(6):
            sums_ref[kind : kind + 1, :] = jnp.sum(acc_vec[kind].T, axis=0, keepdims=True)
        sums_ref[6:8, :] = jnp.zeros((2, D), f32)
        for at in range(4):
            sums_ref[8 + at : 9 + at, :] = acc_up[D : D + 1, at * D : (at + 1) * D]
        sums_ref[12:16, :] = jnp.zeros((4, D), f32)


def attend_back_kernel(
    codes, mine_ref, limits_ref, seg_ref, xt_ref, qt_ref, kt_ref, k_ref, v_ref, att_ref, ga_ref,
    logsum_ref, grads_ref, keep_ref, send_ref, sums_ref, bias, acc_key, acc_value, weight_grad,
):
    @pl.when(pl.program_id(0) == 0)
    def _():
        fill_bias(bias, seg_ref, limits_ref)

    blocks = bias.shape[0]
    acc_key[...] = jnp.zeros_like(acc_key)
    acc_value[...] = jnp.zeros_like(acc_value)

    def one_block(block, carry):
        here = pl.ds(pl.multiple_of(block * LANES, LANES), LANES)
        begin = pl.multiple_of(jnp.clip(block - 1, 0, blocks - 3) * LANES, LANES)
        window = pl.ds(begin, WINDOW)
        mask = bias[block]
        query = two_heads(qt_ref[:, here])
        grad_low = ga_ref[:, here]
        grad = two_heads(grad_low)
        product = grad_low.astype(f32) * att_ref[:, here].astype(f32)
        centre = jnp.concatenate(
            [
                jnp.sum(product[:HD], axis=0, keepdims=True),
                jnp.sum(product[HD:], axis=0, keepdims=True),
            ],
            axis=1,
        )
        scores = nn(k_ref[window, :], query) + jnp.concatenate([mask, mask], axis=1)
        chances = jnp.exp(scores - logsum_ref[0, pl.ds(block, 1), :])
        grad_chances = nn(v_ref[window, :], grad)
        grad_scores = (chances * (grad_chances - centre)).astype(bf16)
        grad_query = own_heads(nn(kt_ref[:, window], grad_scores)) * HD ** (-0.5)
        grads_ref[0, :PAIR, here] = grad_query.astype(bf16)
        acc_key[:, window] += nt(query, grad_scores)
        acc_value[:, window] += nt(grad, chances.astype(bf16))
        return carry

    lax.fori_loop(0, blocks, one_block, 0, unroll=2)
    grads_ref[0, PAIR : 2 * PAIR, :] = acc_key[...].astype(bf16)
    grads_ref[0, 2 * PAIR :, :] = acc_value[...].astype(bf16)
    grads = grads_ref[0]
    weight_grad[...] = nt(xt_ref[...], grads)
    spread_blocks((keep_ref, send_ref), weight_grad, codes, mine_ref[0], 0, 3 * PAIR)
    sums_ref[0] = nt(jnp.ones((BLOCK, grads.shape[1]), bf16), grads)[:8]


def input_kernel(grads_ref, weights_ref, both_ref, out_ref):
    total = both_ref[...]
    for pair in range(PAIRS):
        total = total + nn(weights_ref[:, pair * 3 * PAIR : (pair + 1) * 3 * PAIR], grads_ref[pair])
    unit = identity(256)
    high = total.astype(bf16)
    rest = (total - high.astype(f32)).astype(bf16)
    for at in range(0, total.shape[1], 256):
        out_ref[at : at + 256, :] = nt(unit, high[:, at : at + 256]) + nt(unit, rest[:, at : at + 256])


def exchange(values, bit, count):
    return lax.ppermute(values, "dp", [(at, at ^ bit) for at in range(count)])


def gather_halves(block, count):
    bit = count // 2
    while bit > 1:
        block = jnp.concatenate([block, exchange(block, bit, count)], axis=0)
        bit //= 2
    return block, exchange(block, 1, count)


def scatter_sum(keep, send, count):
    bit = 1
    while True:
        arrived = exchange(send, bit, count)
        total = keep.astype(f32) + arrived.astype(f32)
        bit *= 2
        if bit == count:
            return total
        half = total.shape[0] // 2
        total = total.astype(bf16)
        keep, send = total[:half], total[half:]


def sum_everywhere(values, count):
    bit = 1
    while bit < count:
        values = values + exchange(values, bit, count)
        bit *= 2
    return values


def reversed_bits(count):
    width = count.bit_length() - 1
    return [sum(((at >> k) & 1) << (width - 1 - k) for k in range(width)) for at in range(count)]


def whole(shape):
    return pl.BlockSpec(shape, lambda *at: (0,) * len(shape))


def smem():
    return pl.BlockSpec(memory_space=pltpu.SMEM)


def shaped(shape, dtype):
    return jax.ShapeDtypeStruct(shape, dtype)


def params_of(**more):
    return pltpu.CompilerParams(vmem_limit_bytes=VMEM_BYTES, **more)


def body(tokens, cotangent, segment_ids, row_lengths, row_widths, params, momenta, averages):
    slots = tokens.shape[0]
    count = lax.axis_size("dp")
    mine = lax.axis_index("dp").astype(jnp.int32)
    own_count = D // count
    table_width = params.shape[0] // own_count
    blocks = slots // LANES
    direct = own_count == BLOCK
    if direct:
        codes = reversed_bits(count)
        origin = mine.reshape(1)
    else:
        codes = list(range(BLOCKS))
        origin = jnp.zeros((1,), jnp.int32)
        reverse = jnp.array(reversed_bits(count), jnp.int32)

    def to_kernel(near, far):
        if direct:
            return near, far
        table = jnp.concatenate([near, far], axis=0).reshape(count, own_count, -1)
        table = jnp.take(table, reverse[jnp.arange(count) ^ mine], axis=0).reshape(D, -1)
        return table[: D // 2], table[D // 2 :]

    def from_kernel(keep, send):
        if direct:
            return keep, send
        table = jnp.concatenate([keep, send], axis=0).reshape(count, own_count, -1)
        table = jnp.take(table, reverse ^ mine, axis=0).reshape(D, -1)
        return table[: D // 2], table[D // 2 :]

    own_table = params.astype(bf16).reshape(own_count, table_width)
    own_first = jnp.concatenate(
        [
            own_table[:, : 3 * D],
            jnp.pad(own_table[:, 12 * D :], ((0, 0), (0, LANES - VECTORS))),
        ],
        axis=1,
    )
    first_near, first_far = to_kernel(*gather_halves(own_first, count))
    rest_near, rest_far = to_kernel(*gather_halves(own_table[:, 3 * D : 12 * D], count))
    limits = jnp.concatenate([row_lengths, row_widths])
    segments = segment_ids.reshape(blocks, LANES)

    tile = 256
    steps = slots // tile
    across = pl.BlockSpec((D, tile), lambda at: (0, at))
    down = pl.BlockSpec((tile, D), lambda at: (at, 0))
    half_first = whole((D // 2, FIRST_WIDTH))
    xt, qt, kt, vt, key, value, vectors, pair_weights = pl.pallas_call(
        functools.partial(project_kernel, codes),
        grid=(steps,),
        in_specs=[smem(), down, half_first, half_first],
        out_specs=[across] * 4 + [down] * 2 + [whole((D, LANES)), whole((D, 3 * D))],
        out_shape=[shaped((D, slots), bf16)] * 4
        + [shaped((slots, D), bf16)] * 2
        + [shaped((D, LANES), f32), shaped((D, 3 * D), bf16)],
        scratch_shapes=[
            pltpu.VMEM((D, FIRST_WIDTH), bf16),
            pltpu.VMEM((3 * D, D), bf16),
            pltpu.VMEM((2, D, LANES), f32),
            pltpu.VMEM((8, D), f32),
        ],
        compiler_params=params_of(),
        name="project",
    )(origin, tokens, first_near, first_far)

    pair_rows = pl.BlockSpec((PAIR, slots), lambda at: (at, 0))
    pair_columns = pl.BlockSpec((slots, PAIR), lambda at: (0, at))
    sums_block = pl.BlockSpec((1, blocks, 2 * LANES), lambda at: (at, 0, 0))
    attended, logsum = pl.pallas_call(
        attend_kernel,
        grid=(PAIRS,),
        in_specs=[smem(), whole((blocks, LANES)), pair_rows, pair_columns, pair_rows],
        out_specs=[pair_rows, sums_block],
        out_shape=[shaped((D, slots), bf16), shaped((PAIRS, blocks, 2 * LANES), f32)],
        scratch_shapes=[pltpu.VMEM((blocks, WINDOW, LANES), f32)],
        compiler_params=params_of(),
        name="attend",
    )(limits, segments, qt, key, vt)

    up_bias = jnp.broadcast_to(vectors[:, 8:VECTORS].reshape(FF, 1), (FF, LANES))
    half_rest = whole((D // 2, REST_WIDTH))
    layer_output, grad_attended, grad_both, keep_rest, send_rest, feed_sums = pl.pallas_call(
        functools.partial(feed_kernel, codes),
        grid=(steps,),
        in_specs=[
            smem(), smem(), across, across, down,
            whole((D, LANES)), whole((FF, LANES)), half_rest, half_rest,
        ],
        out_specs=[down, across, across, half_rest, half_rest, whole((16, D))],
        out_shape=[
            shaped((slots, D), bf16),
            shaped((D, slots), bf16),
            shaped((D, slots), f32),
            shaped((D // 2, REST_WIDTH), bf16),
            shaped((D // 2, REST_WIDTH), bf16),
            shaped((16, D), f32),
        ],
        scratch_shapes=[
            pltpu.VMEM((D, REST_WIDTH), bf16),
            pltpu.VMEM((D, D), bf16),
            pltpu.VMEM((FF, D), bf16),
            pltpu.VMEM((FF, D), bf16),
            pltpu.VMEM((6, D, LANES), f32),
            pltpu.VMEM((FF, tile), f32),
            pltpu.VMEM((FF, tile), bf16),
            pltpu.VMEM((FF, tile), bf16),
            pltpu.VMEM((D, FF), f32),
            pltpu.VMEM((D + BLOCK, FF), f32),
            pltpu.VMEM((D, D), f32),
            pltpu.VMEM((6, D, LANES), f32),
        ],
        compiler_params=params_of(),
        name="feed",
    )(origin, limits, xt, attended, cotangent, vectors, up_bias, rest_near, rest_far)

    own_rest = scatter_sum(*from_kernel(keep_rest, send_rest), count)
    feed_sums = sum_everywhere(feed_sums, count)

    half_pairs = pl.BlockSpec((D // 2, 3 * PAIR), lambda at: (0, at))
    grads, keep_first, send_first, pair_sums = pl.pallas_call(
        functools.partial(attend_back_kernel, codes),
        grid=(PAIRS,),
        in_specs=[
            smem(), smem(), whole((blocks, LANES)), whole((D, slots)),
            pair_rows, pair_rows, pair_columns, pair_columns, pair_rows, pair_rows, sums_block,
        ],
        out_specs=[
            pl.BlockSpec((1, 3 * PAIR, slots), lambda at: (at, 0, 0)),
            half_pairs,
            half_pairs,
            pl.BlockSpec((1, 8, 3 * PAIR), lambda at: (at, 0, 0)),
        ],
        out_shape=[
            shaped((PAIRS, 3 * PAIR, slots), bf16),
            shaped((D // 2, 3 * D), bf16),
            shaped((D // 2, 3 * D), bf16),
            shaped((PAIRS, 8, 3 * PAIR), f32),
        ],
        scratch_shapes=[
            pltpu.VMEM((blocks, WINDOW, LANES), f32),
            pltpu.VMEM((PAIR, slots), f32),
            pltpu.VMEM((PAIR, slots), f32),
            pltpu.VMEM((D, 3 * PAIR), f32),
        ],
        compiler_params=params_of(),
        name="attend_back",
    )(origin, limits, segments, xt, qt, kt, key, value, attended, grad_attended, logsum)

    own_first_grad = scatter_sum(*from_kernel(keep_first, send_first), count)
    pair_sums = sum_everywhere(pair_sums[:, 0, :], count)

    input_grad = pl.pallas_call(
        input_kernel,
        grid=(steps,),
        in_specs=[
            pl.BlockSpec((PAIRS, 3 * PAIR, tile), lambda at: (0, 0, at)),
            whole((D, 3 * D)),
            across,
        ],
        out_specs=down,
        out_shape=shaped((slots, D), f32),
        compiler_params=params_of(),
        name="input_grad",
    )(grads, pair_weights, grad_both)

    pair_sums = pair_sums.reshape(PAIRS, 3, PAIR)
    vector_grads = jnp.concatenate(
        [
            jnp.stack([pair_sums[:, 0].reshape(D), pair_sums[:, 2].reshape(D)], axis=1),
            feed_sums[:6].T,
            feed_sums[8:12].reshape(D, 4),
        ],
        axis=1,
    )
    own_first_grad = own_first_grad.reshape(own_count, PAIRS, 3, PAIR)
    own_first_grad = own_first_grad.transpose(0, 2, 1, 3).reshape(own_count, 3 * D)
    squares = jnp.sum(own_first_grad * own_first_grad) + jnp.sum(own_rest * own_rest)
    squares = sum_everywhere(squares.reshape(1, 1), count)[0, 0]
    grad_norm = jnp.sqrt(squares + jnp.sum(vector_grads * vector_grads))
    own_vectors = lax.dynamic_slice_in_dim(vector_grads, mine * own_count, own_count)
    own_grad = jnp.concatenate([own_first_grad, own_rest, own_vectors], axis=1).reshape(-1)
    clipped = own_grad * jnp.minimum(1.0, CLIP_NORM / (grad_norm + 1e-06))
    new_momenta = MOMENTUM * momenta + clipped
    new_params = params - LEARN_RATE * (clipped + MOMENTUM * new_momenta)
    new_averages = AVERAGE_DECAY * averages + (1.0 - AVERAGE_DECAY) * new_params
    return (
        layer_output, input_grad, grad_norm, vector_grads, new_params, new_momenta, new_averages,
    )


def solution(mesh):
    placed = (P("dp", None), P("dp", None), P("dp"), P("dp"), P("dp"), P("dp"), P("dp"), P("dp"))
    return jax.shard_map(
        body,
        mesh=mesh,
        in_specs=placed,
        out_specs=(P("dp", None), P("dp", None), P(), P(), P("dp"), P("dp"), P("dp")),
        check_vma=False,
    )
```

```python
import functools

import jax
import jax.numpy as jnp
from jax import lax
from jax.experimental import pallas as pl
from jax.experimental.pallas import tpu as pltpu
from jax.sharding import PartitionSpec as P

HD = 64
ROW = 1024
EPSILON = 1e-05
CLIP_NORM = 1.0
LEARN_RATE = 20.0
MOMENTUM = 0.5
AVERAGE_DECAY = 0.5
MASKED = -1e30
GELU_IN = 0.7978845608028654
GELU_CUBE = 0.044715

D = 512
FF = 2048
PAIR = 2 * HD
PAIRS = D // PAIR
LANES = 128
WINDOW = 3 * LANES
BLOCK = 16
BLOCKS = D // BLOCK
VECTORS = 12
TILE = 256
FIRST_WIDTH = 3 * D + LANES
REST_WIDTH = D + 2 * FF
VMEM_BYTES = 60 * 1024 * 1024

f32 = jnp.float32
bf16 = jnp.bfloat16


def nn(left, right):
    return lax.dot_general(left, right, (((1,), (0,)), ((), ())), preferred_element_type=f32)


def nt(left, right):
    return lax.dot_general(left, right, (((1,), (1,)), ((), ())), preferred_element_type=f32)


def identity(size):
    down = lax.broadcasted_iota(jnp.int32, (size, size), 0)
    across = lax.broadcasted_iota(jnp.int32, (size, size), 1)
    return jnp.where(down == across, 1.0, 0.0).astype(bf16)


def turned(values, unit):
    return nt(unit, values).astype(bf16)


def place_blocks(target, halves, codes, mine, width):
    for half_at, half in enumerate(halves):
        for block_at in range(BLOCKS // 2):
            natural = mine ^ codes[half_at * (BLOCKS // 2) + block_at]
            to_rows = pl.ds(pl.multiple_of(natural * BLOCK, BLOCK), BLOCK)
            target[to_rows, :width] = half[block_at * BLOCK : (block_at + 1) * BLOCK, :width]


def spread_blocks(halves, source, codes, mine, begin, width):
    for half_at, half in enumerate(halves):
        for block_at in range(BLOCKS // 2):
            natural = mine ^ codes[half_at * (BLOCKS // 2) + block_at]
            from_rows = pl.ds(pl.multiple_of(natural * BLOCK, BLOCK), BLOCK)
            rows = slice(block_at * BLOCK, (block_at + 1) * BLOCK)
            half[rows, pl.ds(begin, width)] = source[from_rows, :].astype(bf16)


def project_kernel(
    codes, mine_ref, x_ref, near_ref, far_ref,
    xt_ref, qt_ref, kt_ref, vt_ref, k_ref, v_ref, vec_ref, pairs_ref,
    table, turned_weights, columns, rows,
):
    @pl.when(pl.program_id(0) == 0)
    def _():
        place_blocks(table, (near_ref, far_ref), codes, mine_ref[0], FIRST_WIDTH)
        unit = identity(256)
        for kind in range(3):
            for half in range(2):
                turned_weights[kind * D + half * 256 : kind * D + half * 256 + 256, :] = turned(
                    table[:, kind * D + half * 256 : kind * D + half * 256 + 256], unit
                )
        for pair in range(PAIRS):
            for kind in range(3):
                at = pair * 3 * PAIR + kind * PAIR
                pairs_ref[:, at : at + PAIR] = table[
                    :, kind * D + pair * PAIR : kind * D + (pair + 1) * PAIR
                ]
        vectors = table[:, 3 * D :].astype(f32)
        vec_ref[...] = vectors
        columns[0] = jnp.broadcast_to(vectors[:, 0:1], (D, LANES))
        columns[1] = jnp.broadcast_to(vectors[:, 1:2], (D, LANES))
        rows[...] = vectors.T[:8, :]

    x = x_ref[...]
    width = x.shape[0]
    reps = width // LANES
    unit = identity(256)
    for half in range(2):
        xt_ref[half * 256 : half * 256 + 256, :] = turned(x[:, half * 256 : half * 256 + 256], unit)
    bias_q = jnp.concatenate([columns[0]] * reps, axis=1)
    bias_v = jnp.concatenate([columns[1]] * reps, axis=1)
    query = nt(turned_weights[:D, :], x) + bias_q
    qt_ref[...] = (query.astype(bf16).astype(f32) * HD ** (-0.5)).astype(bf16)
    kt_ref[...] = nt(turned_weights[D : 2 * D, :], x).astype(bf16)
    vt_ref[...] = (nt(turned_weights[2 * D :, :], x) + bias_v).astype(bf16)
    k_ref[...] = nn(x, table[:, D : 2 * D]).astype(bf16)
    v_ref[...] = (nn(x, table[:, 2 * D : 3 * D]) + rows[1:2, :]).astype(bf16)


def fill_bias(bias, seg_ref, limits_ref):
    blocks = bias.shape[0]
    lane = lax.broadcasted_iota(jnp.int32, (1, LANES), 1)
    across = lax.broadcasted_iota(jnp.int32, (LANES, LANES), 1)
    down = lax.broadcasted_iota(jnp.int32, (LANES, LANES), 0)

    def codes_of(block):
        row = jnp.where(limits_ref[2] == 1, 0, block // (ROW // LANES))
        limit = jnp.where(row == 0, limits_ref[0], limits_ref[1])
        code = seg_ref[pl.ds(block, 1), :] * 2 + row
        live = lane + block * LANES - row * ROW < limit
        return code.astype(f32), jnp.where(live, code, -1).astype(f32)

    def one_block(block, carry):
        query_code, _ = codes_of(block)
        first = jnp.clip(block - 1, 0, blocks - 3)
        for part in range(3):
            _, key_code = codes_of(first + part)
            key_column = jnp.broadcast_to(key_code, (LANES, LANES)).T
            same = (first + part - block) * LANES
            allowed = (key_column == query_code) | (down + same == across)
            bias[block, part * LANES : (part + 1) * LANES, :] = jnp.where(allowed, 0.0, MASKED)
        return carry

    lax.fori_loop(0, blocks, one_block, 0)


def two_heads(values):
    zeros = jnp.zeros((HD, values.shape[1]), values.dtype)
    left = jnp.concatenate([values[:HD], zeros], axis=0)
    right = jnp.concatenate([zeros, values[HD:]], axis=0)
    return jnp.concatenate([left, right], axis=1)


def own_heads(values):
    return jnp.concatenate([values[:HD, :LANES], values[HD:, LANES:]], axis=0)


def down_tree(values, combine):
    rows = values.shape[0]
    if rows == WINDOW:
        values = combine(
            combine(values[:LANES], values[LANES : 2 * LANES]), values[2 * LANES : 3 * LANES]
        )
        rows = LANES
    while rows > 8:
        rows //= 2
        values = combine(values[:rows], values[rows : 2 * rows])
    return values


def top_down(values):
    return jnp.max(down_tree(values, jnp.maximum), axis=0, keepdims=True)


def sum_down(values):
    return jnp.sum(down_tree(values, jnp.add), axis=0, keepdims=True)


def places(block, blocks):
    begin = min(max(block - 1, 0), blocks - 3) * LANES
    return slice(block * LANES, (block + 1) * LANES), slice(begin, begin + WINDOW)


def pipelined(amount, *stages):
    depth = len(stages)
    held = {}
    for step in range(amount + depth - 1):
        for at, stage in enumerate(stages):
            item = step - at
            if 0 <= item < amount:
                held[item] = stage(item, held.get(item))
                if at == depth - 1:
                    del held[item]


def attend_kernel(limits_ref, seg_ref, qt_ref, k_ref, vt_ref, att_ref, logsum_ref, bias):
    @pl.when(pl.program_id(0) == 0)
    def _():
        fill_bias(bias, seg_ref, limits_ref)

    blocks = bias.shape[0]

    def score(block, _):
        here, window = places(block, blocks)
        mask = bias[block]
        scores = nn(k_ref[window, :], two_heads(qt_ref[:, here]))
        return scores + jnp.concatenate([mask, mask], axis=1)

    def finish(block, scores):
        here, window = places(block, blocks)
        highest = top_down(scores)
        exponent = jnp.exp(scores - highest)
        total = sum_down(exponent)
        outputs = nn(vt_ref[:, window], exponent.astype(bf16)) * (1.0 / total)
        att_ref[:, here] = own_heads(outputs).astype(bf16)
        logsum_ref[0, block : block + 1, :] = highest + jnp.log(total)

    pipelined(blocks, score, finish)


def mean_down(values):
    return sum_down(values) * (1.0 / D)


def lane_parts(values):
    return values[:, :LANES] + values[:, LANES:]


def weight_parts(kept, acc_down, acc_up, acc_out):
    hidden, grad_up, first_low, grad_feed, grad_branch, att = kept

    def part(target, left, right, at):
        def run():
            target[:, at : at + TILE] += nt(left[...], right[at : at + TILE, :])

        return run

    parts = [part(acc_down, grad_feed, hidden, at) for at in range(0, FF, TILE)]
    parts += [part(acc_up, first_low, grad_up, at) for at in range(0, FF, TILE)]
    parts += [part(acc_out, grad_branch, att, at) for at in range(0, D, TILE)]
    return parts


def feed_kernel(
    codes, mine_ref, limits_ref, xt_ref, att_ref, cot_ref, vec_ref, near_ref, far_ref,
    layer_ref, ga_ref, both_ref, keep_ref, send_ref, sums_ref,
    table, out_turned, up_turned, down_turned, columns, up_bias, slopes,
    acc_down, acc_up, acc_out, acc_vec, *kept,
):
    step = pl.program_id(0)
    unit = identity(TILE)
    chunk = 512
    chunks = FF // chunk
    each = len(kept) // 2

    @pl.when(step == 0)
    def _():
        place_blocks(table, (near_ref, far_ref), codes, mine_ref[0], REST_WIDTH)
        for at in range(0, D, TILE):
            out_turned[at : at + TILE, :] = turned(table[:, at : at + TILE], unit)
        for at in range(0, FF, TILE):
            up_turned[at : at + TILE, :] = turned(table[:, D + at : D + at + TILE], unit)
            down_turned[at : at + TILE, :] = turned(
                table[:, D + FF + at : D + FF + at + TILE], unit
            )
        for kind in range(6):
            columns[kind] = jnp.broadcast_to(vec_ref[:, kind + 2 : kind + 3], (D, LANES))
        for at in range(4):
            up_bias[pl.ds(at, D, stride=4), :] = jnp.broadcast_to(
                vec_ref[:, 8 + at : 9 + at], (D, LANES)
            )
        for buffer in (acc_down, acc_up, acc_out, acc_vec) + kept[each:]:
            buffer[...] = jnp.zeros_like(buffer)
        for buffer in (kept[2], kept[each + 2]):
            buffer[D:, :] = jnp.ones((BLOCK, TILE), bf16)

    def column(kind):
        return jnp.concatenate([columns[kind]] * 2, axis=1)

    def one_tile(tile, now, before):
        hidden, grad_up, first_keep, feed_keep, branch_keep, att_keep = now
        fill = weight_parts(before, acc_down, acc_up, acc_out)
        here = slice(tile * TILE, (tile + 1) * TILE)
        place = lax.broadcasted_iota(jnp.int32, (1, TILE), 1) + (step * 2 + tile) * TILE
        row = jnp.where(limits_ref[2] == 1, 0, place // ROW)
        limit = jnp.where(row == 0, limits_ref[0], limits_ref[1])
        live = place - row * ROW < limit

        x = xt_ref[:, here].astype(f32)
        att = att_ref[:, here]
        att_keep[...] = att
        z_one = x + nn(table[:, :D], att) + column(0)
        for part in fill[:5]:
            part()
        centred = z_one - mean_down(z_one)
        inverse_one = lax.rsqrt(mean_down(centred * centred) + EPSILON)
        normed_one = centred * inverse_one
        first = normed_one * column(2) + column(3)
        first_low = first.astype(bf16)
        first_keep[:D, :] = first_low
        partial = [first + x + column(1)]

        def widen(at, _):
            rows = slice(at * chunk, (at + 1) * chunk)
            bias = jnp.concatenate([up_bias[rows, :]] * 2, axis=1)
            return nn(up_turned[rows, :], first_low) + bias

        def bend(at, pre):
            rows = slice(at * chunk, (at + 1) * chunk)
            square = pre * pre
            tanh = jnp.tanh(pre * (GELU_IN + (GELU_IN * GELU_CUBE) * square))
            half = 0.5 + 0.5 * tanh
            value = pre * half
            slopes[rows, :] = half + value * (1.0 - tanh) * (
                GELU_IN + (3.0 * GELU_IN * GELU_CUBE) * square
            )
            low = value.astype(bf16)
            hidden[rows, :] = low
            return low

        def narrow(at, low):
            columns_at = slice(D + FF + at * chunk, D + FF + (at + 1) * chunk)
            partial[0] = partial[0] + nn(table[:, columns_at], low)

        pipelined(chunks, widen, bend, narrow)
        z_two = partial[0]
        cot = jnp.concatenate(
            [nt(unit, cot_ref[here, at : at + TILE]) for at in range(0, D, TILE)], axis=0
        )
        for part in fill[5:13]:
            part()
        centred = z_two - mean_down(z_two)
        inverse_two = lax.rsqrt(mean_down(centred * centred) + EPSILON)
        normed_two = centred * inverse_two
        gain_two = column(4)
        layer = jnp.where(live, normed_two * gain_two + column(5), 0.0).astype(bf16)
        cot = jnp.where(live, cot, 0.0)
        scaled = cot * gain_two
        grad_two = inverse_two * (
            scaled - mean_down(scaled) - normed_two * mean_down(scaled * normed_two)
        )
        grad_feed = grad_two.astype(bf16)
        feed_keep[...] = grad_feed
        acc_vec[1] += lane_parts(grad_feed.astype(f32))
        acc_vec[4] += lane_parts(cot * normed_two)
        acc_vec[5] += lane_parts(cot)
        partial[0] = grad_two

        def widen_back(at, _):
            return nn(down_turned[at * chunk : (at + 1) * chunk, :], grad_feed)

        def bend_back(at, grad_hidden):
            rows = slice(at * chunk, (at + 1) * chunk)
            low = (grad_hidden * slopes[rows, :]).astype(bf16)
            grad_up[rows, :] = low
            return low

        def narrow_back(at, low):
            partial[0] = partial[0] + nn(table[:, D + at * chunk : D + (at + 1) * chunk], low)

        pipelined(chunks, widen_back, bend_back, narrow_back)
        grad_first = partial[0]
        layer_ref[here, :] = nt(unit, layer).astype(bf16)
        for part in fill[13:]:
            part()
        acc_vec[2] += lane_parts(grad_first * normed_one)
        acc_vec[3] += lane_parts(grad_first)
        scaled = grad_first * column(2)
        grad_one = inverse_one * (
            scaled - mean_down(scaled) - normed_one * mean_down(scaled * normed_one)
        )
        both_ref[:, here] = grad_two + grad_one
        grad_branch = grad_one.astype(bf16)
        branch_keep[...] = grad_branch
        acc_vec[0] += lane_parts(grad_branch.astype(f32))
        ga_ref[:, here] = nn(out_turned[...], grad_branch).astype(bf16)

    one_tile(0, kept[:each], kept[each:])
    one_tile(1, kept[each:], kept[:each])

    @pl.when(step == pl.num_programs(0) - 1)
    def _():
        for part in weight_parts(kept[each:], acc_down, acc_up, acc_out):
            part()
        halves = (keep_ref, send_ref)
        spread_blocks(halves, acc_out, codes, mine_ref[0], 0, D)
        spread_blocks(halves, acc_up, codes, mine_ref[0], D, FF)
        spread_blocks(halves, acc_down, codes, mine_ref[0], D + FF, FF)
        up_sums = jnp.broadcast_to(acc_up[D : D + 1, :], (LANES, FF))
        for at in range(0, FF, LANES):
            up_bias[at : at + LANES, :] = up_sums[:, at : at + LANES].T
        lane = lax.broadcasted_iota(jnp.int32, (D, LANES), 1)
        vectors = jnp.zeros((D, LANES), f32)
        for kind in range(6):
            total = jnp.sum(acc_vec[kind], axis=1, keepdims=True)
            vectors = jnp.where(lane == kind + 2, total, vectors)
        for at in range(4):
            vectors = jnp.where(lane == 8 + at, up_bias[pl.ds(at, D, stride=4), :], vectors)
        sums_ref[...] = vectors


def attend_back_kernel(
    codes, mine_ref, limits_ref, seg_ref, xt_ref, qt_ref, kt_ref, k_ref, v_ref, att_ref, ga_ref,
    logsum_ref, sums_ref, grads_ref, keep_ref, send_ref, bias, acc_key, acc_value, weight_grad,
    vectors,
):
    pair = pl.program_id(0)

    @pl.when(pair == 0)
    def _():
        fill_bias(bias, seg_ref, limits_ref)

    blocks = bias.shape[0]
    acc_key[...] = jnp.zeros_like(acc_key)
    acc_value[...] = jnp.zeros_like(acc_value)

    def score(block, _):
        here, window = places(block, blocks)
        mask = bias[block]
        query = two_heads(qt_ref[:, here])
        grad = two_heads(ga_ref[:, here])
        scores = nn(k_ref[window, :], query) + jnp.concatenate([mask, mask], axis=1)
        return query, grad, scores, nn(v_ref[window, :], grad)

    def finish(block, held):
        query, grad, scores, grad_chances = held
        here, window = places(block, blocks)
        product = ga_ref[:, here].astype(f32) * att_ref[:, here].astype(f32)
        centre = jnp.concatenate([sum_down(product[:HD]), sum_down(product[HD:])], axis=1)
        chances = jnp.exp(scores - logsum_ref[0, block : block + 1, :])
        grad_scores = (chances * (grad_chances - centre)).astype(bf16)
        acc_value[:, window] += nt(grad, chances.astype(bf16))
        grad_query = own_heads(nn(kt_ref[:, window], grad_scores)) * HD ** (-0.5)
        grads_ref[0, :PAIR, here] = grad_query.astype(bf16)
        acc_key[:, window] += nt(query, grad_scores)

    pipelined(blocks, score, finish)
    grads_ref[0, PAIR : 2 * PAIR, :] = acc_key[...].astype(bf16)
    grads_ref[0, 2 * PAIR :, :] = acc_value[...].astype(bf16)
    grads = grads_ref[0]
    weight_grad[...] = nt(xt_ref[...], grads)
    halves = (keep_ref, send_ref)
    begin = pl.multiple_of(pair * (3 * PAIR), 3 * PAIR)
    spread_blocks(halves, weight_grad, codes, mine_ref[0], begin, 3 * PAIR)
    rows = pl.ds(pl.multiple_of(pair * PAIR, PAIR), PAIR)
    lane = lax.broadcasted_iota(jnp.int32, (PAIR, LANES), 1)
    query_sum = jnp.sum(grads[:PAIR].astype(f32), axis=1, keepdims=True)
    value_sum = jnp.sum(grads[2 * PAIR :].astype(f32), axis=1, keepdims=True)
    total = jnp.where(lane == 0, query_sum, jnp.where(lane == 1, value_sum, sums_ref[rows, :]))
    high = total.astype(bf16).astype(f32)
    vectors[rows, :LANES] = high
    vectors[rows, LANES:] = total - high

    @pl.when(pair == PAIRS - 1)
    def _():
        spread_blocks(halves, vectors, codes, mine_ref[0], 3 * D, 2 * LANES)


def input_kernel(grads_ref, weights_ref, both_ref, out_ref):
    unit = identity(TILE)
    width = both_ref.shape[1]

    def multiply(at, _):
        here = slice(at * TILE, (at + 1) * TILE)
        grads = jnp.concatenate([grads_ref[pair, :, here] for pair in range(PAIRS)], axis=0)
        return both_ref[:, here] + nn(weights_ref[...], grads)

    def turn(at, total):
        high = total.astype(bf16)
        rest = (total - high.astype(f32)).astype(bf16)
        out_ref[at * TILE : (at + 1) * TILE, :] = nt(unit, high) + nt(unit, rest)

    pipelined(width // TILE, multiply, turn)


def own_kernel(*refs):
    own_ref, share_ref = refs[-2:]
    rest_ref = refs[-3]
    total = sum(part[...].astype(f32) for part in refs[:-3])
    squares = jnp.sum(rest_ref[...] * rest_ref[...], axis=1, keepdims=True)
    for pair in range(PAIRS):
        for kind in range(3):
            at = pair * 3 * PAIR + kind * PAIR
            piece = total[:, at : at + PAIR]
            own_ref[:, kind * D + pair * PAIR : kind * D + (pair + 1) * PAIR] = piece
            squares = squares + jnp.sum(piece * piece, axis=1, keepdims=True)
    vectors = total[:, -2 * LANES : -LANES] + total[:, -LANES:]
    lane = lax.broadcasted_iota(jnp.int32, vectors.shape, 1)
    vectors = jnp.where(lane < VECTORS, vectors, 0.0)
    squares = squares + jnp.sum(vectors * vectors, axis=1, keepdims=True)
    share_ref[...] = jnp.where(lane == VECTORS, squares, vectors)


def settle_kernel(codes, mine_ref, near_ref, far_ref, vectors_ref, norm_ref, table):
    place_blocks(table, (near_ref, far_ref), codes, mine_ref[0], LANES)
    vectors_ref[...] = table[...].T[:VECTORS, :]
    squares = jnp.sum(table[...], axis=0, keepdims=True)[:, VECTORS : VECTORS + 1]
    norm_ref[...] = jnp.broadcast_to(jnp.sqrt(squares), (8, LANES))


def exchange(values, bit, count):
    return lax.ppermute(values, "dp", [(at, at ^ bit) for at in range(count)])


def mask_phases(count):
    bits = [1 << at for at in range(1, count.bit_length() - 1)]
    phases = [bits[at : at + 2] for at in range(0, len(bits), 2)]
    return [[0, 1]] + [
        [sum(bit for at, bit in enumerate(phase) if choice >> at & 1) for choice in range(1 << len(phase))]
        for phase in phases
    ]


def block_codes(count):
    codes = [0]
    for masks in reversed(mask_phases(count)):
        codes = [mask ^ code for mask in masks for code in codes]
    return codes


def gather_phase(block, masks, count):
    return [block] + [exchange(block, mask, count) for mask in masks[1:]]


def scatter_phase(pieces, masks, count):
    return [pieces[0]] + [
        exchange(piece, mask, count) for piece, mask in zip(pieces[1:], masks[1:], strict=True)
    ]


def with_vectors(total):
    vectors = total[:, -2 * LANES : -LANES] + total[:, -LANES:]
    high = vectors.astype(bf16).astype(f32)
    before = [total[:, : -2 * LANES]] if total.shape[1] > 2 * LANES else []
    return jnp.concatenate(before + [high, vectors - high], axis=1)


def cut_kernel(*refs):
    width = refs[0].shape[1]
    rows = refs[-1].shape[0]
    amount = refs[0].shape[0] // rows
    pieces = refs[len(refs) - amount :]
    parts = refs[: len(refs) - amount]
    for at, piece in enumerate(pieces):
        for begin in range(0, width, 2 * LANES):
            here = slice(begin, begin + 2 * LANES)
            total = sum(part[at * rows : (at + 1) * rows, here].astype(f32) for part in parts)
            if begin + 2 * LANES == width:
                total = with_vectors(total)
            piece[:, here] = total.astype(piece.dtype)


def cut_sum(parts, amount, dtype, holds_vectors):
    rows, width = parts[0].shape
    few = rows // amount
    if few % BLOCK or not holds_vectors:
        total = sum(part.astype(f32) for part in parts)
        total = (with_vectors(total) if holds_vectors else total).astype(dtype)
        return [total[at * few : (at + 1) * few] for at in range(amount)]
    return pl.pallas_call(
        cut_kernel,
        out_shape=[shaped((few, width), dtype)] * amount,
        compiler_params=params_of(),
        name="cut",
    )(*parts)


def together(*values):
    return lax.optimization_barrier(values)


def whole(shape):
    return pl.BlockSpec(shape, lambda *at: (0,) * len(shape))


def smem():
    return pl.BlockSpec(memory_space=pltpu.SMEM)


def shaped(shape, dtype):
    return jax.ShapeDtypeStruct(shape, dtype)


def params_of(**more):
    return pltpu.CompilerParams(vmem_limit_bytes=VMEM_BYTES, **more)


def body(tokens, cotangent, segment_ids, row_lengths, row_widths, params, momenta, averages):
    slots = tokens.shape[0]
    count = lax.axis_size("dp")
    mine = lax.axis_index("dp").astype(jnp.int32)
    own_count = D // count
    table_width = params.shape[0] // own_count
    blocks = slots // LANES
    direct = own_count == BLOCK
    if direct:
        codes = block_codes(count)
        origin = mine.reshape(1)
    else:
        codes = list(range(BLOCKS))
        origin = jnp.zeros((1,), jnp.int32)
        spread = jnp.array(block_codes(count), jnp.int32)
        places_of = jnp.argsort(spread)

    def to_kernel(near, far):
        if direct:
            return near, far
        table = jnp.concatenate([near, far], axis=0).reshape(count, own_count, -1)
        table = jnp.take(table, places_of[jnp.arange(count) ^ mine], axis=0).reshape(D, -1)
        return table[: D // 2], table[D // 2 :]

    def from_kernel(keep, send):
        if direct:
            return keep, send
        table = jnp.concatenate([keep, send], axis=0).reshape(count, own_count, -1)
        table = jnp.take(table, spread ^ mine, axis=0).reshape(D, -1)
        return table[: D // 2], table[D // 2 :]

    own_table = params.astype(bf16).reshape(own_count, table_width)
    own_first = jnp.concatenate(
        [
            own_table[:, : 3 * D],
            jnp.pad(own_table[:, 12 * D :], ((0, 0), (0, LANES - VECTORS))),
        ],
        axis=1,
    )
    own_rest = own_table[:, 3 * D : 12 * D]
    phases = mask_phases(count)
    outer = phases[:0:-1]
    first, rest = own_first, own_rest
    for masks in outer:
        first = jnp.concatenate(gather_phase(first, masks, count), axis=0)
        first, rest = together(first, rest)
        rest_pieces = gather_phase(rest, masks, count)
        if masks is not outer[-1]:
            rest = jnp.concatenate(rest_pieces, axis=0)
    first_near, first_far = to_kernel(*gather_phase(first, phases[0], count))
    limits = jnp.concatenate([row_lengths, row_widths])
    segments = segment_ids.reshape(blocks, LANES)

    tile = 2 * TILE
    steps = slots // tile
    across = pl.BlockSpec((D, tile), lambda at: (0, at))
    down = pl.BlockSpec((tile, D), lambda at: (at, 0))
    half_first = whole((D // 2, FIRST_WIDTH))
    xt, qt, kt, vt, key, value, vectors, pair_weights = pl.pallas_call(
        functools.partial(project_kernel, codes),
        grid=(steps,),
        in_specs=[smem(), down, half_first, half_first],
        out_specs=[across] * 4 + [down] * 2 + [whole((D, LANES)), whole((D, 3 * D))],
        out_shape=[shaped((D, slots), bf16)] * 4
        + [shaped((slots, D), bf16)] * 2
        + [shaped((D, LANES), f32), shaped((D, 3 * D), bf16)],
        scratch_shapes=[
            pltpu.VMEM((D, FIRST_WIDTH), bf16),
            pltpu.VMEM((3 * D, D), bf16),
            pltpu.VMEM((2, D, LANES), f32),
            pltpu.VMEM((8, D), f32),
        ],
        compiler_params=params_of(),
        name="project",
    )(origin, tokens, first_near, first_far)

    pair_rows = pl.BlockSpec((PAIR, slots), lambda at: (at, 0))
    pair_columns = pl.BlockSpec((slots, PAIR), lambda at: (0, at))
    sums_block = pl.BlockSpec((1, blocks, 2 * LANES), lambda at: (at, 0, 0))
    attended, logsum = pl.pallas_call(
        attend_kernel,
        grid=(PAIRS,),
        in_specs=[smem(), whole((blocks, LANES)), pair_rows, pair_columns, pair_rows],
        out_specs=[pair_rows, sums_block],
        out_shape=[shaped((D, slots), bf16), shaped((PAIRS, blocks, 2 * LANES), f32)],
        scratch_shapes=[pltpu.VMEM((blocks, WINDOW, LANES), f32)],
        compiler_params=params_of(),
        name="attend",
    )(limits, segments, qt, key, vt)

    attended, *rest_pieces = together(attended, *rest_pieces)
    rest = jnp.concatenate(rest_pieces, axis=0)
    rest_near, rest_far = to_kernel(*gather_phase(rest, phases[0], count))
    half_rest = whole((D // 2, REST_WIDTH))
    layer_output, grad_attended, grad_both, keep_rest, send_rest, feed_sums = pl.pallas_call(
        functools.partial(feed_kernel, codes),
        grid=(steps,),
        in_specs=[
            smem(), smem(), across, across, down,
            whole((D, LANES)), half_rest, half_rest,
        ],
        out_specs=[down, across, across, half_rest, half_rest, whole((D, LANES))],
        out_shape=[
            shaped((slots, D), bf16),
            shaped((D, slots), bf16),
            shaped((D, slots), f32),
            shaped((D // 2, REST_WIDTH), bf16),
            shaped((D // 2, REST_WIDTH), bf16),
            shaped((D, LANES), f32),
        ],
        scratch_shapes=[
            pltpu.VMEM((D, REST_WIDTH), bf16),
            pltpu.VMEM((D, D), bf16),
            pltpu.VMEM((FF, D), bf16),
            pltpu.VMEM((FF, D), bf16),
            pltpu.VMEM((6, D, LANES), f32),
            pltpu.VMEM((FF, LANES), f32),
            pltpu.VMEM((FF, TILE), f32),
            pltpu.VMEM((D, FF), f32),
            pltpu.VMEM((D + BLOCK, FF), f32),
            pltpu.VMEM((D, D), f32),
            pltpu.VMEM((6, D, LANES), f32),
        ]
        + [pltpu.VMEM((rows, TILE), bf16) for rows in (FF, FF, D + BLOCK, D, D, D)] * 2,
        compiler_params=params_of(),
        name="feed",
    )(origin, limits, xt, attended, cotangent, vectors, rest_near, rest_far)

    def scatter(parts, at, holds_vectors):
        if at == len(phases) - 1:
            return cut_sum(parts, 1, f32, holds_vectors)
        return cut_sum(parts, len(phases[at + 1]), bf16, holds_vectors)

    parts = scatter_phase(from_kernel(keep_rest, send_rest), phases[0], count)
    grad_attended, *pieces = together(grad_attended, *scatter(parts, 0, False))
    rest_parts = scatter_phase(pieces, phases[1], count)

    half_all = whole((D // 2, 3 * D + 2 * LANES))
    grads, keep_first, send_first = pl.pallas_call(
        functools.partial(attend_back_kernel, codes),
        grid=(PAIRS,),
        in_specs=[
            smem(), smem(), whole((blocks, LANES)), whole((D, slots)),
            pair_rows, pair_rows, pair_columns, pair_columns, pair_rows, pair_rows, sums_block,
            whole((D, LANES)),
        ],
        out_specs=[
            pl.BlockSpec((1, 3 * PAIR, slots), lambda at: (at, 0, 0)),
            half_all,
            half_all,
        ],
        out_shape=[
            shaped((PAIRS, 3 * PAIR, slots), bf16),
            shaped((D // 2, 3 * D + 2 * LANES), bf16),
            shaped((D // 2, 3 * D + 2 * LANES), bf16),
        ],
        scratch_shapes=[
            pltpu.VMEM((blocks, WINDOW, LANES), f32),
            pltpu.VMEM((PAIR, slots), f32),
            pltpu.VMEM((PAIR, slots), f32),
            pltpu.VMEM((D, 3 * PAIR), f32),
            pltpu.VMEM((D, 2 * LANES), f32),
        ],
        compiler_params=params_of(),
        name="attend_back",
    )(origin, limits, segments, xt, qt, kt, key, value, attended, grad_attended, logsum, feed_sums)

    keep_first, send_first, *rest_parts = together(keep_first, send_first, *rest_parts)
    parts = scatter_phase(from_kernel(keep_first, send_first), phases[0], count)
    pieces = scatter(parts, 0, True)
    grads, *held = together(grads, *pieces, *rest_parts)
    pieces, rest_parts = held[: len(pieces)], held[len(pieces) :]
    parts = scatter_phase(pieces, phases[1], count)
    rest_pieces = scatter(rest_parts, 1, False)
    grads, *rest_pieces = together(grads, *rest_pieces)
    input_grad = pl.pallas_call(
        input_kernel,
        grid=(steps,),
        in_specs=[
            pl.BlockSpec((PAIRS, 3 * PAIR, tile), lambda at: (0, 0, at)),
            whole((D, 3 * D)),
            across,
        ],
        out_specs=down,
        out_shape=shaped((slots, D), f32),
        compiler_params=params_of(),
        name="input_grad",
    )(grads, pair_weights, grad_both)

    input_grad, *parts = together(input_grad, *parts)
    for at in range(2, len(phases)):
        pieces = scatter(parts, at - 1, True)
        parts = scatter_phase(pieces, phases[at], count)
        rest_parts = scatter_phase(rest_pieces, phases[at], count)
        rest_pieces = scatter(rest_parts, at, False)
    (own_rest,) = rest_pieces
    own_first, share = pl.pallas_call(
        own_kernel,
        out_shape=[shaped((own_count, 3 * D), f32), shaped((own_count, LANES), f32)],
        compiler_params=params_of(),
        name="own",
    )(*parts, own_rest)
    shares = share
    for masks in outer:
        shares = jnp.concatenate(gather_phase(shares, masks, count), axis=0)
    vector_grads, norms = pl.pallas_call(
        functools.partial(settle_kernel, codes),
        in_specs=[smem()] + [whole((D // 2, LANES))] * 2,
        out_specs=[whole((VECTORS, D)), whole((8, LANES))],
        out_shape=[shaped((VECTORS, D), f32), shaped((8, LANES), f32)],
        scratch_shapes=[pltpu.VMEM((D, LANES), f32)],
        compiler_params=params_of(),
        name="settle",
    )(origin, *to_kernel(*gather_phase(shares, phases[0], count)))
    grad_norm = norms[0, 0]
    vector_grads = vector_grads.T

    own_grad = jnp.concatenate([own_first, own_rest, share[:, :VECTORS]], axis=1).reshape(-1)
    clipped = own_grad * jnp.minimum(1.0, CLIP_NORM / (grad_norm + 1e-06))
    new_momenta = MOMENTUM * momenta + clipped
    new_params = params - LEARN_RATE * (clipped + MOMENTUM * new_momenta)
    new_averages = AVERAGE_DECAY * averages + (1.0 - AVERAGE_DECAY) * new_params
    return (
        layer_output, input_grad, grad_norm, vector_grads, new_params, new_momenta, new_averages,
    )


def solution(mesh):
    placed = (P("dp", None), P("dp", None), P("dp"), P("dp"), P("dp"), P("dp"), P("dp"), P("dp"))
    return jax.shard_map(
        body,
        mesh=mesh,
        in_specs=placed,
        out_specs=(P("dp", None), P("dp", None), P(), P(), P("dp"), P("dp"), P("dp")),
        check_vma=False,
    )
```

```python
import functools

import jax
import jax.numpy as jnp
from jax import lax
from jax.experimental import pallas as pl
from jax.experimental.pallas import tpu as pltpu
from jax.sharding import PartitionSpec as P

HD = 64
ROW = 1024
EPSILON = 1e-05
CLIP_NORM = 1.0
LEARN_RATE = 20.0
MOMENTUM = 0.5
AVERAGE_DECAY = 0.5
MASKED = -1e30
GELU_IN = 0.7978845608028654
GELU_CUBE = 0.044715

D = 512
FF = 2048
PAIR = 2 * HD
PAIRS = D // PAIR
LANES = 128
WINDOW = 3 * LANES
BLOCK = 16
BLOCKS = D // BLOCK
VECTORS = 12
TILE = 256
FIRST_WIDTH = 3 * D + LANES
REST_WIDTH = D + 2 * FF
MIB = 1024 * 1024

f32 = jnp.float32
bf16 = jnp.bfloat16


def nn(left, right):
    return lax.dot_general(left, right, (((1,), (0,)), ((), ())), preferred_element_type=f32)


def nt(left, right):
    return lax.dot_general(left, right, (((1,), (1,)), ((), ())), preferred_element_type=f32)


def turned(values):
    return values.T


def place_blocks(target, pieces, codes, mine):
    place = 0
    for piece in pieces:
        width = piece.shape[1]
        for begin in range(0, piece.shape[0], BLOCK):
            to_rows = pl.ds(pl.multiple_of((mine ^ codes[place]) * BLOCK, BLOCK), BLOCK)
            target[to_rows, :width] = piece[begin : begin + BLOCK, :]
            place += 1


def spread_blocks(halves, source, codes, mine, begin, width):
    for half_at, half in enumerate(halves):
        for block_at in range(BLOCKS // 2):
            natural = mine ^ codes[half_at * (BLOCKS // 2) + block_at]
            from_rows = pl.ds(pl.multiple_of(natural * BLOCK, BLOCK), BLOCK)
            rows = slice(block_at * BLOCK, (block_at + 1) * BLOCK)
            half[rows, pl.ds(begin, width)] = source[from_rows, :].astype(bf16)


def project_kernel(
    codes, mine_ref, x_ref, near_ref, far_ref,
    xt_ref, qt_ref, kt_ref, vt_ref, k_ref, v_ref, vec_ref, pairs_ref,
    table, turned_weights, columns, rows,
):
    @pl.when(pl.program_id(0) == 0)
    def _():
        place_blocks(table, (near_ref, far_ref), codes, mine_ref[0])
        for kind in range(3):
            for half in range(2):
                at = kind * D + half * TILE
                turned_weights[at : at + TILE, :] = turned(table[:, at : at + TILE])
        for pair in range(PAIRS):
            for kind in range(3):
                at = pair * 3 * PAIR + kind * PAIR
                pairs_ref[:, at : at + PAIR] = table[
                    :, kind * D + pair * PAIR : kind * D + (pair + 1) * PAIR
                ]
        vectors = table[:, 3 * D :].astype(f32)
        vec_ref[...] = vectors
        columns[0] = jnp.broadcast_to(vectors[:, 0:1], (D, LANES))
        columns[1] = jnp.broadcast_to(vectors[:, 1:2], (D, LANES))
        rows[...] = vectors.T[:8, :]

    x = x_ref[...]
    width = x.shape[0]
    reps = width // LANES
    for half in range(2):
        xt_ref[half * 256 : half * 256 + 256, :] = turned(x[:, half * 256 : half * 256 + 256])
    bias_q = jnp.concatenate([columns[0]] * reps, axis=1)
    bias_v = jnp.concatenate([columns[1]] * reps, axis=1)
    query = nt(turned_weights[:D, :], x) + bias_q
    qt_ref[...] = (query.astype(bf16).astype(f32) * HD ** (-0.5)).astype(bf16)
    kt_ref[...] = nt(turned_weights[D : 2 * D, :], x).astype(bf16)
    vt_ref[...] = (nt(turned_weights[2 * D :, :], x) + bias_v).astype(bf16)
    k_ref[...] = nn(x, table[:, D : 2 * D]).astype(bf16)
    v_ref[...] = (nn(x, table[:, 2 * D : 3 * D]) + rows[1:2, :]).astype(bf16)


def fill_bias(bias, seg_ref, limits_ref):
    blocks = bias.shape[0]
    lane = lax.broadcasted_iota(jnp.int32, (1, LANES), 1)
    across = lax.broadcasted_iota(jnp.int32, (LANES, LANES), 1)
    down = lax.broadcasted_iota(jnp.int32, (LANES, LANES), 0)

    def codes_of(block):
        row = jnp.where(limits_ref[2] == 1, 0, block // (ROW // LANES))
        limit = jnp.where(row == 0, limits_ref[0], limits_ref[1])
        code = seg_ref[block : block + 1, :] * 2 + row
        live = lane + block * LANES - row * ROW < limit
        return code.astype(f32), jnp.where(live, code, -1).astype(f32)

    codes = [codes_of(block) for block in range(blocks)]
    for block in range(blocks):
        key_column = jnp.broadcast_to(codes[block][1], (LANES, LANES)).T
        for query in range(max(block - 2, 0), min(block + 3, blocks)):
            first = min(max(query - 1, 0), blocks - 3)
            if 0 <= block - first < 3:
                allowed = key_column == codes[query][0]
                if query == block:
                    allowed = allowed | (down == across)
                at = (block - first) * LANES
                bias[query, at : at + LANES, :] = jnp.where(allowed, 0.0, MASKED)


def two_heads(values):
    zeros = jnp.zeros((HD, values.shape[1]), values.dtype)
    left = jnp.concatenate([values[:HD], zeros], axis=0)
    right = jnp.concatenate([zeros, values[HD:]], axis=0)
    return jnp.concatenate([left, right], axis=1)


def own_heads(values):
    return jnp.concatenate([values[:HD, :LANES], values[HD:, LANES:]], axis=0)


def down_tree(values, combine):
    rows = values.shape[0]
    if rows == WINDOW:
        values = combine(
            combine(values[:LANES], values[LANES : 2 * LANES]), values[2 * LANES : 3 * LANES]
        )
        rows = LANES
    while rows > 8:
        rows //= 2
        values = combine(values[:rows], values[rows : 2 * rows])
    return values


def top_down(values):
    return jnp.max(down_tree(values, jnp.maximum), axis=0, keepdims=True)


def sum_down(values):
    return jnp.sum(down_tree(values, jnp.add), axis=0, keepdims=True)


def places(block, blocks):
    begin = min(max(block - 1, 0), blocks - 3) * LANES
    return slice(block * LANES, (block + 1) * LANES), slice(begin, begin + WINDOW)


def pipelined(amount, *stages):
    depth = len(stages)
    held = {}
    for step in range(amount + depth - 1):
        for at, stage in enumerate(stages):
            item = step - at
            if 0 <= item < amount:
                held[item] = stage(item, held.get(item))
                if at == depth - 1:
                    del held[item]


def attend_kernel(limits_ref, seg_ref, qt_ref, k_ref, vt_ref, att_ref, logsum_ref, bias):
    @pl.when(pl.program_id(0) == 0)
    def _():
        fill_bias(bias, seg_ref, limits_ref)

    blocks = bias.shape[0]

    def score(block, _):
        here, window = places(block, blocks)
        mask = bias[block]
        scores = nn(k_ref[window, :], two_heads(qt_ref[:, here]))
        return scores + jnp.concatenate([mask, mask], axis=1)

    def finish(block, scores):
        here, window = places(block, blocks)
        highest = top_down(scores)
        exponent = jnp.exp(scores - highest)
        total = sum_down(exponent)
        outputs = nn(vt_ref[:, window], exponent.astype(bf16)) * (1.0 / total)
        att_ref[:, here] = own_heads(outputs).astype(bf16)
        logsum_ref[0, block : block + 1, :] = highest + jnp.log(total)

    pipelined(blocks, score, finish)


def mean_down(values):
    return sum_down(values) * (1.0 / D)


def lane_parts(values):
    return values[:, :LANES] + values[:, LANES:]


def weight_parts(kept, acc_down, acc_up, acc_out):
    hidden, grad_up, first_low, grad_feed, grad_branch, att = kept

    def part(target, left, right, at):
        def run():
            target[:, at : at + TILE] += nt(left[...], right[at : at + TILE, :])

        return run

    parts = [part(acc_down, grad_feed, hidden, at) for at in range(0, FF, TILE)]
    parts += [part(acc_up, first_low, grad_up, at) for at in range(0, FF, TILE)]
    parts += [part(acc_out, grad_branch, att, at) for at in range(0, D, TILE)]
    return parts


def feed_kernel(codes, amount, *refs):
    mine_ref, limits_ref, xt_ref, att_ref, cot_ref, vec_ref = refs[:6]
    piece_refs = refs[6 : 6 + amount]
    layer_ref, ga_ref, both_ref, keep_ref, send_ref, sums_ref = refs[6 + amount : 12 + amount]
    table, out_turned, up_turned, down_turned, columns, up_bias, slopes = refs[
        12 + amount : 19 + amount
    ]
    acc_down, acc_up, acc_out, acc_vec, *kept = refs[19 + amount :]
    step = pl.program_id(0)
    chunk = TILE
    chunks = FF // chunk
    each = len(kept) // 2

    @pl.when(step == 0)
    def _():
        place_blocks(table, piece_refs, codes, mine_ref[0])
        for at in range(0, D, TILE):
            out_turned[at : at + TILE, :] = turned(table[:, at : at + TILE])
        for at in range(0, FF, TILE):
            up_turned[at : at + TILE, :] = turned(table[:, D + at : D + at + TILE])
            down_turned[at : at + TILE, :] = turned(table[:, D + FF + at : D + FF + at + TILE])
        for kind in range(6):
            columns[kind] = jnp.broadcast_to(vec_ref[:, kind + 2 : kind + 3], (D, LANES))
        for at in range(4):
            up_bias[pl.ds(at, D, stride=4), :] = jnp.broadcast_to(
                vec_ref[:, 8 + at : 9 + at], (D, LANES)
            )
        for buffer in (acc_down, acc_up, acc_out, acc_vec, *kept[each:]):
            buffer[...] = jnp.zeros_like(buffer)
        for buffer in (kept[2], kept[each + 2]):
            buffer[D:, :] = jnp.ones((BLOCK, TILE), bf16)

    def column(kind):
        return jnp.concatenate([columns[kind]] * 2, axis=1)

    def one_tile(tile, now, before):
        hidden, grad_up, first_keep, feed_keep, branch_keep, att_keep = now
        fill = iter(weight_parts(before, acc_down, acc_up, acc_out))

        def tick(amount=1):
            for _ in range(amount):
                next(fill)()

        here = slice(tile * TILE, (tile + 1) * TILE)
        place = lax.broadcasted_iota(jnp.int32, (1, TILE), 1) + (step * 2 + tile) * TILE
        row = jnp.where(limits_ref[2] == 1, 0, place // ROW)
        limit = jnp.where(row == 0, limits_ref[0], limits_ref[1])
        live = place - row * ROW < limit

        x = xt_ref[:, here].astype(f32)
        att = att_ref[:, here]
        att_keep[...] = att
        z_one = x + nn(table[:, :D], att) + column(0)
        tick(5)
        centred = z_one - mean_down(z_one)
        inverse_one = lax.rsqrt(mean_down(centred * centred) + EPSILON)
        normed_one = centred * inverse_one
        first = normed_one * column(2) + column(3)
        first_low = first.astype(bf16)
        first_keep[:D, :] = first_low
        partial = [first + x + column(1)]

        def widen(at, _):
            rows = slice(at * chunk, (at + 1) * chunk)
            bias = jnp.concatenate([up_bias[rows, :]] * 2, axis=1)
            return nn(up_turned[rows, :], first_low) + bias

        def bend(at, pre):
            rows = slice(at * chunk, (at + 1) * chunk)
            square = pre * pre
            tanh = jnp.tanh(pre * (GELU_IN + (GELU_IN * GELU_CUBE) * square))
            half = 0.5 + 0.5 * tanh
            value = pre * half
            slopes[rows, :] = half + value * (1.0 - tanh) * (
                GELU_IN + (3.0 * GELU_IN * GELU_CUBE) * square
            )
            low = value.astype(bf16)
            hidden[rows, :] = low
            return low

        def narrow(at, low):
            columns_at = slice(D + FF + at * chunk, D + FF + (at + 1) * chunk)
            partial[0] = partial[0] + nn(table[:, columns_at], low)

        pipelined(chunks, widen, bend, narrow)
        z_two = partial[0]
        cot = cot_ref[here, :].T.astype(f32)
        tick(8)
        centred = z_two - mean_down(z_two)
        inverse_two = lax.rsqrt(mean_down(centred * centred) + EPSILON)
        normed_two = centred * inverse_two
        gain_two = column(4)
        layer = jnp.where(live, normed_two * gain_two + column(5), 0.0).astype(bf16)
        cot = jnp.where(live, cot, 0.0)
        scaled = cot * gain_two
        scaled_mean = mean_down(scaled)
        product_mean = mean_down(scaled * normed_two)
        grad_two = inverse_two * (scaled - scaled_mean - normed_two * product_mean)
        grad_feed = grad_two.astype(bf16)
        feed_keep[...] = grad_feed
        acc_vec[1] += lane_parts(grad_feed.astype(f32))
        acc_vec[4] += lane_parts(cot * normed_two)
        acc_vec[5] += lane_parts(cot)
        partial[0] = grad_two

        def widen_back(at, _):
            return nn(down_turned[at * chunk : (at + 1) * chunk, :], grad_feed)

        def bend_back(at, grad_hidden):
            rows = slice(at * chunk, (at + 1) * chunk)
            low = (grad_hidden * slopes[rows, :]).astype(bf16)
            grad_up[rows, :] = low
            return low

        def narrow_back(at, low):
            partial[0] = partial[0] + nn(table[:, D + at * chunk : D + (at + 1) * chunk], low)

        pipelined(chunks, widen_back, bend_back, narrow_back)
        grad_first = partial[0]
        layer_ref[here, :] = layer.T
        tick(5)
        acc_vec[2] += lane_parts(grad_first * normed_one)
        acc_vec[3] += lane_parts(grad_first)
        scaled = grad_first * column(2)
        scaled_mean = mean_down(scaled)
        product_mean = mean_down(scaled * normed_one)
        grad_one = inverse_one * (scaled - scaled_mean - normed_one * product_mean)
        both_ref[:, here] = (grad_two + grad_one).astype(bf16)
        grad_branch = grad_one.astype(bf16)
        branch_keep[...] = grad_branch
        acc_vec[0] += lane_parts(grad_branch.astype(f32))
        ga_ref[:, here] = nn(out_turned[...], grad_branch).astype(bf16)

    one_tile(0, kept[:each], kept[each:])
    one_tile(1, kept[each:], kept[:each])

    @pl.when(step == pl.num_programs(0) - 1)
    def _():
        for part in weight_parts(kept[each:], acc_down, acc_up, acc_out):
            part()
        halves = (keep_ref, send_ref)
        spread_blocks(halves, acc_out, codes, mine_ref[0], 0, D)
        spread_blocks(halves, acc_up, codes, mine_ref[0], D, FF)
        spread_blocks(halves, acc_down, codes, mine_ref[0], D + FF, FF)
        up_sums = jnp.broadcast_to(acc_up[D : D + 1, :], (LANES, FF))
        for at in range(0, FF, LANES):
            up_bias[at : at + LANES, :] = up_sums[:, at : at + LANES].T
        lane = lax.broadcasted_iota(jnp.int32, (D, LANES), 1)
        vectors = jnp.zeros((D, LANES), f32)
        for kind in range(6):
            total = jnp.sum(acc_vec[kind], axis=1, keepdims=True)
            vectors = jnp.where(lane == kind + 2, total, vectors)
        for at in range(4):
            vectors = jnp.where(lane == 8 + at, up_bias[pl.ds(at, D, stride=4), :], vectors)
        sums_ref[...] = vectors


def attend_back_kernel(
    codes, mine_ref, limits_ref, seg_ref, xt_ref, qt_ref, kt_ref, k_ref, v_ref, att_ref, ga_ref,
    logsum_ref, sums_ref, grads_ref, keep_ref, send_ref, bias, acc_key, acc_value, weight_grad,
    vectors,
):
    pair = pl.program_id(0)

    @pl.when(pair == 0)
    def _():
        fill_bias(bias, seg_ref, limits_ref)

    blocks = bias.shape[0]
    acc_key[...] = jnp.zeros_like(acc_key)
    acc_value[...] = jnp.zeros_like(acc_value)

    def score(block, _):
        here, window = places(block, blocks)
        mask = bias[block]
        query = two_heads(qt_ref[:, here])
        grad = two_heads(ga_ref[:, here])
        scores = nn(k_ref[window, :], query) + jnp.concatenate([mask, mask], axis=1)
        return query, grad, scores, nn(v_ref[window, :], grad)

    def finish(block, held):
        query, grad, scores, grad_chances = held
        here, window = places(block, blocks)
        product = ga_ref[:, here].astype(f32) * att_ref[:, here].astype(f32)
        centre = jnp.concatenate([sum_down(product[:HD]), sum_down(product[HD:])], axis=1)
        chances = jnp.exp(scores - logsum_ref[0, block : block + 1, :])
        grad_scores = (chances * (grad_chances - centre)).astype(bf16)
        acc_value[:, window] += nt(grad, chances.astype(bf16))
        grad_query = own_heads(nn(kt_ref[:, window], grad_scores)) * HD ** (-0.5)
        grads_ref[0, :PAIR, here] = grad_query.astype(bf16)
        acc_key[:, window] += nt(query, grad_scores)

    pipelined(blocks, score, finish)
    grads_ref[0, PAIR : 2 * PAIR, :] = acc_key[...].astype(bf16)
    grads_ref[0, 2 * PAIR :, :] = acc_value[...].astype(bf16)
    grads = grads_ref[0]
    weight_grad[...] = nt(xt_ref[...], grads)
    halves = (keep_ref, send_ref)
    begin = pl.multiple_of(pair * (3 * PAIR), 3 * PAIR)
    spread_blocks(halves, weight_grad, codes, mine_ref[0], begin, 3 * PAIR)
    rows = pl.ds(pl.multiple_of(pair * PAIR, PAIR), PAIR)
    lane = lax.broadcasted_iota(jnp.int32, (PAIR, LANES), 1)
    query_sum = jnp.sum(grads[:PAIR].astype(f32), axis=1, keepdims=True)
    value_sum = jnp.sum(grads[2 * PAIR :].astype(f32), axis=1, keepdims=True)
    total = jnp.where(lane == 0, query_sum, jnp.where(lane == 1, value_sum, sums_ref[rows, :]))
    vectors[rows, :] = total

    @pl.when(pair == PAIRS - 1)
    def _():
        spread_blocks(halves, vectors, codes, mine_ref[0], 3 * D, LANES)


def input_kernel(grads_ref, weights_ref, both_ref, out_ref):
    width = both_ref.shape[1]

    def multiply(at, _):
        here = slice(at * TILE, (at + 1) * TILE)
        grads = jnp.concatenate([grads_ref[pair, :, here] for pair in range(PAIRS)], axis=0)
        return both_ref[:, here].astype(f32) + nn(weights_ref[...], grads)

    def turn(at, total):
        out_ref[at * TILE : (at + 1) * TILE, :] = total.T

    pipelined(width // TILE, multiply, turn)


def own_kernel(*refs):
    own_ref, share_ref = refs[-2:]
    rest_ref = refs[-3]
    total = sum(part[...].astype(f32) for part in refs[:-3])
    squares = jnp.sum(rest_ref[...] * rest_ref[...], axis=1, keepdims=True)
    for pair in range(PAIRS):
        for kind in range(3):
            at = pair * 3 * PAIR + kind * PAIR
            piece = total[:, at : at + PAIR]
            own_ref[:, kind * D + pair * PAIR : kind * D + (pair + 1) * PAIR] = piece
            squares = squares + jnp.sum(piece * piece, axis=1, keepdims=True)
    vectors = total[:, -LANES:]
    lane = lax.broadcasted_iota(jnp.int32, vectors.shape, 1)
    vectors = jnp.where(lane < VECTORS, vectors, 0.0)
    squares = squares + jnp.sum(vectors * vectors, axis=1, keepdims=True)
    share_ref[...] = jnp.where(lane == VECTORS, squares, vectors)


def settle_kernel(codes, mine_ref, near_ref, far_ref, vectors_ref, norm_ref, table):
    place_blocks(table, (near_ref, far_ref), codes, mine_ref[0])
    vectors_ref[...] = table[...].T[:VECTORS, :]
    squares = jnp.sum(table[...], axis=0, keepdims=True)[:, VECTORS : VECTORS + 1]
    norm_ref[...] = jnp.broadcast_to(jnp.sqrt(squares), (8, LANES))


def exchange(values, bit, count):
    return lax.ppermute(values, "dp", [(at, at ^ bit) for at in range(count)])


def mask_phases(count):
    bits = [1 << at for at in range(1, count.bit_length() - 1)]
    phases = [bits[at : at + 2] for at in range(0, len(bits), 2)]
    return [[0, 1]] + [
        [sum(bit for at, bit in enumerate(phase) if choice >> at & 1) for choice in range(1 << len(phase))]
        for phase in phases
    ]


def block_codes(count):
    codes = [0]
    for masks in reversed(mask_phases(count)):
        codes = [mask ^ code for mask in masks for code in codes]
    return codes


def gather_phase(block, masks, count):
    return [block] + [exchange(block, mask, count) for mask in masks[1:]]


def scatter_phase(pieces, masks, count):
    return [pieces[0]] + [
        exchange(piece, mask, count) for piece, mask in zip(pieces[1:], masks[1:], strict=True)
    ]


def cut_sum(parts, amount, dtype):
    rows = parts[0].shape[0] // amount
    return [
        sum(part[at * rows : (at + 1) * rows].astype(f32) for part in parts).astype(dtype)
        for at in range(amount)
    ]


def together(*values):
    return lax.optimization_barrier(values)


def whole(shape):
    return pl.BlockSpec(shape, lambda *at: (0,) * len(shape))


def smem():
    return pl.BlockSpec(memory_space=pltpu.SMEM)


def shaped(shape, dtype):
    return jax.ShapeDtypeStruct(shape, dtype)


def resident():
    return pl.BlockSpec(memory_space=pltpu.VMEM)


def params_of(mib):
    return pltpu.CompilerParams(vmem_limit_bytes=mib * MIB)


def body(tokens, cotangent, segment_ids, row_lengths, row_widths, params, momenta, averages):
    slots = tokens.shape[0]
    count = lax.axis_size("dp")
    mine = lax.axis_index("dp").astype(jnp.int32)
    own_count = D // count
    table_width = params.shape[0] // own_count
    blocks = slots // LANES
    direct = own_count == BLOCK
    if direct:
        codes = block_codes(count)
        origin = mine.reshape(1)
    else:
        codes = list(range(BLOCKS))
        origin = jnp.zeros((1,), jnp.int32)
        spread = jnp.array(block_codes(count), jnp.int32)
        places_of = jnp.argsort(spread)

    def to_kernel(pieces, amount):
        if direct:
            return pieces
        table = jnp.concatenate(pieces, axis=0).reshape(count, own_count, -1)
        table = jnp.take(table, places_of[jnp.arange(count) ^ mine], axis=0)
        return list(table.reshape(amount, D // amount, -1))

    def from_kernel(keep, send):
        if direct:
            return keep, send
        table = jnp.concatenate([keep, send], axis=0).reshape(count, own_count, -1)
        table = jnp.take(table, spread ^ mine, axis=0).reshape(D, -1)
        return table[: D // 2], table[D // 2 :]

    own_table = params.astype(bf16).reshape(own_count, table_width)
    own_first = jnp.concatenate(
        [
            own_table[:, : 3 * D],
            jnp.pad(own_table[:, 12 * D :], ((0, 0), (0, LANES - VECTORS))),
        ],
        axis=1,
    )
    own_rest = own_table[:, 3 * D : 12 * D]
    phases = mask_phases(count)
    outer = phases[:0:-1]
    first, rest = own_first, own_rest
    for masks in outer:
        first = jnp.concatenate(gather_phase(first, masks, count), axis=0)
        first, rest = together(first, rest)
        rest_pieces = gather_phase(rest, masks, count)
        if masks is not outer[-1]:
            rest = jnp.concatenate(rest_pieces, axis=0)
    rest_far = [exchange(rest, 1, count)]
    first_near, first_far = to_kernel(gather_phase(first, phases[0], count), 2)
    limits = jnp.concatenate([row_lengths, row_widths])
    segments = segment_ids.reshape(blocks, LANES)

    tile = 2 * TILE
    steps = slots // tile
    across = pl.BlockSpec((D, tile), lambda at: (0, at))
    down = pl.BlockSpec((tile, D), lambda at: (at, 0))
    xt, qt, kt, vt, key, value, vectors, pair_weights = pl.pallas_call(
        functools.partial(project_kernel, codes),
        grid=(steps,),
        in_specs=[smem(), down, resident(), resident()],
        out_specs=[across] * 4 + [down] * 2 + [whole((D, LANES)), whole((D, 3 * D))],
        out_shape=[shaped((D, slots), bf16)] * 4
        + [shaped((slots, D), bf16)] * 2
        + [shaped((D, LANES), f32), shaped((D, 3 * D), bf16)],
        scratch_shapes=[
            pltpu.VMEM((D, FIRST_WIDTH), bf16),
            pltpu.VMEM((3 * D, D), bf16),
            pltpu.VMEM((2, D, LANES), f32),
            pltpu.VMEM((8, D), f32),
        ],
        compiler_params=params_of(52),
        name="project",
    )(origin, tokens, first_near, first_far)

    pair_rows = pl.BlockSpec((PAIR, slots), lambda at: (at, 0))
    pair_columns = pl.BlockSpec((slots, PAIR), lambda at: (0, at))
    sums_block = pl.BlockSpec((1, blocks, 2 * LANES), lambda at: (at, 0, 0))
    attended, logsum = pl.pallas_call(
        attend_kernel,
        grid=(PAIRS,),
        in_specs=[smem(), whole((blocks, LANES)), pair_rows, pair_columns, pair_rows],
        out_specs=[pair_rows, sums_block],
        out_shape=[shaped((D, slots), bf16), shaped((PAIRS, blocks, 2 * LANES), f32)],
        scratch_shapes=[pltpu.VMEM((blocks, WINDOW, LANES), f32)],
        compiler_params=params_of(56),
        name="attend",
    )(limits, segments, qt, key, vt)

    attended, *rest_pieces = together(attended, *rest_pieces)
    rest_far += [exchange(piece, 1, count) for piece in rest_pieces[1:]]
    rest_pieces = to_kernel(rest_pieces + rest_far, 1)
    half_rest = whole((D // 2, REST_WIDTH))
    layer_output, grad_attended, grad_both, keep_rest, send_rest, feed_sums = pl.pallas_call(
        functools.partial(feed_kernel, codes, len(rest_pieces)),
        grid=(steps,),
        in_specs=[
            smem(), smem(), across, across, down,
            whole((D, LANES)),
        ]
        + [whole(piece.shape) for piece in rest_pieces],
        out_specs=[down, across, across, half_rest, half_rest, whole((D, LANES))],
        out_shape=[
            shaped((slots, D), bf16),
            shaped((D, slots), bf16),
            shaped((D, slots), bf16),
            shaped((D // 2, REST_WIDTH), bf16),
            shaped((D // 2, REST_WIDTH), bf16),
            shaped((D, LANES), f32),
        ],
        scratch_shapes=[
            pltpu.VMEM((D, REST_WIDTH), bf16),
            pltpu.VMEM((D, D), bf16),
            pltpu.VMEM((FF, D), bf16),
            pltpu.VMEM((FF, D), bf16),
            pltpu.VMEM((6, D, LANES), f32),
            pltpu.VMEM((FF, LANES), f32),
            pltpu.VMEM((FF, TILE), f32),
            pltpu.VMEM((D, FF), f32),
            pltpu.VMEM((D + BLOCK, FF), f32),
            pltpu.VMEM((D, D), f32),
            pltpu.VMEM((6, D, LANES), f32),
        ]
        + [pltpu.VMEM((rows, TILE), bf16) for rows in (FF, FF, D + BLOCK, D, D, D)] * 2,
        compiler_params=params_of(60),
        name="feed",
    )(origin, limits, xt, attended, cotangent, vectors, *rest_pieces)

    def scatter(parts, at):
        if at == len(phases) - 1:
            return cut_sum(parts, 1, f32)
        return cut_sum(parts, len(phases[at + 1]), bf16)

    parts = scatter_phase(from_kernel(keep_rest, send_rest), phases[0], count)
    grad_attended, *pieces = together(grad_attended, *scatter(parts, 0))
    rest_parts = scatter_phase(pieces, phases[1], count)

    grads, keep_first, send_first = pl.pallas_call(
        functools.partial(attend_back_kernel, codes),
        grid=(PAIRS,),
        in_specs=[
            smem(), smem(), whole((blocks, LANES)), whole((D, slots)),
            pair_rows, pair_rows, pair_columns, pair_columns, pair_rows, pair_rows, sums_block,
            whole((D, LANES)),
        ],
        out_specs=[
            pl.BlockSpec((1, 3 * PAIR, slots), lambda at: (at, 0, 0)),
            resident(),
            resident(),
        ],
        out_shape=[
            shaped((PAIRS, 3 * PAIR, slots), bf16),
            shaped((D // 2, FIRST_WIDTH), bf16),
            shaped((D // 2, FIRST_WIDTH), bf16),
        ],
        scratch_shapes=[
            pltpu.VMEM((blocks, WINDOW, LANES), f32),
            pltpu.VMEM((PAIR, slots), f32),
            pltpu.VMEM((PAIR, slots), f32),
            pltpu.VMEM((D, 3 * PAIR), f32),
            pltpu.VMEM((D, LANES), f32),
        ],
        compiler_params=params_of(54),
        name="attend_back",
    )(origin, limits, segments, xt, qt, kt, key, value, attended, grad_attended, logsum, feed_sums)

    keep_first, send_first, *rest_parts = together(keep_first, send_first, *rest_parts)
    parts = scatter_phase(from_kernel(keep_first, send_first), phases[0], count)
    pieces = scatter(parts, 0)
    grads, *held = together(grads, *pieces, *rest_parts)
    pieces, rest_parts = held[: len(pieces)], held[len(pieces) :]
    parts = scatter_phase(pieces, phases[1], count)
    rest_pieces = scatter(rest_parts, 1)
    for at in range(2, len(phases)):
        pieces = scatter(parts, at - 1)
        grads, *pieces = together(grads, *pieces)
        parts = scatter_phase(pieces, phases[at], count)
        rest_parts = scatter_phase(rest_pieces, phases[at], count)
        if at < len(phases) - 1:
            rest_pieces = scatter(rest_parts, at)
    input_grad = pl.pallas_call(
        input_kernel,
        grid=(steps,),
        in_specs=[
            pl.BlockSpec((PAIRS, 3 * PAIR, tile), lambda at: (0, 0, at)),
            whole((D, 3 * D)),
            across,
        ],
        out_specs=down,
        out_shape=shaped((slots, D), f32),
        compiler_params=params_of(20),
        name="input_grad",
    )(grads, pair_weights, grad_both)
    input_grad, *rest_parts = together(input_grad, *rest_parts)
    input_grad, *parts = together(input_grad, *parts)
    (own_rest,) = scatter(rest_parts, len(phases) - 1)
    own_first, share = pl.pallas_call(
        own_kernel,
        out_shape=[shaped((own_count, 3 * D), f32), shaped((own_count, LANES), f32)],
        compiler_params=params_of(8),
        name="own",
    )(*parts, own_rest)
    shares = share
    for masks in outer:
        shares = jnp.concatenate(gather_phase(shares, masks, count), axis=0)
    vector_grads, norms = pl.pallas_call(
        functools.partial(settle_kernel, codes),
        in_specs=[smem()] + [resident()] * 2,
        out_specs=[whole((VECTORS, D)), whole((8, LANES))],
        out_shape=[shaped((VECTORS, D), f32), shaped((8, LANES), f32)],
        scratch_shapes=[pltpu.VMEM((D, LANES), f32)],
        compiler_params=params_of(8),
        name="settle",
    )(origin, *to_kernel(gather_phase(shares, phases[0], count), 2))
    grad_norm = norms[0, 0]
    vector_grads = vector_grads.T

    own_grad = jnp.concatenate([own_first, own_rest, share[:, :VECTORS]], axis=1).reshape(-1)
    clipped = own_grad * jnp.minimum(1.0, CLIP_NORM / (grad_norm + 1e-06))
    new_momenta = MOMENTUM * momenta + clipped
    new_params = params - LEARN_RATE * (clipped + MOMENTUM * new_momenta)
    new_averages = AVERAGE_DECAY * averages + (1.0 - AVERAGE_DECAY) * new_params
    return (
        layer_output, input_grad, grad_norm, vector_grads, new_params, new_momenta, new_averages,
    )


def solution(mesh):
    placed = (P("dp", None), P("dp", None), P("dp"), P("dp"), P("dp"), P("dp"), P("dp"), P("dp"))
    return jax.shard_map(
        body,
        mesh=mesh,
        in_specs=placed,
        out_specs=(P("dp", None), P("dp", None), P(), P(), P("dp"), P("dp"), P("dp")),
        check_vma=False,
    )
```

```python
import functools

import jax
import jax.numpy as jnp
from jax import lax
from jax.experimental import pallas as pl
from jax.experimental.pallas import tpu as pltpu
from jax.sharding import PartitionSpec as P

HD = 64
ROW = 1024
EPSILON = 1e-05
CLIP_NORM = 1.0
LEARN_RATE = 20.0
MOMENTUM = 0.5
AVERAGE_DECAY = 0.5
MASKED = -1e30
GELU_IN = 0.7978845608028654
GELU_CUBE = 0.044715

D = 512
FF = 2048
PAIR = 2 * HD
PAIRS = D // PAIR
LANES = 128
WINDOW = 3 * LANES
BLOCK = 16
BLOCKS = D // BLOCK
VECTORS = 12
TILE = 256
FIRST_WIDTH = 3 * D + LANES
REST_WIDTH = D + 2 * FF
MIB = 1024 * 1024

f32 = jnp.float32
bf16 = jnp.bfloat16


def nn(left, right):
    return lax.dot_general(left, right, (((1,), (0,)), ((), ())), preferred_element_type=f32)


def nt(left, right):
    return lax.dot_general(left, right, (((1,), (1,)), ((), ())), preferred_element_type=f32)


def turned(values):
    return values.T


def place_blocks(target, pieces, codes, mine):
    place = 0
    for piece in pieces:
        width = piece.shape[1]
        for begin in range(0, piece.shape[0], BLOCK):
            to_rows = pl.ds(pl.multiple_of((mine ^ codes[place]) * BLOCK, BLOCK), BLOCK)
            target[to_rows, :width] = piece[begin : begin + BLOCK, :]
            place += 1


def spread_blocks(halves, source, codes, mine, begin, width):
    for half_at, half in enumerate(halves):
        for block_at in range(BLOCKS // 2):
            natural = mine ^ codes[half_at * (BLOCKS // 2) + block_at]
            from_rows = pl.ds(pl.multiple_of(natural * BLOCK, BLOCK), BLOCK)
            rows = slice(block_at * BLOCK, (block_at + 1) * BLOCK)
            half[rows, pl.ds(begin, width)] = source[from_rows, :].astype(bf16)


def project_kernel(
    codes, mine_ref, x_ref, near_ref, far_ref,
    xt_ref, qt_ref, kt_ref, vt_ref, k_ref, v_ref, vec_ref, pairs_ref,
    table, turned_weights, columns, rows,
):
    @pl.when(pl.program_id(0) == 0)
    def _():
        place_blocks(table, (near_ref, far_ref), codes, mine_ref[0])
        for kind in range(3):
            for half in range(2):
                at = kind * D + half * TILE
                turned_weights[at : at + TILE, :] = turned(table[:, at : at + TILE])
        for pair in range(PAIRS):
            for kind in range(3):
                at = pair * 3 * PAIR + kind * PAIR
                pairs_ref[:, at : at + PAIR] = table[
                    :, kind * D + pair * PAIR : kind * D + (pair + 1) * PAIR
                ]
        vectors = table[:, 3 * D :].astype(f32)
        vec_ref[...] = vectors
        columns[0] = jnp.broadcast_to(vectors[:, 0:1], (D, LANES))
        columns[1] = jnp.broadcast_to(vectors[:, 1:2], (D, LANES))
        rows[...] = vectors.T[:8, :]

    x = x_ref[...]
    width = x.shape[0]
    reps = width // LANES
    for half in range(2):
        xt_ref[half * 256 : half * 256 + 256, :] = turned(x[:, half * 256 : half * 256 + 256])
    bias_q = jnp.concatenate([columns[0]] * reps, axis=1)
    bias_v = jnp.concatenate([columns[1]] * reps, axis=1)
    query = nt(turned_weights[:D, :], x) + bias_q
    qt_ref[...] = (query.astype(bf16).astype(f32) * HD ** (-0.5)).astype(bf16)
    kt_ref[...] = nt(turned_weights[D : 2 * D, :], x).astype(bf16)
    vt_ref[...] = (nt(turned_weights[2 * D :, :], x) + bias_v).astype(bf16)
    k_ref[...] = nn(x, table[:, D : 2 * D]).astype(bf16)
    v_ref[...] = (nn(x, table[:, 2 * D : 3 * D]) + rows[1:2, :]).astype(bf16)


def fill_bias(bias, seg_ref, limits_ref):
    blocks = bias.shape[0]
    lane = lax.broadcasted_iota(jnp.int32, (1, LANES), 1)
    across = lax.broadcasted_iota(jnp.int32, (LANES, LANES), 1)
    down = lax.broadcasted_iota(jnp.int32, (LANES, LANES), 0)

    def codes_of(block):
        row = jnp.where(limits_ref[2] == 1, 0, block // (ROW // LANES))
        limit = jnp.where(row == 0, limits_ref[0], limits_ref[1])
        code = seg_ref[block : block + 1, :] * 2 + row
        live = lane + block * LANES - row * ROW < limit
        return code.astype(f32), jnp.where(live, code, -1).astype(f32)

    codes = [codes_of(block) for block in range(blocks)]
    for block in range(blocks):
        key_column = jnp.broadcast_to(codes[block][1], (LANES, LANES)).T
        for query in range(max(block - 2, 0), min(block + 3, blocks)):
            first = min(max(query - 1, 0), blocks - 3)
            if 0 <= block - first < 3:
                allowed = key_column == codes[query][0]
                if query == block:
                    allowed = allowed | (down == across)
                at = (block - first) * LANES
                bias[query, at : at + LANES, :] = jnp.where(allowed, 0.0, MASKED)


def two_heads(values):
    zeros = jnp.zeros((HD, values.shape[1]), values.dtype)
    left = jnp.concatenate([values[:HD], zeros], axis=0)
    right = jnp.concatenate([zeros, values[HD:]], axis=0)
    return jnp.concatenate([left, right], axis=1)


def own_heads(values):
    return jnp.concatenate([values[:HD, :LANES], values[HD:, LANES:]], axis=0)


def down_tree(values, combine):
    rows = values.shape[0]
    if rows == WINDOW:
        values = combine(
            combine(values[:LANES], values[LANES : 2 * LANES]), values[2 * LANES : 3 * LANES]
        )
        rows = LANES
    while rows > 8:
        rows //= 2
        values = combine(values[:rows], values[rows : 2 * rows])
    return values


def top_down(values):
    return jnp.max(down_tree(values, jnp.maximum), axis=0, keepdims=True)


def sum_down(values):
    return jnp.sum(down_tree(values, jnp.add), axis=0, keepdims=True)


def places(block, blocks):
    begin = min(max(block - 1, 0), blocks - 3) * LANES
    return slice(block * LANES, (block + 1) * LANES), slice(begin, begin + WINDOW)


def pipelined(amount, *stages):
    depth = len(stages)
    held = {}
    for step in range(amount + depth - 1):
        for at, stage in enumerate(stages):
            item = step - at
            if 0 <= item < amount:
                held[item] = stage(item, held.get(item))
                if at == depth - 1:
                    del held[item]


def attend_kernel(limits_ref, seg_ref, qt_ref, k_ref, vt_ref, att_ref, logsum_ref, bias):
    @pl.when(pl.program_id(0) == 0)
    def _():
        fill_bias(bias, seg_ref, limits_ref)

    blocks = bias.shape[0]

    def score(block, _):
        here, window = places(block, blocks)
        mask = bias[block]
        scores = nn(k_ref[window, :], two_heads(qt_ref[:, here]))
        return scores + jnp.concatenate([mask, mask], axis=1)

    def finish(block, scores):
        here, window = places(block, blocks)
        highest = top_down(scores)
        exponent = jnp.exp(scores - highest)
        total = sum_down(exponent)
        outputs = nn(vt_ref[:, window], exponent.astype(bf16)) * (1.0 / total)
        att_ref[:, here] = own_heads(outputs).astype(bf16)
        logsum_ref[0, block : block + 1, :] = highest + jnp.log(total)

    pipelined(blocks, score, finish)


def mean_down(values):
    return sum_down(values) * (1.0 / D)


def lane_parts(values):
    return values[:, :LANES] + values[:, LANES:]


def weight_parts(kept, acc_down, acc_up, acc_out):
    hidden, grad_up, first_low, grad_feed, grad_branch, att = kept

    def part(target, left, right, at):
        def run():
            target[:, at : at + TILE] += nt(left[...], right[at : at + TILE, :])

        return run

    parts = [part(acc_down, grad_feed, hidden, at) for at in range(0, FF, TILE)]
    parts += [part(acc_up, first_low, grad_up, at) for at in range(0, FF, TILE)]
    parts += [part(acc_out, grad_branch, att, at) for at in range(0, D, TILE)]
    return parts


def feed_kernel(codes, amount, *refs):
    mine_ref, limits_ref, xt_ref, att_ref, cot_ref, vec_ref = refs[:6]
    piece_refs = refs[6 : 6 + amount]
    layer_ref, ga_ref, both_ref, keep_ref, send_ref, sums_ref = refs[6 + amount : 12 + amount]
    table, out_turned, up_turned, down_turned, columns, up_bias, slopes = refs[
        12 + amount : 19 + amount
    ]
    acc_down, acc_up, acc_out, acc_vec, done, *kept = refs[19 + amount :]
    step = pl.program_id(0)
    chunk = TILE
    chunks = FF // chunk
    each = len(kept) // 2

    @pl.when(step == 0)
    def _():
        place_blocks(table, piece_refs, codes, mine_ref[0])
        for at in range(0, D, TILE):
            out_turned[at : at + TILE, :] = turned(table[:, at : at + TILE])
        for at in range(0, FF, TILE):
            up_turned[at : at + TILE, :] = turned(table[:, D + at : D + at + TILE])
            down_turned[at : at + TILE, :] = turned(table[:, D + FF + at : D + FF + at + TILE])
        for kind in range(6):
            columns[kind] = jnp.broadcast_to(vec_ref[:, kind + 2 : kind + 3], (D, LANES))
        for at in range(4):
            up_bias[pl.ds(at, D, stride=4), :] = jnp.broadcast_to(
                vec_ref[:, 8 + at : 9 + at], (D, LANES)
            )
        for buffer in (acc_down, acc_up, acc_out, acc_vec, *kept[each:]):
            buffer[...] = jnp.zeros_like(buffer)
        for buffer in (kept[2], kept[each + 2]):
            buffer[D:, :] = jnp.ones((BLOCK, TILE), bf16)

    def column(kind):
        return jnp.concatenate([columns[kind]] * 2, axis=1)

    def one_tile(tile, now, before):
        hidden, grad_up, first_keep, feed_keep, branch_keep, att_keep = now
        fill = iter(weight_parts(before, acc_down, acc_up, acc_out))

        def tick(amount=1):
            for _ in range(amount):
                next(fill)()

        here = slice(tile * TILE, (tile + 1) * TILE)
        place = lax.broadcasted_iota(jnp.int32, (1, TILE), 1) + (step * 2 + tile) * TILE
        row = jnp.where(limits_ref[2] == 1, 0, place // ROW)
        limit = jnp.where(row == 0, limits_ref[0], limits_ref[1])
        live = place - row * ROW < limit

        x = xt_ref[:, here].astype(f32)
        att = att_ref[:, here]
        att_keep[...] = att
        z_one = x + nn(table[:, :D], att) + column(0)
        tick(5)
        centred = z_one - mean_down(z_one)
        inverse_one = lax.rsqrt(mean_down(centred * centred) + EPSILON)
        normed_one = centred * inverse_one
        first = normed_one * column(2) + column(3)
        first_low = first.astype(bf16)
        first_keep[:D, :] = first_low
        partial = [first + x + column(1)]

        def widen(at, _):
            rows = slice(at * chunk, (at + 1) * chunk)
            bias = jnp.concatenate([up_bias[rows, :]] * 2, axis=1)
            return nn(up_turned[rows, :], first_low) + bias

        def bend(at, pre):
            rows = slice(at * chunk, (at + 1) * chunk)
            square = pre * pre
            tanh = jnp.tanh(pre * (GELU_IN + (GELU_IN * GELU_CUBE) * square))
            half = 0.5 + 0.5 * tanh
            value = pre * half
            slopes[rows, :] = half + value * (1.0 - tanh) * (
                GELU_IN + (3.0 * GELU_IN * GELU_CUBE) * square
            )
            low = value.astype(bf16)
            hidden[rows, :] = low
            return low

        def narrow(at, low):
            columns_at = slice(D + FF + at * chunk, D + FF + (at + 1) * chunk)
            partial[0] = partial[0] + nn(table[:, columns_at], low)

        pipelined(chunks, widen, bend, narrow)
        z_two = partial[0]
        cot = cot_ref[here, :].T.astype(f32)
        tick(8)
        centred = z_two - mean_down(z_two)
        inverse_two = lax.rsqrt(mean_down(centred * centred) + EPSILON)
        normed_two = centred * inverse_two
        gain_two = column(4)
        layer = jnp.where(live, normed_two * gain_two + column(5), 0.0).astype(bf16)
        cot = jnp.where(live, cot, 0.0)
        scaled = cot * gain_two
        scaled_mean = mean_down(scaled)
        product_mean = mean_down(scaled * normed_two)
        grad_two = inverse_two * (scaled - scaled_mean - normed_two * product_mean)
        grad_feed = grad_two.astype(bf16)
        feed_keep[...] = grad_feed
        acc_vec[1] += lane_parts(grad_feed.astype(f32))
        acc_vec[4] += lane_parts(cot * normed_two)
        acc_vec[5] += lane_parts(cot)
        partial[0] = grad_two

        def widen_back(at, _):
            return nn(down_turned[at * chunk : (at + 1) * chunk, :], grad_feed)

        def bend_back(at, grad_hidden):
            rows = slice(at * chunk, (at + 1) * chunk)
            low = (grad_hidden * slopes[rows, :]).astype(bf16)
            grad_up[rows, :] = low
            return low

        def narrow_back(at, low):
            partial[0] = partial[0] + nn(table[:, D + at * chunk : D + (at + 1) * chunk], low)

        pipelined(chunks, widen_back, bend_back, narrow_back)
        grad_first = partial[0]
        layer_ref[here, :] = layer.T
        tick(5)
        acc_vec[2] += lane_parts(grad_first * normed_one)
        acc_vec[3] += lane_parts(grad_first)
        scaled = grad_first * column(2)
        scaled_mean = mean_down(scaled)
        product_mean = mean_down(scaled * normed_one)
        grad_one = inverse_one * (scaled - scaled_mean - normed_one * product_mean)
        both_ref[:, here] = (grad_two + grad_one).astype(bf16)
        grad_branch = grad_one.astype(bf16)
        branch_keep[...] = grad_branch
        acc_vec[0] += lane_parts(grad_branch.astype(f32))
        ga_ref[:, here] = nn(out_turned[...], grad_branch).astype(bf16)

    one_tile(0, kept[:each], kept[each:])
    one_tile(1, kept[each:], kept[:each])

    @pl.when(step == pl.num_programs(0) - 1)
    def _():
        parts = weight_parts(kept[each:], acc_down, acc_up, acc_out)
        copies = []
        for source, begin, width, some in (
            (acc_up, D, FF, parts[8:16]),
            (acc_down, D + FF, FF, parts[:8]),
            (acc_out, 0, D, parts[16:]),
        ):
            for part in some:
                part()
            halves = (table.at[: D // 2, :], table.at[D // 2 :, :])
            spread_blocks(halves, source, codes, mine_ref[0], begin, width)
            across = slice(begin, begin + width)
            for half, target in zip(halves, (keep_ref, send_ref), strict=True):
                copies.append(
                    pltpu.make_async_copy(
                        half.at[:, across], target.at[:, across], done.at[len(copies)]
                    )
                )
                copies[-1].start()
        up_sums = jnp.broadcast_to(acc_up[D : D + 1, :], (LANES, FF))
        for at in range(0, FF, LANES):
            up_bias[at : at + LANES, :] = up_sums[:, at : at + LANES].T
        lane = lax.broadcasted_iota(jnp.int32, (D, LANES), 1)
        vectors = jnp.zeros((D, LANES), f32)
        for kind in range(6):
            total = jnp.sum(acc_vec[kind], axis=1, keepdims=True)
            vectors = jnp.where(lane == kind + 2, total, vectors)
        for at in range(4):
            vectors = jnp.where(lane == 8 + at, up_bias[pl.ds(at, D, stride=4), :], vectors)
        sums_ref[...] = vectors
        for copy in copies:
            copy.wait()


def attend_back_kernel(
    codes, mine_ref, limits_ref, seg_ref, xt_ref, qt_ref, kt_ref, k_ref, v_ref, att_ref, ga_ref,
    logsum_ref, sums_ref, grads_ref, keep_ref, send_ref, bias, acc_key, acc_value, weight_grad,
    vectors,
):
    pair = pl.program_id(0)

    @pl.when(pair == 0)
    def _():
        fill_bias(bias, seg_ref, limits_ref)

    blocks = bias.shape[0]
    acc_key[...] = jnp.zeros_like(acc_key)
    acc_value[...] = jnp.zeros_like(acc_value)

    def score(block, _):
        here, window = places(block, blocks)
        mask = bias[block]
        query = two_heads(qt_ref[:, here])
        grad = two_heads(ga_ref[:, here])
        scores = nn(k_ref[window, :], query) + jnp.concatenate([mask, mask], axis=1)
        return query, grad, scores, nn(v_ref[window, :], grad)

    def finish(block, held):
        query, grad, scores, grad_chances = held
        here, window = places(block, blocks)
        product = ga_ref[:, here].astype(f32) * att_ref[:, here].astype(f32)
        centre = jnp.concatenate([sum_down(product[:HD]), sum_down(product[HD:])], axis=1)
        chances = jnp.exp(scores - logsum_ref[0, block : block + 1, :])
        grad_scores = (chances * (grad_chances - centre)).astype(bf16)
        acc_value[:, window] += nt(grad, chances.astype(bf16))
        grad_query = own_heads(nn(kt_ref[:, window], grad_scores)) * HD ** (-0.5)
        grads_ref[0, :PAIR, here] = grad_query.astype(bf16)
        acc_key[:, window] += nt(query, grad_scores)

    pipelined(blocks, score, finish)
    grads_ref[0, PAIR : 2 * PAIR, :] = acc_key[...].astype(bf16)
    grads_ref[0, 2 * PAIR :, :] = acc_value[...].astype(bf16)
    grads = grads_ref[0]
    weight_grad[...] = nt(xt_ref[...], grads)
    halves = (keep_ref, send_ref)
    begin = pl.multiple_of(pair * (3 * PAIR), 3 * PAIR)
    spread_blocks(halves, weight_grad, codes, mine_ref[0], begin, 3 * PAIR)
    rows = pl.ds(pl.multiple_of(pair * PAIR, PAIR), PAIR)
    lane = lax.broadcasted_iota(jnp.int32, (PAIR, LANES), 1)
    query_sum = jnp.sum(grads[:PAIR].astype(f32), axis=1, keepdims=True)
    value_sum = jnp.sum(grads[2 * PAIR :].astype(f32), axis=1, keepdims=True)
    total = jnp.where(lane == 0, query_sum, jnp.where(lane == 1, value_sum, sums_ref[rows, :]))
    vectors[rows, :] = total

    @pl.when(pair == PAIRS - 1)
    def _():
        spread_blocks(halves, vectors, codes, mine_ref[0], 3 * D, LANES)


def input_kernel(grads_ref, weights_ref, both_ref, out_ref):
    width = both_ref.shape[1]

    def multiply(at, _):
        here = slice(at * TILE, (at + 1) * TILE)
        grads = jnp.concatenate([grads_ref[pair, :, here] for pair in range(PAIRS)], axis=0)
        return both_ref[:, here].astype(f32) + nn(weights_ref[...], grads)

    def turn(at, total):
        out_ref[at * TILE : (at + 1) * TILE, :] = total.T

    pipelined(width // TILE, multiply, turn)


def own_kernel(*refs):
    own_ref, share_ref = refs[-2:]
    rest_ref = refs[-3]
    total = sum(part[...].astype(f32) for part in refs[:-3])
    squares = jnp.sum(rest_ref[...] * rest_ref[...], axis=1, keepdims=True)
    for pair in range(PAIRS):
        for kind in range(3):
            at = pair * 3 * PAIR + kind * PAIR
            piece = total[:, at : at + PAIR]
            own_ref[:, kind * D + pair * PAIR : kind * D + (pair + 1) * PAIR] = piece
            squares = squares + jnp.sum(piece * piece, axis=1, keepdims=True)
    vectors = total[:, -LANES:]
    lane = lax.broadcasted_iota(jnp.int32, vectors.shape, 1)
    vectors = jnp.where(lane < VECTORS, vectors, 0.0)
    squares = squares + jnp.sum(vectors * vectors, axis=1, keepdims=True)
    share_ref[...] = jnp.where(lane == VECTORS, squares, vectors)


def settle_kernel(codes, mine_ref, near_ref, far_ref, vectors_ref, norm_ref, table):
    place_blocks(table, (near_ref, far_ref), codes, mine_ref[0])
    vectors_ref[...] = table[...].T[:VECTORS, :]
    squares = jnp.sum(table[...], axis=0, keepdims=True)[:, VECTORS : VECTORS + 1]
    norm_ref[...] = jnp.broadcast_to(jnp.sqrt(squares), (8, LANES))


def exchange(values, bit, count):
    return lax.ppermute(values, "dp", [(at, at ^ bit) for at in range(count)])


def mask_phases(count, size):
    bits = [1 << at for at in range(1, count.bit_length() - 1)]
    groups = [bits[:2]]
    for bit in bits[2:]:
        if len(groups[-1]) < size and len(groups) > 1:
            groups[-1].append(bit)
        else:
            groups.append([bit])
    return [[0, 1]] + [
        [
            sum(bit for at, bit in enumerate(group) if choice >> at & 1)
            for choice in range(1 << len(group))
        ]
        for group in groups
    ]


def block_codes(phases):
    codes = [0]
    for masks in reversed(phases):
        codes = [mask ^ code for mask in masks for code in codes]
    return codes


def gather_phase(block, masks, count):
    return [block] + [exchange(block, mask, count) for mask in masks[1:]]


def scatter_phase(pieces, masks, count):
    return [pieces[0]] + [
        exchange(piece, mask, count) for piece, mask in zip(pieces[1:], masks[1:], strict=True)
    ]


def cut_sum(parts, amount, dtype):
    rows = parts[0].shape[0] // amount
    return [
        sum(part[at * rows : (at + 1) * rows].astype(f32) for part in parts).astype(dtype)
        for at in range(amount)
    ]


def together(*values):
    return lax.optimization_barrier(values)


def whole(shape):
    return pl.BlockSpec(shape, lambda *at: (0,) * len(shape))


def smem():
    return pl.BlockSpec(memory_space=pltpu.SMEM)


def shaped(shape, dtype):
    return jax.ShapeDtypeStruct(shape, dtype)


def resident():
    return pl.BlockSpec(memory_space=pltpu.VMEM)


def params_of(mib):
    return pltpu.CompilerParams(vmem_limit_bytes=mib * MIB)


def body(tokens, cotangent, segment_ids, row_lengths, row_widths, params, momenta, averages):
    slots = tokens.shape[0]
    count = lax.axis_size("dp")
    mine = lax.axis_index("dp").astype(jnp.int32)
    own_count = D // count
    table_width = params.shape[0] // own_count
    blocks = slots // LANES
    direct = own_count == BLOCK
    phases = mask_phases(count, 2)
    slow_phases = mask_phases(count, 1)
    order = block_codes(phases)
    slow_order = block_codes(slow_phases)
    if direct:
        codes, slow_codes = order, slow_order
        origin = mine.reshape(1)
    else:
        codes = slow_codes = list(range(BLOCKS))
        origin = jnp.zeros((1,), jnp.int32)

    def to_kernel(pieces, order, amount):
        if direct:
            return pieces
        places = jnp.argsort(jnp.array(order, jnp.int32))[jnp.arange(count) ^ mine]
        table = jnp.concatenate(pieces, axis=0).reshape(count, own_count, -1)
        return list(jnp.take(table, places, axis=0).reshape(amount, D // amount, -1))

    def from_kernel(keep, send, order):
        if direct:
            return keep, send
        table = jnp.concatenate([keep, send], axis=0).reshape(count, own_count, -1)
        table = jnp.take(table, jnp.array(order, jnp.int32) ^ mine, axis=0).reshape(D, -1)
        return table[: D // 2], table[D // 2 :]

    own_table = params.astype(bf16).reshape(own_count, table_width)
    own_first = jnp.concatenate(
        [
            own_table[:, : 3 * D],
            jnp.pad(own_table[:, 12 * D :], ((0, 0), (0, LANES - VECTORS))),
        ],
        axis=1,
    )
    own_rest = own_table[:, 3 * D : 12 * D]
    outer = phases[:0:-1]
    first, rest = own_first, own_rest
    for at, masks in enumerate(slow_phases[:1:-1]):
        if at == 1:
            first = jnp.concatenate(gather_phase(first, outer[0], count), axis=0)
            _, rest = together(first, rest)
        rest = jnp.concatenate(gather_phase(rest, masks, count), axis=0)
    for masks in outer[1:]:
        first = jnp.concatenate(gather_phase(first, masks, count), axis=0)
    first, rest = together(first, rest)
    rest_pieces = gather_phase(rest, slow_phases[1], count)
    rest_far = [exchange(rest, 1, count)]
    first_near, first_far = to_kernel(gather_phase(first, phases[0], count), order, 2)
    limits = jnp.concatenate([row_lengths, row_widths])
    segments = segment_ids.reshape(blocks, LANES)

    tile = 2 * TILE
    steps = slots // tile
    across = pl.BlockSpec((D, tile), lambda at: (0, at))
    down = pl.BlockSpec((tile, D), lambda at: (at, 0))
    xt, qt, kt, vt, key, value, vectors, pair_weights = pl.pallas_call(
        functools.partial(project_kernel, codes),
        grid=(steps,),
        in_specs=[smem(), down, resident(), resident()],
        out_specs=[across] * 4 + [down] * 2 + [whole((D, LANES)), whole((D, 3 * D))],
        out_shape=[shaped((D, slots), bf16)] * 4
        + [shaped((slots, D), bf16)] * 2
        + [shaped((D, LANES), f32), shaped((D, 3 * D), bf16)],
        scratch_shapes=[
            pltpu.VMEM((D, FIRST_WIDTH), bf16),
            pltpu.VMEM((3 * D, D), bf16),
            pltpu.VMEM((2, D, LANES), f32),
            pltpu.VMEM((8, D), f32),
        ],
        compiler_params=params_of(52),
        name="project",
    )(origin, tokens, first_near, first_far)

    pair_rows = pl.BlockSpec((PAIR, slots), lambda at: (at, 0))
    pair_columns = pl.BlockSpec((slots, PAIR), lambda at: (0, at))
    sums_block = pl.BlockSpec((1, blocks, 2 * LANES), lambda at: (at, 0, 0))
    attended, logsum = pl.pallas_call(
        attend_kernel,
        grid=(PAIRS,),
        in_specs=[smem(), whole((blocks, LANES)), pair_rows, pair_columns, pair_rows],
        out_specs=[pair_rows, sums_block],
        out_shape=[shaped((D, slots), bf16), shaped((PAIRS, blocks, 2 * LANES), f32)],
        scratch_shapes=[pltpu.VMEM((blocks, WINDOW, LANES), f32)],
        compiler_params=params_of(56),
        name="attend",
    )(limits, segments, qt, key, vt)

    attended, *rest_pieces = together(attended, *rest_pieces)
    rest_far += [exchange(piece, 1, count) for piece in rest_pieces[1:]]
    rest_pieces = to_kernel(rest_pieces + rest_far, slow_order, 1)
    layer_output, grad_attended, grad_both, keep_rest, send_rest, feed_sums = pl.pallas_call(
        functools.partial(feed_kernel, slow_codes, len(rest_pieces)),
        grid=(steps,),
        in_specs=[
            smem(), smem(), across, across, down,
            whole((D, LANES)),
        ]
        + [whole(piece.shape) for piece in rest_pieces],
        out_specs=[down, across, across]
        + [pl.BlockSpec(memory_space=pl.ANY)] * 2
        + [whole((D, LANES))],
        out_shape=[
            shaped((slots, D), bf16),
            shaped((D, slots), bf16),
            shaped((D, slots), bf16),
            shaped((D // 2, REST_WIDTH), bf16),
            shaped((D // 2, REST_WIDTH), bf16),
            shaped((D, LANES), f32),
        ],
        scratch_shapes=[
            pltpu.VMEM((D, REST_WIDTH), bf16),
            pltpu.VMEM((D, D), bf16),
            pltpu.VMEM((FF, D), bf16),
            pltpu.VMEM((FF, D), bf16),
            pltpu.VMEM((6, D, LANES), f32),
            pltpu.VMEM((FF, LANES), f32),
            pltpu.VMEM((FF, TILE), f32),
            pltpu.VMEM((D, FF), f32),
            pltpu.VMEM((D + BLOCK, FF), f32),
            pltpu.VMEM((D, D), f32),
            pltpu.VMEM((6, D, LANES), f32),
            pltpu.SemaphoreType.DMA((6,)),
        ]
        + [pltpu.VMEM((rows, TILE), bf16) for rows in (FF, FF, D + BLOCK, D, D, D)] * 2,
        compiler_params=params_of(46 if direct else 60),
        name="feed",
    )(origin, limits, xt, attended, cotangent, vectors, *rest_pieces)

    def scatter(parts, way, at):
        if at == len(way) - 1:
            return cut_sum(parts, 1, f32)
        return cut_sum(parts, len(way[at + 1]), bf16)

    parts = scatter_phase(from_kernel(keep_rest, send_rest, slow_order), slow_phases[0], count)
    grad_attended, *pieces = together(grad_attended, *scatter(parts, slow_phases, 0))
    rest_parts = scatter_phase(pieces, slow_phases[1], count)

    grads, keep_first, send_first = pl.pallas_call(
        functools.partial(attend_back_kernel, codes),
        grid=(PAIRS,),
        in_specs=[
            smem(), smem(), whole((blocks, LANES)), whole((D, slots)),
            pair_rows, pair_rows, pair_columns, pair_columns, pair_rows, pair_rows, sums_block,
            whole((D, LANES)),
        ],
        out_specs=[
            pl.BlockSpec((1, 3 * PAIR, slots), lambda at: (at, 0, 0)),
            resident(),
            resident(),
        ],
        out_shape=[
            shaped((PAIRS, 3 * PAIR, slots), bf16),
            shaped((D // 2, FIRST_WIDTH), bf16),
            shaped((D // 2, FIRST_WIDTH), bf16),
        ],
        scratch_shapes=[
            pltpu.VMEM((blocks, WINDOW, LANES), f32),
            pltpu.VMEM((PAIR, slots), f32),
            pltpu.VMEM((PAIR, slots), f32),
            pltpu.VMEM((D, 3 * PAIR), f32),
            pltpu.VMEM((D, LANES), f32),
        ],
        compiler_params=params_of(31),
        name="attend_back",
    )(origin, limits, segments, xt, qt, kt, key, value, attended, grad_attended, logsum, feed_sums)

    keep_first, send_first, *rest_parts = together(keep_first, send_first, *rest_parts)
    parts = scatter_phase(from_kernel(keep_first, send_first, order), phases[0], count)
    pieces = scatter(parts, phases, 0)
    grads, *held = together(grads, *pieces, *rest_parts)
    pieces, rest_parts = held[: len(pieces)], held[len(pieces) :]
    parts = scatter_phase(pieces, phases[1], count)
    grads, *rest_pieces = together(grads, *scatter(rest_parts, slow_phases, 1))
    rest_parts = scatter_phase(rest_pieces, slow_phases[2], count)
    input_grad = pl.pallas_call(
        input_kernel,
        grid=(steps,),
        in_specs=[
            pl.BlockSpec((PAIRS, 3 * PAIR, tile), lambda at: (0, 0, at)),
            whole((D, 3 * D)),
            across,
        ],
        out_specs=down,
        out_shape=shaped((slots, D), f32),
        compiler_params=params_of(20),
        name="input_grad",
    )(grads, pair_weights, grad_both)
    input_grad, *parts = together(input_grad, *parts)
    for at in range(2, len(phases)):
        pieces = scatter(parts, phases, at - 1)
        pieces[0], *rest_parts = together(pieces[0], *rest_parts)
        parts = scatter_phase(pieces, phases[at], count)
    for at in range(3, len(slow_phases)):
        rest_pieces = scatter(rest_parts, slow_phases, at - 1)
        rest_parts = scatter_phase(rest_pieces, slow_phases[at], count)
    (own_rest,) = scatter(rest_parts, slow_phases, len(slow_phases) - 1)
    own_first, share = pl.pallas_call(
        own_kernel,
        out_shape=[shaped((own_count, 3 * D), f32), shaped((own_count, LANES), f32)],
        compiler_params=params_of(8),
        name="own",
    )(*parts, own_rest)
    shares = share
    for masks in outer:
        shares = jnp.concatenate(gather_phase(shares, masks, count), axis=0)
    vector_grads, norms = pl.pallas_call(
        functools.partial(settle_kernel, codes),
        in_specs=[smem()] + [resident()] * 2,
        out_specs=[whole((VECTORS, D)), whole((8, LANES))],
        out_shape=[shaped((VECTORS, D), f32), shaped((8, LANES), f32)],
        scratch_shapes=[pltpu.VMEM((D, LANES), f32)],
        compiler_params=params_of(8),
        name="settle",
    )(origin, *to_kernel(gather_phase(shares, phases[0], count), order, 2))
    grad_norm = norms[0, 0]
    vector_grads = vector_grads.T

    own_grad = jnp.concatenate([own_first, own_rest, share[:, :VECTORS]], axis=1).reshape(-1)
    clipped = own_grad * jnp.minimum(1.0, CLIP_NORM / (grad_norm + 1e-06))
    new_momenta = MOMENTUM * momenta + clipped
    new_params = params - LEARN_RATE * (clipped + MOMENTUM * new_momenta)
    new_averages = AVERAGE_DECAY * averages + (1.0 - AVERAGE_DECAY) * new_params
    return (
        layer_output, input_grad, grad_norm, vector_grads, new_params, new_momenta, new_averages,
    )


def solution(mesh):
    placed = (P("dp", None), P("dp", None), P("dp"), P("dp"), P("dp"), P("dp"), P("dp"), P("dp"))
    return jax.shard_map(
        body,
        mesh=mesh,
        in_specs=placed,
        out_specs=(P("dp", None), P("dp", None), P(), P(), P("dp"), P("dp"), P("dp")),
        check_vma=False,
    )
```

```python
import functools

import jax
import jax.numpy as jnp
from jax import lax
from jax.experimental import pallas as pl
from jax.experimental.pallas import tpu as pltpu
from jax.sharding import PartitionSpec as P

HD = 64
ROW = 1024
EPSILON = 1e-05
CLIP_NORM = 1.0
LEARN_RATE = 20.0
MOMENTUM = 0.5
AVERAGE_DECAY = 0.5
MASKED = -1e30
GELU_IN = 0.7978845608028654
GELU_CUBE = 0.044715

D = 512
FF = 2048
PAIR = 2 * HD
PAIRS = D // PAIR
LANES = 128
WINDOW = 3 * LANES
BLOCK = 16
BLOCKS = D // BLOCK
VECTORS = 12
TILE = 256
FIRST_WIDTH = 3 * D + LANES
REST_WIDTH = D + 2 * FF
MIB = 1024 * 1024

f32 = jnp.float32
bf16 = jnp.bfloat16


def nn(left, right):
    return lax.dot_general(left, right, (((1,), (0,)), ((), ())), preferred_element_type=f32)


def nt(left, right):
    return lax.dot_general(left, right, (((1,), (1,)), ((), ())), preferred_element_type=f32)


def turned(values):
    return values.T


def place_blocks(target, pieces, codes, mine):
    place = 0
    for piece in pieces:
        width = piece.shape[1]
        for begin in range(0, piece.shape[0], BLOCK):
            to_rows = pl.ds(pl.multiple_of((mine ^ codes[place]) * BLOCK, BLOCK), BLOCK)
            target[to_rows, :width] = piece[begin : begin + BLOCK, :]
            place += 1


def spread_blocks(halves, source, codes, mine, begin, width):
    for half_at, half in enumerate(halves):
        for block_at in range(BLOCKS // 2):
            natural = mine ^ codes[half_at * (BLOCKS // 2) + block_at]
            from_rows = pl.ds(pl.multiple_of(natural * BLOCK, BLOCK), BLOCK)
            rows = slice(block_at * BLOCK, (block_at + 1) * BLOCK)
            half[rows, pl.ds(begin, width)] = source[from_rows, :].astype(bf16)


def project_kernel(
    codes, mine_ref, x_ref, near_ref, far_ref,
    xt_ref, qt_ref, kt_ref, vt_ref, k_ref, v_ref, vec_ref, pairs_ref,
    table, turned_weights, columns, rows,
):
    @pl.when(pl.program_id(0) == 0)
    def _():
        place_blocks(table, (near_ref, far_ref), codes, mine_ref[0])
        for kind in range(3):
            for half in range(2):
                at = kind * D + half * TILE
                turned_weights[at : at + TILE, :] = turned(table[:, at : at + TILE])
        for pair in range(PAIRS):
            for kind in range(3):
                at = pair * 3 * PAIR + kind * PAIR
                pairs_ref[:, at : at + PAIR] = table[
                    :, kind * D + pair * PAIR : kind * D + (pair + 1) * PAIR
                ]
        vectors = table[:, 3 * D :].astype(f32)
        vec_ref[...] = vectors
        columns[0] = jnp.broadcast_to(vectors[:, 0:1], (D, LANES))
        columns[1] = jnp.broadcast_to(vectors[:, 1:2], (D, LANES))
        rows[...] = vectors.T[:8, :]

    x = x_ref[...]
    width = x.shape[0]
    reps = width // LANES
    for half in range(2):
        xt_ref[half * 256 : half * 256 + 256, :] = turned(x[:, half * 256 : half * 256 + 256])
    bias_q = jnp.concatenate([columns[0]] * reps, axis=1)
    bias_v = jnp.concatenate([columns[1]] * reps, axis=1)
    query = nt(turned_weights[:D, :], x) + bias_q
    qt_ref[...] = (query.astype(bf16).astype(f32) * HD ** (-0.5)).astype(bf16)
    kt_ref[...] = nt(turned_weights[D : 2 * D, :], x).astype(bf16)
    vt_ref[...] = (nt(turned_weights[2 * D :, :], x) + bias_v).astype(bf16)
    k_ref[...] = nn(x, table[:, D : 2 * D]).astype(bf16)
    v_ref[...] = (nn(x, table[:, 2 * D : 3 * D]) + rows[1:2, :]).astype(bf16)


def fill_bias(bias, seg_ref, limits_ref):
    blocks = bias.shape[0]
    lane = lax.broadcasted_iota(jnp.int32, (1, LANES), 1)
    across = lax.broadcasted_iota(jnp.int32, (LANES, LANES), 1)
    down = lax.broadcasted_iota(jnp.int32, (LANES, LANES), 0)

    def codes_of(block):
        row = jnp.where(limits_ref[2] == 1, 0, block // (ROW // LANES))
        limit = jnp.where(row == 0, limits_ref[0], limits_ref[1])
        code = seg_ref[block : block + 1, :] * 2 + row
        live = lane + block * LANES - row * ROW < limit
        return code.astype(f32), jnp.where(live, code, -1).astype(f32)

    codes = [codes_of(block) for block in range(blocks)]
    for block in range(blocks):
        key_column = jnp.broadcast_to(codes[block][1], (LANES, LANES)).T
        for query in range(max(block - 2, 0), min(block + 3, blocks)):
            first = min(max(query - 1, 0), blocks - 3)
            if 0 <= block - first < 3:
                allowed = key_column == codes[query][0]
                if query == block:
                    allowed = allowed | (down == across)
                at = (block - first) * LANES
                bias[query, at : at + LANES, :] = jnp.where(allowed, 0.0, MASKED)


def two_heads(values):
    zeros = jnp.zeros((HD, values.shape[1]), values.dtype)
    left = jnp.concatenate([values[:HD], zeros], axis=0)
    right = jnp.concatenate([zeros, values[HD:]], axis=0)
    return jnp.concatenate([left, right], axis=1)


def own_heads(values):
    return jnp.concatenate([values[:HD, :LANES], values[HD:, LANES:]], axis=0)


def down_tree(values, combine):
    rows = values.shape[0]
    if rows == WINDOW:
        values = combine(
            combine(values[:LANES], values[LANES : 2 * LANES]), values[2 * LANES : 3 * LANES]
        )
        rows = LANES
    while rows > 8:
        rows //= 2
        values = combine(values[:rows], values[rows : 2 * rows])
    return values


def top_down(values):
    return jnp.max(down_tree(values, jnp.maximum), axis=0, keepdims=True)


def sum_down(values):
    return jnp.sum(down_tree(values, jnp.add), axis=0, keepdims=True)


def places(block, blocks):
    begin = min(max(block - 1, 0), blocks - 3) * LANES
    return slice(block * LANES, (block + 1) * LANES), slice(begin, begin + WINDOW)


def pipelined(amount, *stages):
    depth = len(stages)
    held = {}
    for step in range(amount + depth - 1):
        for at, stage in enumerate(stages):
            item = step - at
            if 0 <= item < amount:
                held[item] = stage(item, held.get(item))
                if at == depth - 1:
                    del held[item]


def attend_kernel(limits_ref, seg_ref, qt_ref, k_ref, vt_ref, att_ref, logsum_ref, bias):
    @pl.when(pl.program_id(0) == 0)
    def _():
        fill_bias(bias, seg_ref, limits_ref)

    blocks = bias.shape[0]

    def score(block, _):
        here, window = places(block, blocks)
        mask = bias[block]
        scores = nn(k_ref[window, :], two_heads(qt_ref[:, here]))
        return scores + jnp.concatenate([mask, mask], axis=1)

    def finish(block, scores):
        here, window = places(block, blocks)
        highest = top_down(scores)
        exponent = jnp.exp(scores - highest)
        total = sum_down(exponent)
        outputs = nn(vt_ref[:, window], exponent.astype(bf16)) * (1.0 / total)
        att_ref[:, here] = own_heads(outputs).astype(bf16)
        logsum_ref[0, block : block + 1, :] = highest + jnp.log(total)

    pipelined(blocks, score, finish)


def mean_down(values):
    return sum_down(values) * (1.0 / D)


def lane_parts(values):
    return values[:, :LANES] + values[:, LANES:]


def weight_parts(kept, acc_down, acc_up, acc_out):
    hidden, grad_up, first_low, grad_feed, grad_branch, att = kept

    def part(target, left, right, at):
        def run():
            target[:, at : at + TILE] += nt(left[...], right[at : at + TILE, :])

        return run

    parts = [part(acc_down, grad_feed, hidden, at) for at in range(0, FF, TILE)]
    parts += [part(acc_up, first_low, grad_up, at) for at in range(0, FF, TILE)]
    parts += [part(acc_out, grad_branch, att, at) for at in range(0, D, TILE)]
    return parts


def feed_kernel(codes, amount, *refs):
    mine_ref, limits_ref, xt_ref, att_ref, cot_ref, vec_ref = refs[:6]
    piece_refs = refs[6 : 6 + amount]
    layer_ref, ga_ref, both_ref, keep_ref, send_ref, sums_ref = refs[6 + amount : 12 + amount]
    table, out_turned, up_turned, down_turned, columns, up_bias, slopes = refs[
        12 + amount : 19 + amount
    ]
    acc_down, acc_up, acc_out, acc_vec, *kept = refs[19 + amount :]
    step = pl.program_id(0)
    chunk = TILE
    chunks = FF // chunk
    each = len(kept) // 2

    @pl.when(step == 0)
    def _():
        place_blocks(table, piece_refs, codes, mine_ref[0])
        for at in range(0, D, TILE):
            out_turned[at : at + TILE, :] = turned(table[:, at : at + TILE])
        for at in range(0, FF, TILE):
            up_turned[at : at + TILE, :] = turned(table[:, D + at : D + at + TILE])
            down_turned[at : at + TILE, :] = turned(table[:, D + FF + at : D + FF + at + TILE])
        for kind in range(6):
            columns[kind] = jnp.broadcast_to(vec_ref[:, kind + 2 : kind + 3], (D, LANES))
        for at in range(4):
            up_bias[pl.ds(at, D, stride=4), :] = jnp.broadcast_to(
                vec_ref[:, 8 + at : 9 + at], (D, LANES)
            )
        for buffer in (acc_down, acc_up, acc_out, acc_vec, *kept[each:]):
            buffer[...] = jnp.zeros_like(buffer)
        for buffer in (kept[2], kept[each + 2]):
            buffer[D:, :] = jnp.ones((BLOCK, TILE), bf16)

    def column(kind):
        return jnp.concatenate([columns[kind]] * 2, axis=1)

    def one_tile(tile, now, before):
        hidden, grad_up, first_keep, feed_keep, branch_keep, att_keep = now
        fill = iter(weight_parts(before, acc_down, acc_up, acc_out))

        def tick(amount=1):
            for _ in range(amount):
                next(fill)()

        here = slice(tile * TILE, (tile + 1) * TILE)
        place = lax.broadcasted_iota(jnp.int32, (1, TILE), 1) + (step * 2 + tile) * TILE
        row = jnp.where(limits_ref[2] == 1, 0, place // ROW)
        limit = jnp.where(row == 0, limits_ref[0], limits_ref[1])
        live = place - row * ROW < limit

        x = xt_ref[:, here].astype(f32)
        att = att_ref[:, here]
        att_keep[...] = att
        z_one = x + nn(table[:, :D], att) + column(0)
        tick(5)
        centred = z_one - mean_down(z_one)
        inverse_one = lax.rsqrt(mean_down(centred * centred) + EPSILON)
        normed_one = centred * inverse_one
        first = normed_one * column(2) + column(3)
        first_low = first.astype(bf16)
        first_keep[:D, :] = first_low
        partial = [first + x + column(1)]

        def widen(at, _):
            rows = slice(at * chunk, (at + 1) * chunk)
            bias = jnp.concatenate([up_bias[rows, :]] * 2, axis=1)
            return nn(up_turned[rows, :], first_low) + bias

        def bend(at, pre):
            rows = slice(at * chunk, (at + 1) * chunk)
            square = pre * pre
            tanh = jnp.tanh(pre * (GELU_IN + (GELU_IN * GELU_CUBE) * square))
            half = 0.5 + 0.5 * tanh
            value = pre * half
            slopes[rows, :] = half + value * (1.0 - tanh) * (
                GELU_IN + (3.0 * GELU_IN * GELU_CUBE) * square
            )
            low = value.astype(bf16)
            hidden[rows, :] = low
            return low

        def narrow(at, low):
            columns_at = slice(D + FF + at * chunk, D + FF + (at + 1) * chunk)
            partial[0] = partial[0] + nn(table[:, columns_at], low)

        pipelined(chunks, widen, bend, narrow)
        z_two = partial[0]
        cot = cot_ref[here, :].T.astype(f32)
        tick(8)
        centred = z_two - mean_down(z_two)
        inverse_two = lax.rsqrt(mean_down(centred * centred) + EPSILON)
        normed_two = centred * inverse_two
        gain_two = column(4)
        layer = jnp.where(live, normed_two * gain_two + column(5), 0.0).astype(bf16)
        cot = jnp.where(live, cot, 0.0)
        scaled = cot * gain_two
        scaled_mean = mean_down(scaled)
        product_mean = mean_down(scaled * normed_two)
        grad_two = inverse_two * (scaled - scaled_mean - normed_two * product_mean)
        grad_feed = grad_two.astype(bf16)
        feed_keep[...] = grad_feed
        acc_vec[1] += lane_parts(grad_feed.astype(f32))
        acc_vec[4] += lane_parts(cot * normed_two)
        acc_vec[5] += lane_parts(cot)
        partial[0] = grad_two

        def widen_back(at, _):
            return nn(down_turned[at * chunk : (at + 1) * chunk, :], grad_feed)

        def bend_back(at, grad_hidden):
            rows = slice(at * chunk, (at + 1) * chunk)
            low = (grad_hidden * slopes[rows, :]).astype(bf16)
            grad_up[rows, :] = low
            return low

        def narrow_back(at, low):
            partial[0] = partial[0] + nn(table[:, D + at * chunk : D + (at + 1) * chunk], low)

        pipelined(chunks, widen_back, bend_back, narrow_back)
        grad_first = partial[0]
        layer_ref[here, :] = layer.T
        tick(5)
        acc_vec[2] += lane_parts(grad_first * normed_one)
        acc_vec[3] += lane_parts(grad_first)
        scaled = grad_first * column(2)
        scaled_mean = mean_down(scaled)
        product_mean = mean_down(scaled * normed_one)
        grad_one = inverse_one * (scaled - scaled_mean - normed_one * product_mean)
        both_ref[:, here] = (grad_two + grad_one).astype(bf16)
        grad_branch = grad_one.astype(bf16)
        branch_keep[...] = grad_branch
        acc_vec[0] += lane_parts(grad_branch.astype(f32))
        ga_ref[:, here] = nn(out_turned[...], grad_branch).astype(bf16)

    one_tile(0, kept[:each], kept[each:])
    one_tile(1, kept[each:], kept[:each])

    @pl.when(step == pl.num_programs(0) - 1)
    def _():
        parts = weight_parts(kept[each:], acc_down, acc_up, acc_out)
        for source, begin, width, some in (
            (acc_up, D, FF, parts[8:16]),
            (acc_down, D + FF, FF, parts[:8]),
            (acc_out, 0, D, parts[16:]),
        ):
            for part in some:
                part()
            spread_blocks((keep_ref, send_ref), source, codes, mine_ref[0], begin, width)
        up_sums = jnp.broadcast_to(acc_up[D : D + 1, :], (LANES, FF))
        for at in range(0, FF, LANES):
            up_bias[at : at + LANES, :] = up_sums[:, at : at + LANES].T
        lane = lax.broadcasted_iota(jnp.int32, (D, LANES), 1)
        vectors = jnp.zeros((D, LANES), f32)
        for kind in range(6):
            total = jnp.sum(acc_vec[kind], axis=1, keepdims=True)
            vectors = jnp.where(lane == kind + 2, total, vectors)
        for at in range(4):
            vectors = jnp.where(lane == 8 + at, up_bias[pl.ds(at, D, stride=4), :], vectors)
        sums_ref[...] = vectors


def attend_back_kernel(
    codes, mine_ref, limits_ref, seg_ref, xt_ref, qt_ref, kt_ref, k_ref, v_ref, att_ref, ga_ref,
    logsum_ref, sums_ref, grads_ref, keep_ref, send_ref, bias, acc_key, acc_value, weight_grad,
    vectors,
):
    pair = pl.program_id(0)

    @pl.when(pair == 0)
    def _():
        fill_bias(bias, seg_ref, limits_ref)

    blocks = bias.shape[0]
    acc_key[...] = jnp.zeros_like(acc_key)
    acc_value[...] = jnp.zeros_like(acc_value)

    def score(block, _):
        here, window = places(block, blocks)
        mask = bias[block]
        query = two_heads(qt_ref[:, here])
        grad = two_heads(ga_ref[:, here])
        scores = nn(k_ref[window, :], query) + jnp.concatenate([mask, mask], axis=1)
        return query, grad, scores, nn(v_ref[window, :], grad)

    def finish(block, held):
        query, grad, scores, grad_chances = held
        here, window = places(block, blocks)
        product = ga_ref[:, here].astype(f32) * att_ref[:, here].astype(f32)
        centre = jnp.concatenate([sum_down(product[:HD]), sum_down(product[HD:])], axis=1)
        chances = jnp.exp(scores - logsum_ref[0, block : block + 1, :])
        grad_scores = (chances * (grad_chances - centre)).astype(bf16)
        acc_value[:, window] += nt(grad, chances.astype(bf16))
        grad_query = own_heads(nn(kt_ref[:, window], grad_scores)) * HD ** (-0.5)
        grads_ref[0, :PAIR, here] = grad_query.astype(bf16)
        acc_key[:, window] += nt(query, grad_scores)

    pipelined(blocks, score, finish)
    grads_ref[0, PAIR : 2 * PAIR, :] = acc_key[...].astype(bf16)
    grads_ref[0, 2 * PAIR :, :] = acc_value[...].astype(bf16)
    grads = grads_ref[0]
    weight_grad[...] = nt(xt_ref[...], grads)
    halves = (keep_ref, send_ref)
    begin = pl.multiple_of(pair * (3 * PAIR), 3 * PAIR)
    spread_blocks(halves, weight_grad, codes, mine_ref[0], begin, 3 * PAIR)
    rows = pl.ds(pl.multiple_of(pair * PAIR, PAIR), PAIR)
    lane = lax.broadcasted_iota(jnp.int32, (PAIR, LANES), 1)
    query_sum = jnp.sum(grads[:PAIR].astype(f32), axis=1, keepdims=True)
    value_sum = jnp.sum(grads[2 * PAIR :].astype(f32), axis=1, keepdims=True)
    total = jnp.where(lane == 0, query_sum, jnp.where(lane == 1, value_sum, sums_ref[rows, :]))
    vectors[rows, :] = total

    @pl.when(pair == PAIRS - 1)
    def _():
        spread_blocks(halves, vectors, codes, mine_ref[0], 3 * D, LANES)


def input_kernel(grads_ref, weights_ref, both_ref, out_ref):
    width = both_ref.shape[1]

    def multiply(at, _):
        here = slice(at * TILE, (at + 1) * TILE)
        grads = jnp.concatenate([grads_ref[pair, :, here] for pair in range(PAIRS)], axis=0)
        return both_ref[:, here].astype(f32) + nn(weights_ref[...], grads)

    def turn(at, total):
        out_ref[at * TILE : (at + 1) * TILE, :] = total.T

    pipelined(width // TILE, multiply, turn)


def own_kernel(*refs):
    own_ref, share_ref = refs[-2:]
    rest_ref = refs[-3]
    total = sum(part[...].astype(f32) for part in refs[:-3])
    squares = jnp.sum(rest_ref[...] * rest_ref[...], axis=1, keepdims=True)
    for pair in range(PAIRS):
        for kind in range(3):
            at = pair * 3 * PAIR + kind * PAIR
            piece = total[:, at : at + PAIR]
            own_ref[:, kind * D + pair * PAIR : kind * D + (pair + 1) * PAIR] = piece
            squares = squares + jnp.sum(piece * piece, axis=1, keepdims=True)
    vectors = total[:, -LANES:]
    lane = lax.broadcasted_iota(jnp.int32, vectors.shape, 1)
    vectors = jnp.where(lane < VECTORS, vectors, 0.0)
    squares = squares + jnp.sum(vectors * vectors, axis=1, keepdims=True)
    share_ref[...] = jnp.where(lane == VECTORS, squares, vectors)


def settle_kernel(
    codes, mine_ref, near_ref, far_ref, grad_ref, params_ref, momenta_ref, averages_ref,
    vectors_ref, norm_ref, new_params_ref, new_momenta_ref, new_averages_ref, table,
):
    place_blocks(table, (near_ref, far_ref), codes, mine_ref[0])
    vectors_ref[...] = table[...].T[:VECTORS, :]
    squares = jnp.sum(table[...], axis=0, keepdims=True)[:, VECTORS : VECTORS + 1]
    norm = jnp.sqrt(squares)
    norm_ref[0] = norm[0, 0]
    factor = jnp.minimum(1.0, CLIP_NORM / (norm + 1e-06))[0, 0]
    clipped = grad_ref[...] * factor
    momenta = MOMENTUM * momenta_ref[...] + clipped
    params = params_ref[...] - LEARN_RATE * (clipped + MOMENTUM * momenta)
    new_momenta_ref[...] = momenta
    new_params_ref[...] = params
    new_averages_ref[...] = AVERAGE_DECAY * averages_ref[...] + (1.0 - AVERAGE_DECAY) * params


def exchange(values, bit, count):
    return lax.ppermute(values, "dp", [(at, at ^ bit) for at in range(count)])


def mask_phases(count, size):
    bits = [1 << at for at in range(1, count.bit_length() - 1)]
    groups = [bits[:2]]
    for bit in bits[2:]:
        if len(groups[-1]) < size and len(groups) > 1:
            groups[-1].append(bit)
        else:
            groups.append([bit])
    return [[0, 1]] + [
        [
            sum(bit for at, bit in enumerate(group) if choice >> at & 1)
            for choice in range(1 << len(group))
        ]
        for group in groups
    ]


def block_codes(phases):
    codes = [0]
    for masks in reversed(phases):
        codes = [mask ^ code for mask in masks for code in codes]
    return codes


def gather_phase(block, masks, count):
    return [block] + [exchange(block, mask, count) for mask in masks[1:]]


def scatter_phase(pieces, masks, count):
    return [pieces[0]] + [
        exchange(piece, mask, count) for piece, mask in zip(pieces[1:], masks[1:], strict=True)
    ]


def cut_sum(parts, amount, dtype):
    rows = parts[0].shape[0] // amount
    return [
        sum(part[at * rows : (at + 1) * rows].astype(f32) for part in parts).astype(dtype)
        for at in range(amount)
    ]


def together(*values):
    return lax.optimization_barrier(values)


def whole(shape):
    return pl.BlockSpec(shape, lambda *at: (0,) * len(shape))


def smem():
    return pl.BlockSpec(memory_space=pltpu.SMEM)


def shaped(shape, dtype):
    return jax.ShapeDtypeStruct(shape, dtype)


def resident():
    return pl.BlockSpec(memory_space=pltpu.VMEM)


def params_of(mib):
    return pltpu.CompilerParams(vmem_limit_bytes=mib * MIB)


def body(tokens, cotangent, segment_ids, row_lengths, row_widths, params, momenta, averages):
    slots = tokens.shape[0]
    count = lax.axis_size("dp")
    mine = lax.axis_index("dp").astype(jnp.int32)
    own_count = D // count
    table_width = params.shape[0] // own_count
    blocks = slots // LANES
    direct = own_count == BLOCK
    phases = mask_phases(count, 2)
    slow_phases = mask_phases(count, 1)
    order = block_codes(phases)
    slow_order = block_codes(slow_phases)
    if direct:
        codes, slow_codes = order, slow_order
        origin = mine.reshape(1)
    else:
        codes = slow_codes = list(range(BLOCKS))
        origin = jnp.zeros((1,), jnp.int32)

    def to_kernel(pieces, order, amount):
        if direct:
            return pieces
        places = jnp.argsort(jnp.array(order, jnp.int32))[jnp.arange(count) ^ mine]
        table = jnp.concatenate(pieces, axis=0).reshape(count, own_count, -1)
        return list(jnp.take(table, places, axis=0).reshape(amount, D // amount, -1))

    def from_kernel(keep, send, order):
        if direct:
            return keep, send
        table = jnp.concatenate([keep, send], axis=0).reshape(count, own_count, -1)
        table = jnp.take(table, jnp.array(order, jnp.int32) ^ mine, axis=0).reshape(D, -1)
        return table[: D // 2], table[D // 2 :]

    own_table = params.astype(bf16).reshape(own_count, table_width)
    own_first = jnp.concatenate(
        [
            own_table[:, : 3 * D],
            jnp.pad(own_table[:, 12 * D :], ((0, 0), (0, LANES - VECTORS))),
        ],
        axis=1,
    )
    own_rest = own_table[:, 3 * D : 12 * D]
    outer = phases[:0:-1]
    first, rest = own_first, own_rest
    for at, masks in enumerate(slow_phases[:1:-1]):
        if at == 1:
            first = jnp.concatenate(gather_phase(first, outer[0], count), axis=0)
            _, rest = together(first, rest)
        rest = jnp.concatenate(gather_phase(rest, masks, count), axis=0)
    for masks in outer[1:]:
        first = jnp.concatenate(gather_phase(first, masks, count), axis=0)
    first, rest = together(first, rest)
    rest_pieces = gather_phase(rest, slow_phases[1], count)
    rest_far = [exchange(rest, 1, count)]
    first_near, first_far = to_kernel(gather_phase(first, phases[0], count), order, 2)
    limits = jnp.concatenate([row_lengths, row_widths])
    segments = segment_ids.reshape(blocks, LANES)

    tile = 2 * TILE
    steps = slots // tile
    across = pl.BlockSpec((D, tile), lambda at: (0, at))
    down = pl.BlockSpec((tile, D), lambda at: (at, 0))
    xt, qt, kt, vt, key, value, vectors, pair_weights = pl.pallas_call(
        functools.partial(project_kernel, codes),
        grid=(steps,),
        in_specs=[smem(), down, resident(), resident()],
        out_specs=[across] * 4 + [down] * 2 + [whole((D, LANES)), whole((D, 3 * D))],
        out_shape=[shaped((D, slots), bf16)] * 4
        + [shaped((slots, D), bf16)] * 2
        + [shaped((D, LANES), f32), shaped((D, 3 * D), bf16)],
        scratch_shapes=[
            pltpu.VMEM((D, FIRST_WIDTH), bf16),
            pltpu.VMEM((3 * D, D), bf16),
            pltpu.VMEM((2, D, LANES), f32),
            pltpu.VMEM((8, D), f32),
        ],
        compiler_params=params_of(52),
        name="project",
    )(origin, tokens, first_near, first_far)

    pair_rows = pl.BlockSpec((PAIR, slots), lambda at: (at, 0))
    pair_columns = pl.BlockSpec((slots, PAIR), lambda at: (0, at))
    sums_block = pl.BlockSpec((1, blocks, 2 * LANES), lambda at: (at, 0, 0))
    attended, logsum = pl.pallas_call(
        attend_kernel,
        grid=(PAIRS,),
        in_specs=[smem(), whole((blocks, LANES)), pair_rows, pair_columns, pair_rows],
        out_specs=[pair_rows, sums_block],
        out_shape=[shaped((D, slots), bf16), shaped((PAIRS, blocks, 2 * LANES), f32)],
        scratch_shapes=[pltpu.VMEM((blocks, WINDOW, LANES), f32)],
        compiler_params=params_of(56),
        name="attend",
    )(limits, segments, qt, key, vt)

    attended, *rest_pieces = together(attended, *rest_pieces)
    rest_far += [exchange(piece, 1, count) for piece in rest_pieces[1:]]
    rest_pieces = to_kernel(rest_pieces + rest_far, slow_order, 1)
    layer_output, grad_attended, grad_both, keep_rest, send_rest, feed_sums = pl.pallas_call(
        functools.partial(feed_kernel, slow_codes, len(rest_pieces)),
        grid=(steps,),
        in_specs=[
            smem(), smem(), across, across, down,
            whole((D, LANES)),
        ]
        + [whole(piece.shape) for piece in rest_pieces],
        out_specs=[down, across, across]
        + [resident()] * 2
        + [whole((D, LANES))],
        out_shape=[
            shaped((slots, D), bf16),
            shaped((D, slots), bf16),
            shaped((D, slots), bf16),
            pltpu.VMEM((D // 2, REST_WIDTH), bf16),
            pltpu.VMEM((D // 2, REST_WIDTH), bf16),
            shaped((D, LANES), f32),
        ],
        scratch_shapes=[
            pltpu.VMEM((D, REST_WIDTH), bf16),
            pltpu.VMEM((D, D), bf16),
            pltpu.VMEM((FF, D), bf16),
            pltpu.VMEM((FF, D), bf16),
            pltpu.VMEM((6, D, LANES), f32),
            pltpu.VMEM((FF, LANES), f32),
            pltpu.VMEM((FF, TILE), f32),
            pltpu.VMEM((D, FF), f32),
            pltpu.VMEM((D + BLOCK, FF), f32),
            pltpu.VMEM((D, D), f32),
            pltpu.VMEM((6, D, LANES), f32),
        ]
        + [pltpu.VMEM((rows, TILE), bf16) for rows in (FF, FF, D + BLOCK, D, D, D)] * 2,
        compiler_params=params_of(50 if direct else 54),
        name="feed",
    )(origin, limits, xt, attended, cotangent, vectors, *rest_pieces)

    def scatter(parts, way, at):
        if at == len(way) - 1:
            return cut_sum(parts, 1, f32)
        return cut_sum(parts, len(way[at + 1]), bf16)

    parts = scatter_phase(from_kernel(keep_rest, send_rest, slow_order), slow_phases[0], count)
    grad_attended, *pieces = together(grad_attended, *scatter(parts, slow_phases, 0))
    rest_parts = scatter_phase(pieces, slow_phases[1], count)

    grads, keep_first, send_first = pl.pallas_call(
        functools.partial(attend_back_kernel, codes),
        grid=(PAIRS,),
        in_specs=[
            smem(), smem(), whole((blocks, LANES)), whole((D, slots)),
            pair_rows, pair_rows, pair_columns, pair_columns, pair_rows, pair_rows, sums_block,
            whole((D, LANES)),
        ],
        out_specs=[
            pl.BlockSpec((1, 3 * PAIR, slots), lambda at: (at, 0, 0)),
            resident(),
            resident(),
        ],
        out_shape=[
            shaped((PAIRS, 3 * PAIR, slots), bf16),
            shaped((D // 2, FIRST_WIDTH), bf16),
            shaped((D // 2, FIRST_WIDTH), bf16),
        ],
        scratch_shapes=[
            pltpu.VMEM((blocks, WINDOW, LANES), f32),
            pltpu.VMEM((PAIR, slots), f32),
            pltpu.VMEM((PAIR, slots), f32),
            pltpu.VMEM((D, 3 * PAIR), f32),
            pltpu.VMEM((D, LANES), f32),
        ],
        compiler_params=params_of(31),
        name="attend_back",
    )(origin, limits, segments, xt, qt, kt, key, value, attended, grad_attended, logsum, feed_sums)

    keep_first, send_first, *rest_parts = together(keep_first, send_first, *rest_parts)
    parts = scatter_phase(from_kernel(keep_first, send_first, order), phases[0], count)
    pieces = scatter(parts, phases, 0)
    grads, *held = together(grads, *pieces, *rest_parts)
    pieces, rest_parts = held[: len(pieces)], held[len(pieces) :]
    parts = scatter_phase(pieces, phases[1], count)
    grads, *rest_pieces = together(grads, *scatter(rest_parts, slow_phases, 1))
    rest_parts = scatter_phase(rest_pieces, slow_phases[2], count)
    input_grad = pl.pallas_call(
        input_kernel,
        grid=(steps,),
        in_specs=[
            pl.BlockSpec((PAIRS, 3 * PAIR, tile), lambda at: (0, 0, at)),
            whole((D, 3 * D)),
            across,
        ],
        out_specs=down,
        out_shape=shaped((slots, D), f32),
        compiler_params=params_of(20),
        name="input_grad",
    )(grads, pair_weights, grad_both)
    input_grad, *parts = together(input_grad, *parts)
    for at in range(2, len(phases)):
        pieces = scatter(parts, phases, at - 1)
        pieces[0], *rest_parts = together(pieces[0], *rest_parts)
        parts = scatter_phase(pieces, phases[at], count)
    for at in range(3, len(slow_phases)):
        rest_pieces = scatter(rest_parts, slow_phases, at - 1)
        rest_parts = scatter_phase(rest_pieces, slow_phases[at], count)
    (own_rest,) = scatter(rest_parts, slow_phases, len(slow_phases) - 1)
    own_first, share = pl.pallas_call(
        own_kernel,
        out_shape=[shaped((own_count, 3 * D), f32), shaped((own_count, LANES), f32)],
        compiler_params=params_of(8),
        name="own",
    )(*parts, own_rest)
    shares = share
    for masks in outer:
        shares = jnp.concatenate(gather_phase(shares, masks, count), axis=0)
    own_grad = jnp.concatenate([own_first, own_rest, share[:, :VECTORS]], axis=1).reshape(-1)
    flat = shaped(params.shape, f32)
    vector_grads, norms, new_params, new_momenta, new_averages = pl.pallas_call(
        functools.partial(settle_kernel, codes),
        in_specs=[smem()] + [resident()] * 6,
        out_specs=[whole((VECTORS, D)), smem()] + [resident()] * 3,
        out_shape=[shaped((VECTORS, D), f32), shaped((1,), f32)] + [flat] * 3,
        scratch_shapes=[pltpu.VMEM((D, LANES), f32)],
        compiler_params=params_of(16),
        name="settle",
    )(
        origin,
        *to_kernel(gather_phase(shares, phases[0], count), order, 2),
        own_grad,
        params,
        momenta,
        averages,
    )
    grad_norm = norms.reshape(())
    vector_grads = vector_grads.T
    return (
        layer_output, input_grad, grad_norm, vector_grads, new_params, new_momenta, new_averages,
    )


def solution(mesh):
    placed = (P("dp", None), P("dp", None), P("dp"), P("dp"), P("dp"), P("dp"), P("dp"), P("dp"))
    return jax.shard_map(
        body,
        mesh=mesh,
        in_specs=placed,
        out_specs=(P("dp", None), P("dp", None), P(), P(), P("dp"), P("dp"), P("dp")),
        check_vma=False,
    )
```

```python
import functools

import jax
import jax.numpy as jnp
from jax import lax
from jax.experimental import pallas as pl
from jax.experimental.pallas import tpu as pltpu
from jax.sharding import PartitionSpec as P

HD = 64
ROW = 1024
EPSILON = 1e-05
CLIP_NORM = 1.0
LEARN_RATE = 20.0
MOMENTUM = 0.5
AVERAGE_DECAY = 0.5
MASKED = -1e30
GELU_IN = 0.7978845608028654
GELU_CUBE = 0.044715

D = 512
FF = 2048
PAIR = 2 * HD
PAIRS = D // PAIR
LANES = 128
WINDOW = 3 * LANES
BLOCK = 16
BLOCKS = D // BLOCK
VECTORS = 12
TILE = 256
FIRST_WIDTH = 3 * D + LANES
REST_WIDTH = D + 2 * FF
MIB = 1024 * 1024

f32 = jnp.float32
bf16 = jnp.bfloat16


def nn(left, right):
    return lax.dot_general(left, right, (((1,), (0,)), ((), ())), preferred_element_type=f32)


def nt(left, right):
    return lax.dot_general(left, right, (((1,), (1,)), ((), ())), preferred_element_type=f32)


def turned(values):
    return values.T


def place_blocks(target, pieces, codes, mine):
    place = 0
    for piece in pieces:
        width = piece.shape[1]
        for begin in range(0, piece.shape[0], BLOCK):
            to_rows = pl.ds(pl.multiple_of((mine ^ codes[place]) * BLOCK, BLOCK), BLOCK)
            target[to_rows, :width] = piece[begin : begin + BLOCK, :]
            place += 1


def spread_blocks(halves, source, codes, mine, begin, width):
    for half_at, half in enumerate(halves):
        for block_at in range(BLOCKS // 2):
            natural = mine ^ codes[half_at * (BLOCKS // 2) + block_at]
            from_rows = pl.ds(pl.multiple_of(natural * BLOCK, BLOCK), BLOCK)
            rows = slice(block_at * BLOCK, (block_at + 1) * BLOCK)
            half[rows, pl.ds(begin, width)] = source[from_rows, :].astype(bf16)


def project_kernel(
    codes, mine_ref, x_ref, near_ref, far_ref,
    xt_ref, qt_ref, kt_ref, vt_ref, k_ref, v_ref, vec_ref, pairs_ref,
    table, turned_weights, columns, rows,
):
    @pl.when(pl.program_id(0) == 0)
    def _():
        place_blocks(table, (near_ref, far_ref), codes, mine_ref[0])
        for kind in range(3):
            for half in range(2):
                at = kind * D + half * TILE
                turned_weights[at : at + TILE, :] = turned(table[:, at : at + TILE])
        for pair in range(PAIRS):
            for kind in range(3):
                at = pair * 3 * PAIR + kind * PAIR
                pairs_ref[:, at : at + PAIR] = table[
                    :, kind * D + pair * PAIR : kind * D + (pair + 1) * PAIR
                ]
        vectors = table[:, 3 * D :].astype(f32)
        vec_ref[...] = vectors
        columns[0] = jnp.broadcast_to(vectors[:, 0:1], (D, LANES))
        columns[1] = jnp.broadcast_to(vectors[:, 1:2], (D, LANES))
        rows[...] = vectors.T[:8, :]

    x = x_ref[...]
    width = x.shape[0]
    reps = width // LANES
    for half in range(2):
        xt_ref[half * 256 : half * 256 + 256, :] = turned(x[:, half * 256 : half * 256 + 256])
    bias_q = jnp.concatenate([columns[0]] * reps, axis=1)
    bias_v = jnp.concatenate([columns[1]] * reps, axis=1)
    query = nt(turned_weights[:D, :], x) + bias_q
    qt_ref[...] = (query.astype(bf16).astype(f32) * HD ** (-0.5)).astype(bf16)
    kt_ref[...] = nt(turned_weights[D : 2 * D, :], x).astype(bf16)
    vt_ref[...] = (nt(turned_weights[2 * D :, :], x) + bias_v).astype(bf16)
    k_ref[...] = nn(x, table[:, D : 2 * D]).astype(bf16)
    v_ref[...] = (nn(x, table[:, 2 * D : 3 * D]) + rows[1:2, :]).astype(bf16)


def fill_bias(bias, seg_ref, limits_ref, widths_ref):
    blocks = bias.shape[0]
    lane = lax.broadcasted_iota(jnp.int32, (1, LANES), 1)
    across = lax.broadcasted_iota(jnp.int32, (LANES, LANES), 1)
    down = lax.broadcasted_iota(jnp.int32, (LANES, LANES), 0)

    def codes_of(block):
        row = jnp.where(widths_ref[0] == 1, 0, block // (ROW // LANES))
        limit = jnp.where(row == 0, limits_ref[0], limits_ref[1])
        code = seg_ref[block : block + 1, :] * 2 + row
        live = lane + block * LANES - row * ROW < limit
        return code.astype(f32), jnp.where(live, code, -1).astype(f32)

    codes = [codes_of(block) for block in range(blocks)]
    for block in range(blocks):
        key_column = jnp.broadcast_to(codes[block][1], (LANES, LANES)).T
        for query in range(max(block - 2, 0), min(block + 3, blocks)):
            first = min(max(query - 1, 0), blocks - 3)
            if 0 <= block - first < 3:
                allowed = key_column == codes[query][0]
                if query == block:
                    allowed = allowed | (down == across)
                at = (block - first) * LANES
                bias[query, at : at + LANES, :] = jnp.where(allowed, 0.0, MASKED)


def two_heads(values):
    zeros = jnp.zeros((HD, values.shape[1]), values.dtype)
    left = jnp.concatenate([values[:HD], zeros], axis=0)
    right = jnp.concatenate([zeros, values[HD:]], axis=0)
    return jnp.concatenate([left, right], axis=1)


def own_heads(values):
    return jnp.concatenate([values[:HD, :LANES], values[HD:, LANES:]], axis=0)


def down_tree(values, combine):
    rows = values.shape[0]
    if rows == WINDOW:
        values = combine(
            combine(values[:LANES], values[LANES : 2 * LANES]), values[2 * LANES : 3 * LANES]
        )
        rows = LANES
    while rows > 8:
        rows //= 2
        values = combine(values[:rows], values[rows : 2 * rows])
    return values


def top_down(values):
    return jnp.max(down_tree(values, jnp.maximum), axis=0, keepdims=True)


def sum_down(values):
    return jnp.sum(down_tree(values, jnp.add), axis=0, keepdims=True)


def places(block, blocks):
    begin = min(max(block - 1, 0), blocks - 3) * LANES
    return slice(block * LANES, (block + 1) * LANES), slice(begin, begin + WINDOW)


def pipelined(amount, *stages):
    depth = len(stages)
    held = {}
    for step in range(amount + depth - 1):
        for at, stage in enumerate(stages):
            item = step - at
            if 0 <= item < amount:
                held[item] = stage(item, held.get(item))
                if at == depth - 1:
                    del held[item]


def attend_kernel(
    limits_ref, widths_ref, seg_ref, qt_ref, k_ref, vt_ref, att_ref, logsum_ref, bias
):
    @pl.when(pl.program_id(0) == 0)
    def _():
        fill_bias(bias, seg_ref, limits_ref, widths_ref)

    blocks = bias.shape[0]

    def score(block, _):
        here, window = places(block, blocks)
        mask = bias[block]
        scores = nn(k_ref[window, :], two_heads(qt_ref[:, here]))
        return scores + jnp.concatenate([mask, mask], axis=1)

    def finish(block, scores):
        here, window = places(block, blocks)
        highest = top_down(scores)
        exponent = jnp.exp(scores - highest)
        total = sum_down(exponent)
        outputs = nn(vt_ref[:, window], exponent.astype(bf16)) * (1.0 / total)
        att_ref[:, here] = own_heads(outputs).astype(bf16)
        logsum_ref[0, block : block + 1, :] = highest + jnp.log(total)

    pipelined(blocks, score, finish)


def mean_down(values):
    return sum_down(values) * (1.0 / D)


def lane_parts(values):
    return values[:, :LANES] + values[:, LANES:]


def weight_parts(kept, acc_down, acc_up, acc_out):
    hidden, grad_up, first_low, grad_feed, grad_branch, att = kept

    def part(target, left, right, at):
        def run():
            target[:, at : at + TILE] += nt(left[...], right[at : at + TILE, :])

        return run

    parts = [part(acc_down, grad_feed, hidden, at) for at in range(0, FF, TILE)]
    parts += [part(acc_up, first_low, grad_up, at) for at in range(0, FF, TILE)]
    parts += [part(acc_out, grad_branch, att, at) for at in range(0, D, TILE)]
    return parts


def feed_kernel(codes, amount, *refs):
    mine_ref, limits_ref, widths_ref, xt_ref, att_ref, cot_ref, vec_ref = refs[:7]
    piece_refs = refs[7 : 7 + amount]
    layer_ref, ga_ref, both_ref, keep_ref, send_ref, sums_ref = refs[7 + amount : 13 + amount]
    table, out_turned, up_turned, down_turned, columns, up_bias, slopes = refs[
        13 + amount : 20 + amount
    ]
    acc_down, acc_up, acc_out, acc_vec, *kept = refs[20 + amount :]
    step = pl.program_id(0)
    chunk = TILE
    chunks = FF // chunk
    each = len(kept) // 2

    @pl.when(step == 0)
    def _():
        place_blocks(table, piece_refs, codes, mine_ref[0])
        for at in range(0, D, TILE):
            out_turned[at : at + TILE, :] = turned(table[:, at : at + TILE])
        for at in range(0, FF, TILE):
            up_turned[at : at + TILE, :] = turned(table[:, D + at : D + at + TILE])
            down_turned[at : at + TILE, :] = turned(table[:, D + FF + at : D + FF + at + TILE])
        for kind in range(6):
            columns[kind] = jnp.broadcast_to(vec_ref[:, kind + 2 : kind + 3], (D, LANES))
        for at in range(4):
            up_bias[pl.ds(at, D, stride=4), :] = jnp.broadcast_to(
                vec_ref[:, 8 + at : 9 + at], (D, LANES)
            )
        for buffer in (acc_down, acc_up, acc_out, acc_vec, *kept[each:]):
            buffer[...] = jnp.zeros_like(buffer)
        for buffer in (kept[2], kept[each + 2]):
            buffer[D:, :] = jnp.ones((BLOCK, TILE), bf16)

    def column(kind):
        return jnp.concatenate([columns[kind]] * 2, axis=1)

    def one_tile(tile, now, before):
        hidden, grad_up, first_keep, feed_keep, branch_keep, att_keep = now
        fill = iter(weight_parts(before, acc_down, acc_up, acc_out))

        def tick(amount=1):
            for _ in range(amount):
                next(fill)()

        here = slice(tile * TILE, (tile + 1) * TILE)
        place = lax.broadcasted_iota(jnp.int32, (1, TILE), 1) + (step * 2 + tile) * TILE
        row = jnp.where(widths_ref[0] == 1, 0, place // ROW)
        limit = jnp.where(row == 0, limits_ref[0], limits_ref[1])
        live = place - row * ROW < limit

        x = xt_ref[:, here].astype(f32)
        att = att_ref[:, here]
        att_keep[...] = att
        z_one = x + nn(table[:, :D], att) + column(0)
        tick(5)
        centred = z_one - mean_down(z_one)
        inverse_one = lax.rsqrt(mean_down(centred * centred) + EPSILON)
        normed_one = centred * inverse_one
        first = normed_one * column(2) + column(3)
        first_low = first.astype(bf16)
        first_keep[:D, :] = first_low
        partial = [first + x + column(1)]

        def widen(at, _):
            rows = slice(at * chunk, (at + 1) * chunk)
            bias = jnp.concatenate([up_bias[rows, :]] * 2, axis=1)
            return nn(up_turned[rows, :], first_low) + bias

        def bend(at, pre):
            rows = slice(at * chunk, (at + 1) * chunk)
            square = pre * pre
            tanh = jnp.tanh(pre * (GELU_IN + (GELU_IN * GELU_CUBE) * square))
            half = 0.5 + 0.5 * tanh
            value = pre * half
            slopes[rows, :] = half + value * (1.0 - tanh) * (
                GELU_IN + (3.0 * GELU_IN * GELU_CUBE) * square
            )
            low = value.astype(bf16)
            hidden[rows, :] = low
            return low

        def narrow(at, low):
            columns_at = slice(D + FF + at * chunk, D + FF + (at + 1) * chunk)
            partial[0] = partial[0] + nn(table[:, columns_at], low)

        pipelined(chunks, widen, bend, narrow)
        z_two = partial[0]
        cot = cot_ref[here, :].T.astype(f32)
        tick(8)
        centred = z_two - mean_down(z_two)
        inverse_two = lax.rsqrt(mean_down(centred * centred) + EPSILON)
        normed_two = centred * inverse_two
        gain_two = column(4)
        layer = jnp.where(live, normed_two * gain_two + column(5), 0.0).astype(bf16)
        cot = jnp.where(live, cot, 0.0)
        scaled = cot * gain_two
        scaled_mean = mean_down(scaled)
        product_mean = mean_down(scaled * normed_two)
        grad_two = inverse_two * (scaled - scaled_mean - normed_two * product_mean)
        grad_feed = grad_two.astype(bf16)
        feed_keep[...] = grad_feed
        acc_vec[1] += lane_parts(grad_feed.astype(f32))
        acc_vec[4] += lane_parts(cot * normed_two)
        acc_vec[5] += lane_parts(cot)
        partial[0] = grad_two

        def widen_back(at, _):
            return nn(down_turned[at * chunk : (at + 1) * chunk, :], grad_feed)

        def bend_back(at, grad_hidden):
            rows = slice(at * chunk, (at + 1) * chunk)
            low = (grad_hidden * slopes[rows, :]).astype(bf16)
            grad_up[rows, :] = low
            return low

        def narrow_back(at, low):
            partial[0] = partial[0] + nn(table[:, D + at * chunk : D + (at + 1) * chunk], low)

        pipelined(chunks, widen_back, bend_back, narrow_back)
        grad_first = partial[0]
        layer_ref[here, :] = layer.T
        tick(5)
        acc_vec[2] += lane_parts(grad_first * normed_one)
        acc_vec[3] += lane_parts(grad_first)
        scaled = grad_first * column(2)
        scaled_mean = mean_down(scaled)
        product_mean = mean_down(scaled * normed_one)
        grad_one = inverse_one * (scaled - scaled_mean - normed_one * product_mean)
        both_ref[:, here] = (grad_two + grad_one).astype(bf16)
        grad_branch = grad_one.astype(bf16)
        branch_keep[...] = grad_branch
        acc_vec[0] += lane_parts(grad_branch.astype(f32))
        ga_ref[:, here] = nn(out_turned[...], grad_branch).astype(bf16)

    one_tile(0, kept[:each], kept[each:])
    one_tile(1, kept[each:], kept[:each])

    @pl.when(step == pl.num_programs(0) - 1)
    def _():
        parts = weight_parts(kept[each:], acc_down, acc_up, acc_out)
        for source, begin, width, some in (
            (acc_up, D, FF, parts[8:16]),
            (acc_down, D + FF, FF, parts[:8]),
            (acc_out, 0, D, parts[16:]),
        ):
            for part in some:
                part()
            spread_blocks((keep_ref, send_ref), source, codes, mine_ref[0], begin, width)
        up_sums = jnp.broadcast_to(acc_up[D : D + 1, :], (LANES, FF))
        for at in range(0, FF, LANES):
            up_bias[at : at + LANES, :] = up_sums[:, at : at + LANES].T
        lane = lax.broadcasted_iota(jnp.int32, (D, LANES), 1)
        vectors = jnp.zeros((D, LANES), f32)
        for kind in range(6):
            total = jnp.sum(acc_vec[kind], axis=1, keepdims=True)
            vectors = jnp.where(lane == kind + 2, total, vectors)
        for at in range(4):
            vectors = jnp.where(lane == 8 + at, up_bias[pl.ds(at, D, stride=4), :], vectors)
        sums_ref[...] = vectors


def attend_back_kernel(
    codes, mine_ref, limits_ref, widths_ref, seg_ref, xt_ref, qt_ref, kt_ref, k_ref, v_ref, att_ref, ga_ref,
    logsum_ref, sums_ref, grads_ref, keep_ref, send_ref, bias, acc_key, acc_value, weight_grad,
    vectors,
):
    pair = pl.program_id(0)

    @pl.when(pair == 0)
    def _():
        fill_bias(bias, seg_ref, limits_ref, widths_ref)

    blocks = bias.shape[0]
    acc_key[...] = jnp.zeros_like(acc_key)
    acc_value[...] = jnp.zeros_like(acc_value)

    def score(block, _):
        here, window = places(block, blocks)
        mask = bias[block]
        query = two_heads(qt_ref[:, here])
        grad = two_heads(ga_ref[:, here])
        scores = nn(k_ref[window, :], query) + jnp.concatenate([mask, mask], axis=1)
        return query, grad, scores, nn(v_ref[window, :], grad)

    def finish(block, held):
        query, grad, scores, grad_chances = held
        here, window = places(block, blocks)
        product = ga_ref[:, here].astype(f32) * att_ref[:, here].astype(f32)
        centre = jnp.concatenate([sum_down(product[:HD]), sum_down(product[HD:])], axis=1)
        chances = jnp.exp(scores - logsum_ref[0, block : block + 1, :])
        grad_scores = (chances * (grad_chances - centre)).astype(bf16)
        acc_value[:, window] += nt(grad, chances.astype(bf16))
        grad_query = own_heads(nn(kt_ref[:, window], grad_scores)) * HD ** (-0.5)
        grads_ref[0, :PAIR, here] = grad_query.astype(bf16)
        acc_key[:, window] += nt(query, grad_scores)

    pipelined(blocks, score, finish)
    grads_ref[0, PAIR : 2 * PAIR, :] = acc_key[...].astype(bf16)
    grads_ref[0, 2 * PAIR :, :] = acc_value[...].astype(bf16)
    grads = grads_ref[0]
    weight_grad[...] = nt(xt_ref[...], grads)
    halves = (keep_ref, send_ref)
    begin = pl.multiple_of(pair * (3 * PAIR), 3 * PAIR)
    spread_blocks(halves, weight_grad, codes, mine_ref[0], begin, 3 * PAIR)
    rows = pl.ds(pl.multiple_of(pair * PAIR, PAIR), PAIR)
    lane = lax.broadcasted_iota(jnp.int32, (PAIR, LANES), 1)
    query_sum = jnp.sum(grads[:PAIR].astype(f32), axis=1, keepdims=True)
    value_sum = jnp.sum(grads[2 * PAIR :].astype(f32), axis=1, keepdims=True)
    total = jnp.where(lane == 0, query_sum, jnp.where(lane == 1, value_sum, sums_ref[rows, :]))
    vectors[rows, :] = total

    @pl.when(pair == PAIRS - 1)
    def _():
        spread_blocks(halves, vectors, codes, mine_ref[0], 3 * D, LANES)


def input_kernel(grads_ref, weights_ref, both_ref, out_ref):
    width = both_ref.shape[1]

    def multiply(at, _):
        here = slice(at * TILE, (at + 1) * TILE)
        grads = jnp.concatenate([grads_ref[pair, :, here] for pair in range(PAIRS)], axis=0)
        return both_ref[:, here].astype(f32) + nn(weights_ref[...], grads)

    def turn(at, total):
        out_ref[at * TILE : (at + 1) * TILE, :] = total.T

    pipelined(width // TILE, multiply, turn)


def own_kernel(*refs):
    own_ref, share_ref = refs[-2:]
    rest_ref = refs[-3]
    total = sum(part[...].astype(f32) for part in refs[:-3])
    squares = jnp.sum(rest_ref[...] * rest_ref[...], axis=1, keepdims=True)
    for pair in range(PAIRS):
        for kind in range(3):
            at = pair * 3 * PAIR + kind * PAIR
            piece = total[:, at : at + PAIR]
            own_ref[:, kind * D + pair * PAIR : kind * D + (pair + 1) * PAIR] = piece
            squares = squares + jnp.sum(piece * piece, axis=1, keepdims=True)
    vectors = total[:, -LANES:]
    lane = lax.broadcasted_iota(jnp.int32, vectors.shape, 1)
    vectors = jnp.where(lane < VECTORS, vectors, 0.0)
    squares = squares + jnp.sum(vectors * vectors, axis=1, keepdims=True)
    share_ref[...] = jnp.where(lane == VECTORS, squares, vectors)


def settle_kernel(
    codes, mine_ref, near_ref, far_ref, grad_ref, params_ref, momenta_ref, averages_ref,
    vectors_ref, norm_ref, new_params_ref, new_momenta_ref, new_averages_ref, table,
):
    place_blocks(table, (near_ref, far_ref), codes, mine_ref[0])
    vectors_ref[...] = table[...].T[:VECTORS, :]
    squares = jnp.sum(table[...], axis=0, keepdims=True)[:, VECTORS : VECTORS + 1]
    norm = jnp.sqrt(squares)
    norm_ref[0] = norm[0, 0]
    factor = jnp.minimum(1.0, CLIP_NORM / (norm + 1e-06))[0, 0]
    clipped = grad_ref[...] * factor
    momenta = MOMENTUM * momenta_ref[...] + clipped
    params = params_ref[...] - LEARN_RATE * (clipped + MOMENTUM * momenta)
    new_momenta_ref[...] = momenta
    new_params_ref[...] = params
    new_averages_ref[...] = AVERAGE_DECAY * averages_ref[...] + (1.0 - AVERAGE_DECAY) * params


def exchange(values, bit, count):
    return lax.ppermute(values, "dp", [(at, at ^ bit) for at in range(count)])


def mask_phases(count, size):
    bits = [1 << at for at in range(1, count.bit_length() - 1)]
    groups = [bits[:2]]
    for bit in bits[2:]:
        if len(groups[-1]) < size and len(groups) > 1:
            groups[-1].append(bit)
        else:
            groups.append([bit])
    return [[0, 1]] + [
        [
            sum(bit for at, bit in enumerate(group) if choice >> at & 1)
            for choice in range(1 << len(group))
        ]
        for group in groups
    ]


def block_codes(phases):
    codes = [0]
    for masks in reversed(phases):
        codes = [mask ^ code for mask in masks for code in codes]
    return codes


def gather_phase(block, masks, count):
    return [block] + [exchange(block, mask, count) for mask in masks[1:]]


def scatter_phase(pieces, masks, count):
    return [pieces[0]] + [
        exchange(piece, mask, count) for piece, mask in zip(pieces[1:], masks[1:], strict=True)
    ]


def cut_sum(parts, amount, dtype):
    rows = parts[0].shape[0] // amount
    return [
        sum(part[at * rows : (at + 1) * rows].astype(f32) for part in parts).astype(dtype)
        for at in range(amount)
    ]


def together(*values):
    return lax.optimization_barrier(values)


def whole(shape):
    return pl.BlockSpec(shape, lambda *at: (0,) * len(shape))


def smem():
    return pl.BlockSpec(memory_space=pltpu.SMEM)


def shaped(shape, dtype):
    return jax.ShapeDtypeStruct(shape, dtype)


def resident():
    return pl.BlockSpec(memory_space=pltpu.VMEM)


def params_of(mib):
    return pltpu.CompilerParams(vmem_limit_bytes=mib * MIB)


def body(tokens, cotangent, segment_ids, row_lengths, row_widths, params, momenta, averages):
    slots = tokens.shape[0]
    count = lax.axis_size("dp")
    mine = lax.axis_index("dp").astype(jnp.int32)
    own_count = D // count
    table_width = params.shape[0] // own_count
    blocks = slots // LANES
    direct = own_count == BLOCK
    phases = mask_phases(count, 2)
    slow_phases = mask_phases(count, 1)
    order = block_codes(phases)
    slow_order = block_codes(slow_phases)
    if direct:
        codes, slow_codes = order, slow_order
        origin = mine.reshape(1)
    else:
        codes = slow_codes = list(range(BLOCKS))
        origin = jnp.zeros((1,), jnp.int32)

    def to_kernel(pieces, order, amount):
        if direct:
            return pieces
        places = jnp.argsort(jnp.array(order, jnp.int32))[jnp.arange(count) ^ mine]
        table = jnp.concatenate(pieces, axis=0).reshape(count, own_count, -1)
        return list(jnp.take(table, places, axis=0).reshape(amount, D // amount, -1))

    def from_kernel(keep, send, order):
        if direct:
            return keep, send
        table = jnp.concatenate([keep, send], axis=0).reshape(count, own_count, -1)
        table = jnp.take(table, jnp.array(order, jnp.int32) ^ mine, axis=0).reshape(D, -1)
        return table[: D // 2], table[D // 2 :]

    own_table = params.astype(bf16).reshape(own_count, table_width)
    own_first = jnp.concatenate(
        [
            own_table[:, : 3 * D],
            jnp.pad(own_table[:, 12 * D :], ((0, 0), (0, LANES - VECTORS))),
        ],
        axis=1,
    )
    own_rest = own_table[:, 3 * D : 12 * D]
    outer = phases[:0:-1]
    first, rest = own_first, own_rest
    for at, masks in enumerate(slow_phases[:1:-1]):
        if at == 1:
            first = jnp.concatenate(gather_phase(first, outer[0], count), axis=0)
            _, rest = together(first, rest)
        rest = jnp.concatenate(gather_phase(rest, masks, count), axis=0)
    for masks in outer[1:]:
        first = jnp.concatenate(gather_phase(first, masks, count), axis=0)
    first, rest = together(first, rest)
    rest_pieces = gather_phase(rest, slow_phases[1], count)
    rest_far = [exchange(rest, 1, count)]
    first_near, first_far = to_kernel(gather_phase(first, phases[0], count), order, 2)
    segments = segment_ids.reshape(blocks, LANES)

    tile = 2 * TILE
    steps = slots // tile
    across = pl.BlockSpec((D, tile), lambda at: (0, at))
    down = pl.BlockSpec((tile, D), lambda at: (at, 0))
    xt, qt, kt, vt, key, value, vectors, pair_weights = pl.pallas_call(
        functools.partial(project_kernel, codes),
        grid=(steps,),
        in_specs=[smem(), down, resident(), resident()],
        out_specs=[across] * 4 + [down] * 2 + [whole((D, LANES)), whole((D, 3 * D))],
        out_shape=[shaped((D, slots), bf16)] * 4
        + [shaped((slots, D), bf16)] * 2
        + [shaped((D, LANES), f32), shaped((D, 3 * D), bf16)],
        scratch_shapes=[
            pltpu.VMEM((D, FIRST_WIDTH), bf16),
            pltpu.VMEM((3 * D, D), bf16),
            pltpu.VMEM((2, D, LANES), f32),
            pltpu.VMEM((8, D), f32),
        ],
        compiler_params=params_of(52),
        name="project",
    )(origin, tokens, first_near, first_far)

    pair_rows = pl.BlockSpec((PAIR, slots), lambda at: (at, 0))
    pair_columns = pl.BlockSpec((slots, PAIR), lambda at: (0, at))
    sums_block = pl.BlockSpec((1, blocks, 2 * LANES), lambda at: (at, 0, 0))
    attended, logsum = pl.pallas_call(
        attend_kernel,
        grid=(PAIRS,),
        in_specs=[smem(), smem(), whole((blocks, LANES)), pair_rows, pair_columns, pair_rows],
        out_specs=[pair_rows, sums_block],
        out_shape=[shaped((D, slots), bf16), shaped((PAIRS, blocks, 2 * LANES), f32)],
        scratch_shapes=[pltpu.VMEM((blocks, WINDOW, LANES), f32)],
        compiler_params=params_of(56),
        name="attend",
    )(row_lengths, row_widths, segments, qt, key, vt)

    attended, *rest_pieces = together(attended, *rest_pieces)
    rest_far += [exchange(piece, 1, count) for piece in rest_pieces[1:]]
    rest_pieces = to_kernel(rest_pieces + rest_far, slow_order, 1)
    layer_output, grad_attended, grad_both, keep_rest, send_rest, feed_sums = pl.pallas_call(
        functools.partial(feed_kernel, slow_codes, len(rest_pieces)),
        grid=(steps,),
        in_specs=[
            smem(), smem(), smem(), across, across, down,
            whole((D, LANES)),
        ]
        + [whole(piece.shape) for piece in rest_pieces],
        out_specs=[down, across, across]
        + [resident()] * 2
        + [whole((D, LANES))],
        out_shape=[
            shaped((slots, D), bf16),
            shaped((D, slots), bf16),
            shaped((D, slots), bf16),
            pltpu.VMEM((D // 2, REST_WIDTH), bf16),
            pltpu.VMEM((D // 2, REST_WIDTH), bf16),
            shaped((D, LANES), f32),
        ],
        scratch_shapes=[
            pltpu.VMEM((D, REST_WIDTH), bf16),
            pltpu.VMEM((D, D), bf16),
            pltpu.VMEM((FF, D), bf16),
            pltpu.VMEM((FF, D), bf16),
            pltpu.VMEM((6, D, LANES), f32),
            pltpu.VMEM((FF, LANES), f32),
            pltpu.VMEM((FF, TILE), f32),
            pltpu.VMEM((D, FF), f32),
            pltpu.VMEM((D + BLOCK, FF), f32),
            pltpu.VMEM((D, D), f32),
            pltpu.VMEM((6, D, LANES), f32),
        ]
        + [pltpu.VMEM((rows, TILE), bf16) for rows in (FF, FF, D + BLOCK, D, D, D)] * 2,
        compiler_params=params_of(50 if direct else 54),
        name="feed",
    )(origin, row_lengths, row_widths, xt, attended, cotangent, vectors, *rest_pieces)

    def scatter(parts, way, at):
        if at == len(way) - 1:
            return cut_sum(parts, 1, f32)
        return cut_sum(parts, len(way[at + 1]), bf16)

    parts = scatter_phase(from_kernel(keep_rest, send_rest, slow_order), slow_phases[0], count)
    grad_attended, *pieces = together(grad_attended, *scatter(parts, slow_phases, 0))
    rest_parts = scatter_phase(pieces, slow_phases[1], count)

    grads, keep_first, send_first = pl.pallas_call(
        functools.partial(attend_back_kernel, codes),
        grid=(PAIRS,),
        in_specs=[
            smem(), smem(), smem(), whole((blocks, LANES)), whole((D, slots)),
            pair_rows, pair_rows, pair_columns, pair_columns, pair_rows, pair_rows, sums_block,
            whole((D, LANES)),
        ],
        out_specs=[
            pl.BlockSpec((1, 3 * PAIR, slots), lambda at: (at, 0, 0)),
            resident(),
            resident(),
        ],
        out_shape=[
            pltpu.VMEM((PAIRS, 3 * PAIR, slots), bf16),
            pltpu.VMEM((D // 2, FIRST_WIDTH), bf16),
            pltpu.VMEM((D // 2, FIRST_WIDTH), bf16),
        ],
        scratch_shapes=[
            pltpu.VMEM((blocks, WINDOW, LANES), f32),
            pltpu.VMEM((PAIR, slots), f32),
            pltpu.VMEM((PAIR, slots), f32),
            pltpu.VMEM((D, 3 * PAIR), f32),
            pltpu.VMEM((D, LANES), f32),
        ],
        compiler_params=params_of(46),
        name="attend_back",
    )(origin, row_lengths, row_widths, segments, xt, qt, kt, key, value, attended, grad_attended, logsum, feed_sums)

    keep_first, send_first, *rest_parts = together(keep_first, send_first, *rest_parts)
    parts = scatter_phase(from_kernel(keep_first, send_first, order), phases[0], count)
    pieces = scatter(parts, phases, 0)
    grads, *held = together(grads, *pieces, *rest_parts)
    pieces, rest_parts = held[: len(pieces)], held[len(pieces) :]
    parts = scatter_phase(pieces, phases[1], count)
    grads, *rest_pieces = together(grads, *scatter(rest_parts, slow_phases, 1))
    rest_parts = scatter_phase(rest_pieces, slow_phases[2], count)
    input_grad = pl.pallas_call(
        input_kernel,
        grid=(steps,),
        in_specs=[
            pl.BlockSpec((PAIRS, 3 * PAIR, tile), lambda at: (0, 0, at)),
            whole((D, 3 * D)),
            across,
        ],
        out_specs=down,
        out_shape=shaped((slots, D), f32),
        compiler_params=params_of(20),
        name="input_grad",
    )(grads, pair_weights, grad_both)
    input_grad, *parts = together(input_grad, *parts)
    for at in range(2, len(phases)):
        pieces = scatter(parts, phases, at - 1)
        pieces[0], *rest_parts = together(pieces[0], *rest_parts)
        parts = scatter_phase(pieces, phases[at], count)
    for at in range(3, len(slow_phases)):
        rest_pieces = scatter(rest_parts, slow_phases, at - 1)
        rest_parts = scatter_phase(rest_pieces, slow_phases[at], count)
    (own_rest,) = scatter(rest_parts, slow_phases, len(slow_phases) - 1)
    own_first, share = pl.pallas_call(
        own_kernel,
        out_shape=[shaped((own_count, 3 * D), f32), shaped((own_count, LANES), f32)],
        compiler_params=params_of(8),
        name="own",
    )(*parts, own_rest)
    shares = share
    for masks in outer:
        shares = jnp.concatenate(gather_phase(shares, masks, count), axis=0)
    own_grad = jnp.concatenate([own_first, own_rest, share[:, :VECTORS]], axis=1).reshape(-1)
    flat = shaped(params.shape, f32)
    vector_grads, norms, new_params, new_momenta, new_averages = pl.pallas_call(
        functools.partial(settle_kernel, codes),
        in_specs=[smem()] + [resident()] * 6,
        out_specs=[whole((VECTORS, D)), smem()] + [resident()] * 3,
        out_shape=[shaped((VECTORS, D), f32), shaped((1,), f32)] + [flat] * 3,
        scratch_shapes=[pltpu.VMEM((D, LANES), f32)],
        compiler_params=params_of(16),
        name="settle",
    )(
        origin,
        *to_kernel(gather_phase(shares, phases[0], count), order, 2),
        own_grad,
        params,
        momenta,
        averages,
    )
    grad_norm = norms.reshape(())
    vector_grads = vector_grads.T
    return (
        layer_output, input_grad, grad_norm, vector_grads, new_params, new_momenta, new_averages,
    )


def solution(mesh):
    placed = (P("dp", None), P("dp", None), P("dp"), P("dp"), P("dp"), P("dp"), P("dp"), P("dp"))
    return jax.shard_map(
        body,
        mesh=mesh,
        in_specs=placed,
        out_specs=(P("dp", None), P("dp", None), P(), P(), P("dp"), P("dp"), P("dp")),
        check_vma=False,
    )
```

```python
import functools

import jax
import jax.numpy as jnp
from jax import lax
from jax.experimental import pallas as pl
from jax.experimental.pallas import tpu as pltpu
from jax.sharding import PartitionSpec as P

HD = 64
ROW = 1024
EPSILON = 1e-05
CLIP_NORM = 1.0
LEARN_RATE = 20.0
MOMENTUM = 0.5
AVERAGE_DECAY = 0.5
MASKED = -1e30
GELU_IN = 0.7978845608028654
GELU_CUBE = 0.044715

D = 512
FF = 2048
PAIR = 2 * HD
PAIRS = D // PAIR
LANES = 128
WINDOW = 3 * LANES
BLOCK = 16
BLOCKS = D // BLOCK
VECTORS = 12
TILE = 256
FIRST_WIDTH = 3 * D + LANES
REST_WIDTH = D + 2 * FF
MIB = 1024 * 1024

f32 = jnp.float32
bf16 = jnp.bfloat16


def nn(left, right):
    return lax.dot_general(left, right, (((1,), (0,)), ((), ())), preferred_element_type=f32)


def nt(left, right):
    return lax.dot_general(left, right, (((1,), (1,)), ((), ())), preferred_element_type=f32)


def turned(values):
    return values.T


def place_blocks(target, pieces, codes, mine):
    place = 0
    for piece in pieces:
        width = piece.shape[1]
        for begin in range(0, piece.shape[0], BLOCK):
            to_rows = pl.ds(pl.multiple_of((mine ^ codes[place]) * BLOCK, BLOCK), BLOCK)
            target[to_rows, :width] = piece[begin : begin + BLOCK, :]
            place += 1


def spread_blocks(halves, source, codes, mine, begin, width):
    for half_at, half in enumerate(halves):
        for block_at in range(BLOCKS // 2):
            natural = mine ^ codes[half_at * (BLOCKS // 2) + block_at]
            from_rows = pl.ds(pl.multiple_of(natural * BLOCK, BLOCK), BLOCK)
            rows = slice(block_at * BLOCK, (block_at + 1) * BLOCK)
            half[rows, pl.ds(begin, width)] = source[from_rows, :].astype(bf16)


def project_kernel(
    codes, mine_ref, x_ref, near_ref, far_ref,
    xt_ref, qt_ref, kt_ref, vt_ref, k_ref, v_ref, vec_ref, pairs_ref,
    table, turned_weights, columns, rows,
):
    @pl.when(pl.program_id(0) == 0)
    def _():
        place_blocks(table, (near_ref, far_ref), codes, mine_ref[0])
        for kind in range(3):
            for half in range(2):
                at = kind * D + half * TILE
                turned_weights[at : at + TILE, :] = turned(table[:, at : at + TILE])
        for pair in range(PAIRS):
            for kind in range(3):
                at = pair * 3 * PAIR + kind * PAIR
                pairs_ref[:, at : at + PAIR] = table[
                    :, kind * D + pair * PAIR : kind * D + (pair + 1) * PAIR
                ]
        vectors = table[:, 3 * D :].astype(f32)
        vec_ref[...] = vectors
        columns[0] = jnp.broadcast_to(vectors[:, 0:1], (D, LANES))
        columns[1] = jnp.broadcast_to(vectors[:, 1:2], (D, LANES))
        rows[...] = vectors.T[:8, :]

    x = x_ref[...]
    width = x.shape[0]
    reps = width // LANES
    for half in range(2):
        xt_ref[half * 256 : half * 256 + 256, :] = turned(x[:, half * 256 : half * 256 + 256])
    bias_q = jnp.concatenate([columns[0]] * reps, axis=1)
    bias_v = jnp.concatenate([columns[1]] * reps, axis=1)
    query = nt(turned_weights[:D, :], x) + bias_q
    qt_ref[...] = (query.astype(bf16).astype(f32) * HD ** (-0.5)).astype(bf16)
    kt_ref[...] = nt(turned_weights[D : 2 * D, :], x).astype(bf16)
    vt_ref[...] = (nt(turned_weights[2 * D :, :], x) + bias_v).astype(bf16)
    k_ref[...] = nn(x, table[:, D : 2 * D]).astype(bf16)
    v_ref[...] = (nn(x, table[:, 2 * D : 3 * D]) + rows[1:2, :]).astype(bf16)


def fill_bias(bias, seg_ref, limits_ref, widths_ref):
    blocks = bias.shape[0]
    lane = lax.broadcasted_iota(jnp.int32, (1, LANES), 1)
    across = lax.broadcasted_iota(jnp.int32, (LANES, LANES), 1)
    down = lax.broadcasted_iota(jnp.int32, (LANES, LANES), 0)

    def codes_of(block):
        row = jnp.where(widths_ref[0] == 1, 0, block // (ROW // LANES))
        limit = jnp.where(row == 0, limits_ref[0], limits_ref[1])
        code = seg_ref[block : block + 1, :] * 2 + row
        live = lane + block * LANES - row * ROW < limit
        return code.astype(f32), jnp.where(live, code, -1).astype(f32)

    codes = [codes_of(block) for block in range(blocks)]
    for block in range(blocks):
        key_column = jnp.broadcast_to(codes[block][1], (LANES, LANES)).T
        for query in range(max(block - 2, 0), min(block + 3, blocks)):
            first = min(max(query - 1, 0), blocks - 3)
            if 0 <= block - first < 3:
                allowed = key_column == codes[query][0]
                if query == block:
                    allowed = allowed | (down == across)
                at = (block - first) * LANES
                bias[query, at : at + LANES, :] = jnp.where(allowed, 0.0, MASKED)


def two_heads(values):
    zeros = jnp.zeros((HD, values.shape[1]), values.dtype)
    left = jnp.concatenate([values[:HD], zeros], axis=0)
    right = jnp.concatenate([zeros, values[HD:]], axis=0)
    return jnp.concatenate([left, right], axis=1)


def own_heads(values):
    return jnp.concatenate([values[:HD, :LANES], values[HD:, LANES:]], axis=0)


def down_tree(values, combine):
    rows = values.shape[0]
    if rows == WINDOW:
        values = combine(
            combine(values[:LANES], values[LANES : 2 * LANES]), values[2 * LANES : 3 * LANES]
        )
        rows = LANES
    while rows > 8:
        rows //= 2
        values = combine(values[:rows], values[rows : 2 * rows])
    return values


def top_down(values):
    return jnp.max(down_tree(values, jnp.maximum), axis=0, keepdims=True)


def sum_down(values):
    return jnp.sum(down_tree(values, jnp.add), axis=0, keepdims=True)


def places(block, blocks):
    begin = min(max(block - 1, 0), blocks - 3) * LANES
    return slice(block * LANES, (block + 1) * LANES), slice(begin, begin + WINDOW)


def pipelined(amount, *stages):
    depth = len(stages)
    held = {}
    for step in range(amount + depth - 1):
        for at, stage in enumerate(stages):
            item = step - at
            if 0 <= item < amount:
                held[item] = stage(item, held.get(item))
                if at == depth - 1:
                    del held[item]


def attend_kernel(
    limits_ref, widths_ref, seg_ref, qt_ref, k_ref, vt_ref, att_ref, logsum_ref, bias
):
    @pl.when(pl.program_id(0) == 0)
    def _():
        fill_bias(bias, seg_ref, limits_ref, widths_ref)

    blocks = bias.shape[0]

    def score(block, _):
        here, window = places(block, blocks)
        mask = bias[block]
        scores = nn(k_ref[window, :], two_heads(qt_ref[:, here]))
        return scores + jnp.concatenate([mask, mask], axis=1)

    def finish(block, scores):
        here, window = places(block, blocks)
        highest = top_down(scores)
        exponent = jnp.exp(scores - highest)
        total = sum_down(exponent)
        outputs = nn(vt_ref[:, window], exponent.astype(bf16)) * (1.0 / total)
        att_ref[:, here] = own_heads(outputs).astype(bf16)
        logsum_ref[0, block : block + 1, :] = highest + jnp.log(total)

    pipelined(blocks, score, finish)


def mean_down(values):
    return sum_down(values) * (1.0 / D)


def lane_parts(values):
    return values[:, :LANES] + values[:, LANES:]


def weight_parts(kept, acc_down, acc_up, acc_out):
    hidden, grad_up, first_low, grad_feed, grad_branch, att = kept

    def part(target, left, right, at):
        def run():
            target[:, at : at + TILE] += nt(left[...], right[at : at + TILE, :])

        return run

    parts = [part(acc_down, grad_feed, hidden, at) for at in range(0, FF, TILE)]
    parts += [part(acc_up, first_low, grad_up, at) for at in range(0, FF, TILE)]
    parts += [part(acc_out, grad_branch, att, at) for at in range(0, D, TILE)]
    return parts


def feed_kernel(codes, amount, *refs):
    mine_ref, limits_ref, widths_ref, xt_ref, att_ref, cot_ref, vec_ref = refs[:7]
    piece_refs = refs[7 : 7 + amount]
    layer_ref, ga_ref, both_ref, keep_ref, send_ref, sums_ref = refs[7 + amount : 13 + amount]
    table, out_turned, up_turned, down_turned, columns, up_bias, slopes = refs[
        13 + amount : 20 + amount
    ]
    acc_down, acc_up, acc_out, acc_vec, *kept = refs[20 + amount :]
    step = pl.program_id(0)
    chunk = TILE
    chunks = FF // chunk
    each = len(kept) // 2

    @pl.when(step == 0)
    def _():
        place_blocks(table, piece_refs, codes, mine_ref[0])
        for at in range(0, D, TILE):
            out_turned[at : at + TILE, :] = turned(table[:, at : at + TILE])
        for at in range(0, FF, TILE):
            up_turned[at : at + TILE, :] = turned(table[:, D + at : D + at + TILE])
            down_turned[at : at + TILE, :] = turned(table[:, D + FF + at : D + FF + at + TILE])
        for kind in range(6):
            columns[kind] = jnp.broadcast_to(vec_ref[:, kind + 2 : kind + 3], (D, LANES))
        for at in range(4):
            up_bias[pl.ds(at, D, stride=4), :] = jnp.broadcast_to(
                vec_ref[:, 8 + at : 9 + at], (D, LANES)
            )
        for buffer in (acc_down, acc_up, acc_out, acc_vec, *kept[each:]):
            buffer[...] = jnp.zeros_like(buffer)
        for buffer in (kept[2], kept[each + 2]):
            buffer[D:, :] = jnp.ones((BLOCK, TILE), bf16)

    def column(kind):
        return jnp.concatenate([columns[kind]] * 2, axis=1)

    def one_tile(tile, now, before):
        hidden, grad_up, first_keep, feed_keep, branch_keep, att_keep = now
        fill = iter(weight_parts(before, acc_down, acc_up, acc_out))

        def tick(amount=1):
            for _ in range(amount):
                next(fill)()

        here = slice(tile * TILE, (tile + 1) * TILE)
        place = lax.broadcasted_iota(jnp.int32, (1, TILE), 1) + (step * 2 + tile) * TILE
        row = jnp.where(widths_ref[0] == 1, 0, place // ROW)
        limit = jnp.where(row == 0, limits_ref[0], limits_ref[1])
        live = place - row * ROW < limit

        x = xt_ref[:, here].astype(f32)
        att = att_ref[:, here]
        att_keep[...] = att
        z_one = x + nn(table[:, :D], att) + column(0)
        tick(5)
        centred = z_one - mean_down(z_one)
        inverse_one = lax.rsqrt(mean_down(centred * centred) + EPSILON)
        normed_one = centred * inverse_one
        first = normed_one * column(2) + column(3)
        first_low = first.astype(bf16)
        first_keep[:D, :] = first_low
        partial = [first + x + column(1)]

        def widen(at, _):
            rows = slice(at * chunk, (at + 1) * chunk)
            bias = jnp.concatenate([up_bias[rows, :]] * 2, axis=1)
            return nn(up_turned[rows, :], first_low) + bias

        def bend(at, pre):
            rows = slice(at * chunk, (at + 1) * chunk)
            square = pre * pre
            tanh = jnp.tanh(pre * (GELU_IN + (GELU_IN * GELU_CUBE) * square))
            half = 0.5 + 0.5 * tanh
            value = pre * half
            slopes[rows, :] = half + value * (1.0 - tanh) * (
                GELU_IN + (3.0 * GELU_IN * GELU_CUBE) * square
            )
            low = value.astype(bf16)
            hidden[rows, :] = low
            return low

        def narrow(at, low):
            columns_at = slice(D + FF + at * chunk, D + FF + (at + 1) * chunk)
            partial[0] = partial[0] + nn(table[:, columns_at], low)

        pipelined(chunks, widen, bend, narrow)
        z_two = partial[0]
        cot = cot_ref[here, :].T.astype(f32)
        tick(8)
        centred = z_two - mean_down(z_two)
        inverse_two = lax.rsqrt(mean_down(centred * centred) + EPSILON)
        normed_two = centred * inverse_two
        gain_two = column(4)
        layer = jnp.where(live, normed_two * gain_two + column(5), 0.0).astype(bf16)
        cot = jnp.where(live, cot, 0.0)
        scaled = cot * gain_two
        scaled_mean = mean_down(scaled)
        product_mean = mean_down(scaled * normed_two)
        grad_two = inverse_two * (scaled - scaled_mean - normed_two * product_mean)
        grad_feed = grad_two.astype(bf16)
        feed_keep[...] = grad_feed
        acc_vec[1] += lane_parts(grad_feed.astype(f32))
        acc_vec[4] += lane_parts(cot * normed_two)
        acc_vec[5] += lane_parts(cot)
        partial[0] = grad_two

        def widen_back(at, _):
            return nn(down_turned[at * chunk : (at + 1) * chunk, :], grad_feed)

        def bend_back(at, grad_hidden):
            rows = slice(at * chunk, (at + 1) * chunk)
            low = (grad_hidden * slopes[rows, :]).astype(bf16)
            grad_up[rows, :] = low
            return low

        def narrow_back(at, low):
            partial[0] = partial[0] + nn(table[:, D + at * chunk : D + (at + 1) * chunk], low)

        pipelined(chunks, widen_back, bend_back, narrow_back)
        grad_first = partial[0]
        layer_ref[here, :] = layer.T
        tick(5)
        acc_vec[2] += lane_parts(grad_first * normed_one)
        acc_vec[3] += lane_parts(grad_first)
        scaled = grad_first * column(2)
        scaled_mean = mean_down(scaled)
        product_mean = mean_down(scaled * normed_one)
        grad_one = inverse_one * (scaled - scaled_mean - normed_one * product_mean)
        both_ref[:, here] = (grad_two + grad_one).astype(bf16)
        grad_branch = grad_one.astype(bf16)
        branch_keep[...] = grad_branch
        acc_vec[0] += lane_parts(grad_branch.astype(f32))
        ga_ref[:, here] = nn(out_turned[...], grad_branch).astype(bf16)

    one_tile(0, kept[:each], kept[each:])
    one_tile(1, kept[each:], kept[:each])

    @pl.when(step == pl.num_programs(0) - 1)
    def _():
        parts = weight_parts(kept[each:], acc_down, acc_up, acc_out)
        for source, begin, width, some in (
            (acc_up, D, FF, parts[8:16]),
            (acc_down, D + FF, FF, parts[:8]),
            (acc_out, 0, D, parts[16:]),
        ):
            for part in some:
                part()
            spread_blocks((keep_ref, send_ref), source, codes, mine_ref[0], begin, width)
        up_sums = jnp.broadcast_to(acc_up[D : D + 1, :], (LANES, FF))
        for at in range(0, FF, LANES):
            up_bias[at : at + LANES, :] = up_sums[:, at : at + LANES].T
        lane = lax.broadcasted_iota(jnp.int32, (D, LANES), 1)
        vectors = jnp.zeros((D, LANES), f32)
        for kind in range(6):
            total = jnp.sum(acc_vec[kind], axis=1, keepdims=True)
            vectors = jnp.where(lane == kind + 2, total, vectors)
        for at in range(4):
            vectors = jnp.where(lane == 8 + at, up_bias[pl.ds(at, D, stride=4), :], vectors)
        sums_ref[...] = vectors


def attend_back_kernel(
    codes, mine_ref, limits_ref, widths_ref, seg_ref, xt_ref, qt_ref, kt_ref, k_ref, v_ref, att_ref, ga_ref,
    logsum_ref, sums_ref, grads_ref, keep_ref, send_ref, bias, acc_key, acc_value, weight_grad,
    vectors,
):
    pair = pl.program_id(0)

    @pl.when(pair == 0)
    def _():
        fill_bias(bias, seg_ref, limits_ref, widths_ref)

    blocks = bias.shape[0]
    acc_key[...] = jnp.zeros_like(acc_key)
    acc_value[...] = jnp.zeros_like(acc_value)

    def score(block, _):
        here, window = places(block, blocks)
        mask = bias[block]
        query = two_heads(qt_ref[:, here])
        grad = two_heads(ga_ref[:, here])
        scores = nn(k_ref[window, :], query) + jnp.concatenate([mask, mask], axis=1)
        return query, grad, scores, nn(v_ref[window, :], grad)

    def finish(block, held):
        query, grad, scores, grad_chances = held
        here, window = places(block, blocks)
        product = ga_ref[:, here].astype(f32) * att_ref[:, here].astype(f32)
        centre = jnp.concatenate([sum_down(product[:HD]), sum_down(product[HD:])], axis=1)
        chances = jnp.exp(scores - logsum_ref[0, block : block + 1, :])
        grad_scores = (chances * (grad_chances - centre)).astype(bf16)
        acc_value[:, window] += nt(grad, chances.astype(bf16))
        grad_query = own_heads(nn(kt_ref[:, window], grad_scores)) * HD ** (-0.5)
        grads_ref[0, :PAIR, here] = grad_query.astype(bf16)
        acc_key[:, window] += nt(query, grad_scores)

    pipelined(blocks, score, finish)
    grads_ref[0, PAIR : 2 * PAIR, :] = acc_key[...].astype(bf16)
    grads_ref[0, 2 * PAIR :, :] = acc_value[...].astype(bf16)
    grads = grads_ref[0]
    weight_grad[...] = nt(xt_ref[...], grads)
    halves = (keep_ref, send_ref)
    begin = pl.multiple_of(pair * (3 * PAIR), 3 * PAIR)
    spread_blocks(halves, weight_grad, codes, mine_ref[0], begin, 3 * PAIR)
    rows = pl.ds(pl.multiple_of(pair * PAIR, PAIR), PAIR)
    lane = lax.broadcasted_iota(jnp.int32, (PAIR, LANES), 1)
    query_sum = jnp.sum(grads[:PAIR].astype(f32), axis=1, keepdims=True)
    value_sum = jnp.sum(grads[2 * PAIR :].astype(f32), axis=1, keepdims=True)
    total = jnp.where(lane == 0, query_sum, jnp.where(lane == 1, value_sum, sums_ref[rows, :]))
    vectors[rows, :] = total

    @pl.when(pair == PAIRS - 1)
    def _():
        spread_blocks(halves, vectors, codes, mine_ref[0], 3 * D, LANES)


def input_kernel(grads_ref, weights_ref, both_ref, out_ref):
    width = both_ref.shape[1]

    def multiply(at, _):
        here = slice(at * TILE, (at + 1) * TILE)
        grads = jnp.concatenate([grads_ref[pair, :, here] for pair in range(PAIRS)], axis=0)
        return both_ref[:, here].astype(f32) + nn(weights_ref[...], grads)

    def turn(at, total):
        out_ref[at * TILE : (at + 1) * TILE, :] = total.T

    pipelined(width // TILE, multiply, turn)


def own_kernel(*refs):
    own_ref, share_ref = refs[-2:]
    rest_ref = refs[-3]
    total = sum(part[...].astype(f32) for part in refs[:-3])
    squares = jnp.sum(rest_ref[...] * rest_ref[...], axis=1, keepdims=True)
    for pair in range(PAIRS):
        for kind in range(3):
            at = pair * 3 * PAIR + kind * PAIR
            piece = total[:, at : at + PAIR]
            own_ref[:, kind * D + pair * PAIR : kind * D + (pair + 1) * PAIR] = piece
            squares = squares + jnp.sum(piece * piece, axis=1, keepdims=True)
    vectors = total[:, -LANES:]
    lane = lax.broadcasted_iota(jnp.int32, vectors.shape, 1)
    vectors = jnp.where(lane < VECTORS, vectors, 0.0)
    squares = squares + jnp.sum(vectors * vectors, axis=1, keepdims=True)
    share_ref[...] = jnp.where(lane == VECTORS, squares, vectors)


def settle_kernel(
    codes, mine_ref, near_ref, far_ref, grad_ref, params_ref, momenta_ref, averages_ref,
    vectors_ref, norm_ref, new_params_ref, new_momenta_ref, new_averages_ref, table,
):
    place_blocks(table, (near_ref, far_ref), codes, mine_ref[0])
    vectors_ref[...] = table[...].T[:VECTORS, :]
    squares = jnp.sum(table[...], axis=0, keepdims=True)[:, VECTORS : VECTORS + 1]
    norm = jnp.sqrt(squares)
    norm_ref[0] = norm[0, 0]
    factor = jnp.minimum(1.0, CLIP_NORM / (norm + 1e-06))[0, 0]
    clipped = grad_ref[...] * factor
    momenta = MOMENTUM * momenta_ref[...] + clipped
    params = params_ref[...] - LEARN_RATE * (clipped + MOMENTUM * momenta)
    new_momenta_ref[...] = momenta
    new_params_ref[...] = params
    new_averages_ref[...] = AVERAGE_DECAY * averages_ref[...] + (1.0 - AVERAGE_DECAY) * params


def exchange(values, bit, count):
    return lax.ppermute(values, "dp", [(at, at ^ bit) for at in range(count)])


def mask_phases(count, size):
    bits = [1 << at for at in range(1, count.bit_length() - 1)]
    groups = [bits[:2]]
    for bit in bits[2:]:
        if len(groups[-1]) < size and len(groups) > 1:
            groups[-1].append(bit)
        else:
            groups.append([bit])
    return [[0, 1]] + [
        [
            sum(bit for at, bit in enumerate(group) if choice >> at & 1)
            for choice in range(1 << len(group))
        ]
        for group in groups
    ]


def block_codes(phases):
    codes = [0]
    for masks in reversed(phases):
        codes = [mask ^ code for mask in masks for code in codes]
    return codes


def gather_phase(block, masks, count):
    return [block] + [exchange(block, mask, count) for mask in masks[1:]]


def scatter_phase(pieces, masks, count):
    return [pieces[0]] + [
        exchange(piece, mask, count) for piece, mask in zip(pieces[1:], masks[1:], strict=True)
    ]


def cut_sum(parts, amount, dtype):
    rows = parts[0].shape[0] // amount
    return [
        sum(part[at * rows : (at + 1) * rows].astype(f32) for part in parts).astype(dtype)
        for at in range(amount)
    ]


def together(*values):
    return lax.optimization_barrier(values)


def whole(shape):
    return pl.BlockSpec(shape, lambda *at: (0,) * len(shape))


def smem():
    return pl.BlockSpec(memory_space=pltpu.SMEM)


def shaped(shape, dtype):
    return jax.ShapeDtypeStruct(shape, dtype)


def resident():
    return pl.BlockSpec(memory_space=pltpu.VMEM)


def params_of(mib):
    return pltpu.CompilerParams(vmem_limit_bytes=mib * MIB)


def body(tokens, cotangent, segment_ids, row_lengths, row_widths, params, momenta, averages):
    slots = tokens.shape[0]
    count = lax.axis_size("dp")
    mine = lax.axis_index("dp").astype(jnp.int32)
    own_count = D // count
    table_width = params.shape[0] // own_count
    blocks = slots // LANES
    direct = own_count == BLOCK
    phases = mask_phases(count, 2)
    slow_phases = mask_phases(count, 1)
    order = block_codes(phases)
    slow_order = block_codes(slow_phases)
    if direct:
        codes, slow_codes = order, slow_order
        origin = mine.reshape(1)
    else:
        codes = slow_codes = list(range(BLOCKS))
        origin = jnp.zeros((1,), jnp.int32)

    def to_kernel(pieces, order, amount):
        if direct:
            return pieces
        places = jnp.argsort(jnp.array(order, jnp.int32))[jnp.arange(count) ^ mine]
        table = jnp.concatenate(pieces, axis=0).reshape(count, own_count, -1)
        return list(jnp.take(table, places, axis=0).reshape(amount, D // amount, -1))

    def from_kernel(keep, send, order):
        if direct:
            return keep, send
        table = jnp.concatenate([keep, send], axis=0).reshape(count, own_count, -1)
        table = jnp.take(table, jnp.array(order, jnp.int32) ^ mine, axis=0).reshape(D, -1)
        return table[: D // 2], table[D // 2 :]

    own_table = params.astype(bf16).reshape(own_count, table_width)
    own_first = jnp.concatenate(
        [
            own_table[:, : 3 * D],
            jnp.pad(own_table[:, 12 * D :], ((0, 0), (0, LANES - VECTORS))),
        ],
        axis=1,
    )
    own_rest = own_table[:, 3 * D : 12 * D]
    outer = phases[:0:-1]
    first, rest = own_first, own_rest
    for at, masks in enumerate(slow_phases[:1:-1]):
        if at == 1:
            first = jnp.concatenate(gather_phase(first, outer[0], count), axis=0)
            _, rest = together(first, rest)
        rest = jnp.concatenate(gather_phase(rest, masks, count), axis=0)
    for masks in outer[1:]:
        first = jnp.concatenate(gather_phase(first, masks, count), axis=0)
    first, rest = together(first, rest)
    rest_pieces = gather_phase(rest, slow_phases[1], count)
    rest_far = [exchange(rest, 1, count)]
    first_near, first_far = to_kernel(gather_phase(first, phases[0], count), order, 2)
    segments = segment_ids.reshape(blocks, LANES)

    tile = 2 * TILE
    steps = slots // tile
    across = pl.BlockSpec((D, tile), lambda at: (0, at))
    down = pl.BlockSpec((tile, D), lambda at: (at, 0))
    xt, qt, kt, vt, key, value, vectors, pair_weights = pl.pallas_call(
        functools.partial(project_kernel, codes),
        grid=(steps,),
        in_specs=[smem(), down, resident(), resident()],
        out_specs=[across] * 4 + [down] * 2 + [whole((D, LANES)), whole((D, 3 * D))],
        out_shape=[shaped((D, slots), bf16)] * 4
        + [shaped((slots, D), bf16)] * 2
        + [shaped((D, LANES), f32), shaped((D, 3 * D), bf16)],
        scratch_shapes=[
            pltpu.VMEM((D, FIRST_WIDTH), bf16),
            pltpu.VMEM((3 * D, D), bf16),
            pltpu.VMEM((2, D, LANES), f32),
            pltpu.VMEM((8, D), f32),
        ],
        compiler_params=params_of(52),
        name="project",
    )(origin, tokens, first_near, first_far)

    pair_rows = pl.BlockSpec((PAIR, slots), lambda at: (at, 0))
    pair_columns = pl.BlockSpec((slots, PAIR), lambda at: (0, at))
    sums_block = pl.BlockSpec((1, blocks, 2 * LANES), lambda at: (at, 0, 0))
    attended, logsum = pl.pallas_call(
        attend_kernel,
        grid=(PAIRS,),
        in_specs=[smem(), smem(), whole((blocks, LANES)), pair_rows, pair_columns, pair_rows],
        out_specs=[pair_rows, sums_block],
        out_shape=[shaped((D, slots), bf16), shaped((PAIRS, blocks, 2 * LANES), f32)],
        scratch_shapes=[pltpu.VMEM((blocks, WINDOW, LANES), f32)],
        compiler_params=params_of(52),
        name="attend",
    )(row_lengths, row_widths, segments, qt, key, vt)

    attended, *rest_pieces = together(attended, *rest_pieces)
    rest_far += [exchange(piece, 1, count) for piece in rest_pieces[1:]]
    rest_pieces = to_kernel(rest_pieces + rest_far, slow_order, 1)
    layer_output, grad_attended, grad_both, keep_rest, send_rest, feed_sums = pl.pallas_call(
        functools.partial(feed_kernel, slow_codes, len(rest_pieces)),
        grid=(steps,),
        in_specs=[
            smem(), smem(), smem(), across, across, down,
            whole((D, LANES)),
        ]
        + [whole(piece.shape) for piece in rest_pieces],
        out_specs=[down, across, across]
        + [resident()] * 2
        + [whole((D, LANES))],
        out_shape=[
            shaped((slots, D), bf16),
            shaped((D, slots), bf16),
            shaped((D, slots), bf16),
            pltpu.VMEM((D // 2, REST_WIDTH), bf16),
            pltpu.VMEM((D // 2, REST_WIDTH), bf16),
            shaped((D, LANES), f32),
        ],
        scratch_shapes=[
            pltpu.VMEM((D, REST_WIDTH), bf16),
            pltpu.VMEM((D, D), bf16),
            pltpu.VMEM((FF, D), bf16),
            pltpu.VMEM((FF, D), bf16),
            pltpu.VMEM((6, D, LANES), f32),
            pltpu.VMEM((FF, LANES), f32),
            pltpu.VMEM((FF, TILE), f32),
            pltpu.VMEM((D, FF), f32),
            pltpu.VMEM((D + BLOCK, FF), f32),
            pltpu.VMEM((D, D), f32),
            pltpu.VMEM((6, D, LANES), f32),
        ]
        + [pltpu.VMEM((rows, TILE), bf16) for rows in (FF, FF, D + BLOCK, D, D, D)] * 2,
        compiler_params=params_of(50 if direct else 54),
        name="feed",
    )(origin, row_lengths, row_widths, xt, attended, cotangent, vectors, *rest_pieces)

    def scatter(parts, way, at):
        if at == len(way) - 1:
            return cut_sum(parts, 1, f32)
        return cut_sum(parts, len(way[at + 1]), bf16)

    parts = scatter_phase(from_kernel(keep_rest, send_rest, slow_order), slow_phases[0], count)
    grad_attended, *pieces = together(grad_attended, *scatter(parts, slow_phases, 0))
    rest_parts = scatter_phase(pieces, slow_phases[1], count)

    grads, keep_first, send_first = pl.pallas_call(
        functools.partial(attend_back_kernel, codes),
        grid=(PAIRS,),
        in_specs=[
            smem(), smem(), smem(), whole((blocks, LANES)), whole((D, slots)),
            pair_rows, pair_rows, pair_columns, pair_columns, pair_rows, pair_rows, sums_block,
            whole((D, LANES)),
        ],
        out_specs=[
            pl.BlockSpec((1, 3 * PAIR, slots), lambda at: (at, 0, 0)),
            resident(),
            resident(),
        ],
        out_shape=[
            pltpu.VMEM((PAIRS, 3 * PAIR, slots), bf16),
            pltpu.VMEM((D // 2, FIRST_WIDTH), bf16),
            pltpu.VMEM((D // 2, FIRST_WIDTH), bf16),
        ],
        scratch_shapes=[
            pltpu.VMEM((blocks, WINDOW, LANES), f32),
            pltpu.VMEM((PAIR, slots), f32),
            pltpu.VMEM((PAIR, slots), f32),
            pltpu.VMEM((D, 3 * PAIR), f32),
            pltpu.VMEM((D, LANES), f32),
        ],
        compiler_params=params_of(46),
        name="attend_back",
    )(origin, row_lengths, row_widths, segments, xt, qt, kt, key, value, attended, grad_attended, logsum, feed_sums)

    keep_first, send_first, *rest_parts = together(keep_first, send_first, *rest_parts)
    parts = scatter_phase(from_kernel(keep_first, send_first, order), phases[0], count)
    pieces = scatter(parts, phases, 0)
    grads, *held = together(grads, *pieces, *rest_parts)
    pieces, rest_parts = held[: len(pieces)], held[len(pieces) :]
    parts = scatter_phase(pieces, phases[1], count)
    grads, *rest_pieces = together(grads, *scatter(rest_parts, slow_phases, 1))
    rest_parts = scatter_phase(rest_pieces, slow_phases[2], count)
    input_grad = pl.pallas_call(
        input_kernel,
        grid=(steps,),
        in_specs=[
            pl.BlockSpec((PAIRS, 3 * PAIR, tile), lambda at: (0, 0, at)),
            whole((D, 3 * D)),
            across,
        ],
        out_specs=down,
        out_shape=shaped((slots, D), f32),
        compiler_params=params_of(20),
        name="input_grad",
    )(grads, pair_weights, grad_both)
    input_grad, *parts = together(input_grad, *parts)
    for at in range(2, len(phases)):
        pieces = scatter(parts, phases, at - 1)
        pieces[0], *rest_parts = together(pieces[0], *rest_parts)
        parts = scatter_phase(pieces, phases[at], count)
    for at in range(3, len(slow_phases)):
        rest_pieces = scatter(rest_parts, slow_phases, at - 1)
        rest_parts = scatter_phase(rest_pieces, slow_phases[at], count)
    (own_rest,) = scatter(rest_parts, slow_phases, len(slow_phases) - 1)
    own_first, share = pl.pallas_call(
        own_kernel,
        out_shape=[shaped((own_count, 3 * D), f32), shaped((own_count, LANES), f32)],
        compiler_params=params_of(8),
        name="own",
    )(*parts, own_rest)
    shares = share
    for masks in outer:
        shares = jnp.concatenate(gather_phase(shares, masks, count), axis=0)
    own_grad = jnp.concatenate([own_first, own_rest, share[:, :VECTORS]], axis=1).reshape(-1)
    flat = shaped(params.shape, f32)
    vector_grads, norms, new_params, new_momenta, new_averages = pl.pallas_call(
        functools.partial(settle_kernel, codes),
        in_specs=[smem()] + [resident()] * 6,
        out_specs=[whole((VECTORS, D)), smem()] + [resident()] * 3,
        out_shape=[shaped((VECTORS, D), f32), shaped((1,), f32)] + [flat] * 3,
        scratch_shapes=[pltpu.VMEM((D, LANES), f32)],
        compiler_params=params_of(16),
        name="settle",
    )(
        origin,
        *to_kernel(gather_phase(shares, phases[0], count), order, 2),
        own_grad,
        params,
        momenta,
        averages,
    )
    grad_norm = norms.reshape(())
    vector_grads = vector_grads.T
    return (
        layer_output, input_grad, grad_norm, vector_grads, new_params, new_momenta, new_averages,
    )


def solution(mesh):
    placed = (P("dp", None), P("dp", None), P("dp"), P("dp"), P("dp"), P("dp"), P("dp"), P("dp"))
    return jax.shard_map(
        body,
        mesh=mesh,
        in_specs=placed,
        out_specs=(P("dp", None), P("dp", None), P(), P(), P("dp"), P("dp"), P("dp")),
        check_vma=False,
    )
```
